32 devices in a mesh: seq: 8 (over z, y), head: 4 (over x, core).
Axes of the slice: x: 2, y: 2, z: 4, core: 2. Of those that a mesh axis runs over, the one named last changes fastest.
Arguments:
- tokens: bfloat16 [16, 196, 768], P('seq'), may hold values from -6 to 6
- cls_tokens: bfloat16 [4, 768], replicated, may hold values from -6 to 6
- clip_lengths: int32 [4], replicated, may hold values from 1 to 8, 16 in all
- time_gain: float32 [768], replicated, may hold values from 0.1 to 1.9
- time_beta: float32 [768], replicated, may hold values from -1.75 to 1.75
- time_proj_in: bfloat16 [768, 3, 768], P(None, None, 'head'), may hold values from -0.21875 to 0.21875
- time_qv_bias: float32 [2, 768], P(None, 'head'), may hold values from -1.75 to 1.75
- time_proj_out: bfloat16 [768, 768], P('head'), may hold values from -0.3125 to 0.3125
- time_out_bias: float32 [768], replicated, may hold values from -1.75 to 1.75
- time_linear: bfloat16 [768, 768], replicated, may hold values from -0.21875 to 0.21875
- time_linear_bias: float32 [768], replicated, may hold values from -1.75 to 1.75
- space_gain: float32 [768], replicated, may hold values from 0.1 to 1.9
- space_beta: float32 [768], replicated, may hold values from -1.75 to 1.75
- space_proj_in: bfloat16 [768, 3, 768], P(None, None, 'head'), may hold values from -0.21875 to 0.21875
- space_qv_bias: float32 [2, 768], P(None, 'head'), may hold values from -1.75 to 1.75
- space_proj_out: bfloat16 [768, 768], P('head'), may hold values from -0.625 to 0.625
- space_out_bias: float32 [768], replicated, may hold values from -1.75 to 1.75
- mlp_gain: float32 [768], replicated, may hold values from 0.1 to 1.9
- mlp_beta: float32 [768], replicated, may hold values from -1.75 to 1.75
- mlp_up: bfloat16 [768, 3072], P(None, 'head'), may hold values from -0.21875 to 0.21875
- mlp_up_bias: float32 [3072], P('head'), may hold values from -1.75 to 1.75
- mlp_down: bfloat16 [3072, 768], P('head'), may hold values from -0.109375 to 0.109375
- mlp_down_bias: float32 [768], replicated, may hold values from -1.75 to 1.75
- out_grad: bfloat16 [16, 196, 768], P('seq'), may hold values from -6 to 6
- cls_grad: bfloat16 [4, 768], replicated, may hold values from -6 to 6
Outputs:
- block_out: bfloat16 [16, 196, 768], P('seq')
- cls_out: bfloat16 [4, 768], replicated
- tokens_grad: bfloat16 [16, 196, 768], P('seq')
- cls_tokens_grad: float32 [4, 768], P(None, 'seq')
- time_gain_grad: float32 [768], P('seq')
- time_beta_grad: float32 [768], replicated
- time_proj_in_grad: float32 [768, 3, 768], P('seq', None, 'head')
- time_qv_bias_grad: float32 [2, 768], P(None, 'head')
- time_proj_out_grad: float32 [768, 768], P('head', 'seq')
- time_out_bias_grad: float32 [768], replicated
- time_linear_grad: float32 [768, 768], P('seq', 'head')
- time_linear_bias_grad: float32 [768], replicated
- space_gain_grad: float32 [768], P('seq')
- space_beta_grad: float32 [768], replicated
- space_proj_in_grad: float32 [768, 3, 768], P('seq', None, 'head')
- space_qv_bias_grad: float32 [2, 768], P(None, 'head')
- space_proj_out_grad: float32 [768, 768], P('head', 'seq')
- space_out_bias_grad: float32 [768], replicated
- mlp_gain_grad: float32 [768], P('seq')
- mlp_beta_grad: float32 [768], replicated
- mlp_up_grad: float32 [768, 3072], P('seq', 'head')
- mlp_up_bias_grad: float32 [3072], P('head')
- mlp_down_grad: float32 [3072, 768], P('head', 'seq')
- mlp_down_bias_grad: float32 [768], replicated
The draws below stay inside these ranges and needn't reach their ends.
Inputs may be any that keep to these rules, and one draw needn't show every extreme that they name: clip_lengths sum to 16; some clip has exactly 8 frames.
All inputs are finite; a program needn't handle non-finite values.
Results may differ from the reference program's by a relative error of at most 0.035.
Values may be sent and summed in bfloat16 or wider, within the bound.
A program may use at most 128 MiB of HBM per device.

```python
import math
import jax
import jax.numpy as jnp
import numpy as np
from jax import lax

D = 768
HEADS = 12
HEAD_DIM = 64
FF = 3072
PATCH = 196
MAXLEN = 8
FR_DEV = 2
NF = 16
CLIPS = 4


def strengthened(values, key, source, target, parts, factor):
    def block_of(axis_at):
        return (jnp.arange(values.shape[axis_at]) // (values.shape[axis_at] // parts)).reshape((-1,) + (1,) * (values.ndim - 1 - axis_at))

    first = jax.random.permutation(key, parts)[block_of(target)]
    other_side = (block_of(target) + parts // 2) % parts
    return jnp.where((block_of(source) == first) | (block_of(source) == other_side), factor * values, values)


def steps_of(own_key, dims, shards, low, top_value):
    level, own = 1.0, jax.random.fold_in(own_key, 6)
    for position, shards_of in shards:
        draws = jnp.exp(jax.random.uniform(jax.random.fold_in(own, position), (shards_of,), jnp.float32, low / len(shards), top_value / len(shards)))
        level = level * jnp.repeat(draws, dims[position] // shards_of).reshape([-1 if axis == position else 1 for axis in range(len(dims))])
    return level


def profile(number_of, total, most, lean):
    weights = [(1 << 20) // math.isqrt(rank ** lean) + 1 for rank in range(2, number_of + 1)]
    surplus, holding = total - most - (number_of - 1), [1] * (number_of - 1)
    while surplus > 0:
        free = [i for i in range(number_of - 1) if holding[i] < most]
        whole, remaining = sum([weights[i] for i in free]), surplus
        for i in free:
            addition = min(most - holding[i], max(1, remaining * weights[i] // whole), surplus)
            holding[i] = holding[i] + addition
            surplus = surplus - addition
    return np.array([most] + holding)


def ragged_sizes(own_key, number_of, total, bound, slope):
    if number_of == 2:
        one = jax.random.randint(own_key, (), max(1, total - bound), min(bound, total - 1) + 1)
        return jnp.stack([one, total - one])
    sizes = jnp.asarray(profile(number_of, total, bound, slope), jnp.int32)
    couples = (number_of - 1) // 2
    source_of, receiver = sizes[1:1 + 2 * couples:2], sizes[2:2 + 2 * couples:2]
    margin = jnp.minimum(source_of - 1, bound - receiver)
    moved = jax.random.randint(jax.random.fold_in(own_key, 1), (couples,), 0, 1 << 20) % (margin + 1)
    sizes = sizes.at[1:1 + 2 * couples:2].set(source_of - moved).at[2:2 + 2 * couples:2].set(receiver + moved)
    return sizes[jax.random.permutation(jax.random.fold_in(own_key, 2), number_of)]


def gaussian(own_key, shape, scale, limit, cuts=(), kind=jnp.bfloat16):
    loudness = steps_of(own_key, shape, cuts, -0.22, 0.18) if cuts else 1.0
    entries = jax.random.normal(own_key, shape, jnp.float32) * scale * loudness
    return jnp.minimum(jnp.maximum(entries, -limit), limit).astype(kind)


def noise_with(rng, shape, spread, most, cuts, heavy, kind=jnp.bfloat16):
    values = spread * jax.random.normal(rng, shape, jnp.float32)
    if cuts:
        values = values * steps_of(rng, shape, cuts, -0.22, 0.18)
    return jnp.clip(strengthened(values, jax.random.fold_in(rng, 3), *heavy), -most, most).astype(kind)


def setup_inputs(seed: int = 0) -> dict:
    key_of = jax.random.split(jax.random.key(seed), 26)
    tokens = gaussian(key_of[0], (NF, PATCH, D), 1.0, 6.0, ((0, 8),))
    cls_tokens = gaussian(key_of[1], (CLIPS, D), 1.0, 6.0)
    clip_lengths = ragged_sizes(key_of[2], CLIPS, NF, MAXLEN, 2).astype(jnp.int32)
    time_gain = jnp.clip(1.0 + 0.18 * jax.random.normal(key_of[3], (D,), jnp.float32), 0.1, 1.9)
    time_beta = gaussian(key_of[4], (D,), 0.3, 1.75, (), jnp.float32)
    time_proj_in = gaussian(key_of[5], (D, 3, D), D ** -0.5, 0.21875, ((2, 4),))
    time_qv_bias = gaussian(key_of[6], (2, D), 0.3, 1.75, ((1, 4),), jnp.float32)
    time_proj_out = gaussian(key_of[7], (D, D), (D // 2) ** -0.5, 0.3125, ((0, 4),))
    time_out_bias = gaussian(key_of[8], (D,), 0.3, 1.75, (), jnp.float32)
    time_linear = gaussian(key_of[9], (D, D), D ** -0.5, 0.21875)
    time_linear_bias = gaussian(key_of[10], (D,), 0.3, 1.75, (), jnp.float32)
    space_gain = jnp.clip(1.0 + 0.18 * jax.random.normal(key_of[11], (D,), jnp.float32), 0.1, 1.9)
    space_beta = gaussian(key_of[12], (D,), 0.3, 1.75, (), jnp.float32)
    space_proj_in = gaussian(key_of[13], (D, 3, D), D ** -0.5, 0.21875, ((2, 4),))
    space_qv_bias = gaussian(key_of[14], (2, D), 0.3, 1.75, ((1, 4),), jnp.float32)
    space_proj_out = gaussian(key_of[15], (D, D), (D // 8) ** -0.5, 0.625, ((0, 4),))
    space_out_bias = gaussian(key_of[16], (D,), 0.3, 1.75, (), jnp.float32)
    mlp_gain = jnp.clip(1.0 + 0.18 * jax.random.normal(key_of[17], (D,), jnp.float32), 0.1, 1.9)
    mlp_beta = gaussian(key_of[18], (D,), 0.3, 1.75, (), jnp.float32)
    mlp_up = gaussian(key_of[19], (D, FF), D ** -0.5, 0.21875, ((1, 4),))
    mlp_up_bias = gaussian(key_of[20], (FF,), 0.3, 1.75, ((0, 4),), jnp.float32)
    mlp_down = gaussian(key_of[21], (FF, D), FF ** -0.5, 0.109375, ((0, 4),))
    mlp_down_bias = gaussian(key_of[22], (D,), 0.3, 1.75, (), jnp.float32)
    out_grad = noise_with(key_of[23], (NF, PATCH, D), 1.0, 6.0, ((0, 8),), (0, 2, 8, 2.0))
    cls_grad = gaussian(key_of[24], (CLIPS, D), 1.0, 6.0)
    return {"tokens": tokens, "cls_tokens": cls_tokens, "clip_lengths": clip_lengths, "time_gain": time_gain, "time_beta": time_beta, "time_proj_in": time_proj_in, "time_qv_bias": time_qv_bias, "time_proj_out": time_proj_out, "time_out_bias": time_out_bias, "time_linear": time_linear, "time_linear_bias": time_linear_bias, "space_gain": space_gain, "space_beta": space_beta, "space_proj_in": space_proj_in, "space_qv_bias": space_qv_bias, "space_proj_out": space_proj_out, "space_out_bias": space_out_bias, "mlp_gain": mlp_gain, "mlp_beta": mlp_beta, "mlp_up": mlp_up, "mlp_up_bias": mlp_up_bias, "mlp_down": mlp_down, "mlp_down_bias": mlp_down_bias, "out_grad": out_grad, "cls_grad": cls_grad}


EPS = 1e-06
NEG = -1e+30
HIGH = lax.Precision.HIGHEST

@jax.custom_vjp
def low(v):
    return lax.optimization_barrier(v.astype(jnp.bfloat16)).astype(jnp.float32)

@jax.custom_vjp
def low_back(v):
    return v

def low_keep(v):
    return (low(v), None)

def low_pass(kept, grad):
    return (grad,)

def back_keep(v):
    return (v, None)

def back_low(kept, grad):
    return (low(grad),)
low.defvjp(low_keep, low_pass)
low_back.defvjp(back_keep, back_low)

def matmul(left, right):
    return jnp.matmul(left, right, precision=HIGH)

def norm_rows(rows, gain, shift):
    center = rows - lax.optimization_barrier(jnp.mean(rows, axis=-1, keepdims=True))
    variance = lax.optimization_barrier(jnp.mean(center * center, axis=-1, keepdims=True))
    return center * lax.rsqrt(variance + EPS) * gain + shift

def qkv_bias(pair):
    return jnp.stack([pair[0], jnp.zeros_like(pair[0]), pair[1]], axis=0)

def split_cols(normed, weight, bias_rows):
    width = weight.shape[2]
    product = matmul(normed, weight.reshape(weight.shape[0], 3 * width)) + bias_rows.reshape(3 * width)
    return low(low_back(product.reshape(normed.shape[:-1] + (3, width))))

def time_attention(queries, key_rows, value_rows, valid):
    frames, patches, model_width = queries.shape
    band_reach = MAXLEN - 1
    band_span = 2 * band_reach + 1
    block_size = 4
    score_scale = HEAD_DIM ** (-0.5)

    def one_block(pieces):
        query_block, key_block, value_block = pieces
        key_pad = jnp.pad(key_block, ((0, 0), (band_reach, band_reach), (0, 0)))
        value_pad = jnp.pad(value_block, ((0, 0), (band_reach, band_reach), (0, 0)))
        key_band = jnp.stack([key_pad[:, offset:offset + frames] for offset in range(band_span)], axis=2)
        value_band = jnp.stack([value_pad[:, offset:offset + frames] for offset in range(band_span)], axis=2)
        key_band = key_band.reshape(block_size, frames, band_span, HEADS, HEAD_DIM)
        value_band = value_band.reshape(block_size, frames, band_span, HEADS, HEAD_DIM)
        query_heads = query_block.reshape(block_size, frames, HEADS, HEAD_DIM)
        scores = jnp.einsum('bfhd,bfohd->bfho', query_heads, key_band, precision=HIGH) * score_scale
        scores = jnp.where(valid[None, :, None, :], low_back(scores), NEG)
        largest = lax.optimization_barrier(jnp.max(scores, axis=-1, keepdims=True))
        exponent = jnp.exp(scores - largest)
        attend = exponent / lax.optimization_barrier(jnp.sum(exponent, axis=-1, keepdims=True))
        result = jnp.einsum('bfho,bfohd->bfhd', low(attend), value_band, precision=HIGH)
        return result.reshape(block_size, frames, model_width)

    def arrange(array):
        return jnp.transpose(array, (1, 0, 2)).reshape(patches // block_size, block_size, frames, model_width)
    results = lax.map(jax.checkpoint(one_block), (arrange(queries), arrange(key_rows), arrange(value_rows)))
    return jnp.transpose(results.reshape(patches, frames, model_width), (1, 0, 2))

def space_attention(queries, key_rows, value_rows):
    frames, span_rows, model_width = queries.shape
    score_scale = HEAD_DIM ** (-0.5)

    def one_block(pieces):
        query_block, key_block, value_block = pieces
        query_heads = query_block.reshape(FR_DEV, span_rows, HEADS, HEAD_DIM)
        key_heads = key_block.reshape(FR_DEV, span_rows, HEADS, HEAD_DIM)
        value_heads = value_block.reshape(FR_DEV, span_rows, HEADS, HEAD_DIM)
        scores = jnp.einsum('fqhd,fkhd->fhqk', query_heads, key_heads, precision=HIGH) * score_scale
        scores = low_back(scores)
        largest = lax.optimization_barrier(jnp.max(scores, axis=-1, keepdims=True))
        exponent = jnp.exp(scores - largest)
        attend = exponent / lax.optimization_barrier(jnp.sum(exponent, axis=-1, keepdims=True))
        result = jnp.einsum('fhqk,fkhd->fqhd', low(attend), value_heads, precision=HIGH)
        return result.reshape(FR_DEV, span_rows, model_width)

    def arrange(array):
        return array.reshape(frames // FR_DEV, FR_DEV, span_rows, model_width)
    results = lax.map(jax.checkpoint(one_block), (arrange(queries), arrange(key_rows), arrange(value_rows)))
    return results.reshape(frames, span_rows, model_width)

def reference(tokens, cls_tokens, clip_lengths, time_gain, time_beta, time_proj_in, time_qv_bias, time_proj_out, time_out_bias, time_linear, time_linear_bias, space_gain, space_beta, space_proj_in, space_qv_bias, space_proj_out, space_out_bias, mlp_gain, mlp_beta, mlp_up, mlp_up_bias, mlp_down, mlp_down_bias, out_grad, cls_grad):
    frames, patches, model_width = tokens.shape
    clip_count = clip_lengths.shape[0]
    band_reach = MAXLEN - 1
    clip_ends = jnp.cumsum(clip_lengths)
    frame_ids = jnp.arange(frames, dtype=jnp.int32)
    clip_of = lax.optimization_barrier(jnp.sum((frame_ids[:, None] >= clip_ends[None, :]).astype(jnp.int32), axis=1))
    clip_pad = jnp.pad(clip_of, (band_reach, band_reach), constant_values=-1)
    valid = jnp.stack([clip_pad[offset:offset + frames] == clip_of for offset in range(2 * band_reach + 1)], axis=1)
    onehot = (clip_of[:, None] == jnp.arange(clip_count, dtype=jnp.int32)[None, :]).astype(jnp.float32)
    lengths = clip_lengths.astype(jnp.float32)
    tok_rows = frames * patches

    def forward(token_f, cls_f, tgain, tbeta, tin, tqv, tout, tob, tlin, tlb, sgain, sbeta, sin_w, sqv, sout_w, sob, mgain, mbeta, up_w, upb, down_w, downb):
        time_normed = low(norm_rows(low_back(token_f), tgain, tbeta))
        time_qkv = split_cols(time_normed, tin, qkv_bias(tqv))
        time_att = low(low_back(time_attention(time_qkv[:, :, 0], time_qkv[:, :, 1], time_qkv[:, :, 2], valid)))
        time_mid = low(low_back(matmul(time_att, tout) + tob))
        time_res = low(low_back(matmul(time_mid, tlin) + tlb))
        mid = token_f + time_res
        cls_rows = matmul(onehot, cls_f)
        space_in = jnp.concatenate([cls_rows[:, None, :], mid], axis=1)
        space_normed = low(norm_rows(space_in, sgain, sbeta))
        space_qkv = split_cols(space_normed, sin_w, qkv_bias(sqv))
        space_att = low(low_back(space_attention(space_qkv[:, :, 0], space_qkv[:, :, 1], space_qkv[:, :, 2])))
        space_sum = low_back(matmul(space_att, sout_w) + sob)
        after = mid + space_sum[:, 1:]
        cls_mid = cls_f + matmul(onehot.T, space_sum[:, 0]) / lengths[:, None]
        rows = jnp.concatenate([after.reshape(tok_rows, model_width), cls_mid], axis=0)
        mlp_normed = low(norm_rows(rows, mgain, mbeta))
        pre = matmul(mlp_normed, up_w) + upb
        act = low(jax.nn.gelu(low_back(pre), approximate=False))
        result = rows + matmul(act, down_w) + downb
        return (result[:tok_rows].reshape(frames, patches, model_width), result[tok_rows:])
    params = (tokens, cls_tokens, time_gain, time_beta, time_proj_in, time_qv_bias, time_proj_out, time_out_bias, time_linear, time_linear_bias, space_gain, space_beta, space_proj_in, space_qv_bias, space_proj_out, space_out_bias, mlp_gain, mlp_beta, mlp_up, mlp_up_bias, mlp_down, mlp_down_bias)
    outputs, pull = jax.vjp(forward, *[item.astype(jnp.float32) for item in params])
    grads = pull((out_grad.astype(jnp.float32), cls_grad.astype(jnp.float32)))
    return (outputs[0].astype(jnp.bfloat16), outputs[1].astype(jnp.bfloat16), grads[0].astype(jnp.bfloat16), grads[1], grads[2], grads[3], grads[4], grads[5], grads[6], grads[7], grads[8], grads[9], grads[10], grads[11], grads[12], grads[13], grads[14], grads[15], grads[16], grads[17], grads[18], grads[19], grads[20], grads[21])
```

```python
import functools

import jax
import jax.numpy as jnp
from jax import lax
from jax.experimental import pallas as pl
from jax.experimental.pallas import tpu as pltpu
from jax.sharding import PartitionSpec as P

HEAD_DIM = 64
PATCH = 196
MAXLEN = 8


EPS = 1e-06
NEG = -1e30
FLOAT = jnp.float32
BHALF = jnp.bfloat16


def matmul_plain(left, right):
    return jnp.dot(left, right, preferred_element_type=FLOAT)


def matmul_tn(left, right):
    return lax.dot_general(left, right, (((0,), (0,)), ((), ())), preferred_element_type=FLOAT)


def matmul_nt(left, right):
    return lax.dot_general(left, right, (((1,), (1,)), ((), ())), preferred_element_type=FLOAT)


def exact_tn(left, right):
    return lax.dot_general(
        left,
        right,
        (((0,), (0,)), ((), ())),
        precision=lax.Precision.HIGHEST,
        preferred_element_type=FLOAT,
    )


def exact_nn(left, right):
    return jnp.dot(left, right, precision=lax.Precision.HIGHEST, preferred_element_type=FLOAT)


def layer_norm(rows, gain, shift):
    center = rows - jnp.mean(rows, axis=-1, keepdims=True)
    invstd = lax.rsqrt(jnp.mean(center * center, axis=-1, keepdims=True) + EPS)
    normed = center * invstd
    return (normed * gain + shift, normed, invstd)


def norm_back(grad_out, gain, normed, invstd, row_weight):
    feature_count = grad_out.shape[-1]
    grad_norm = grad_out * gain
    weighted = grad_out * row_weight
    gain_grad = jnp.sum((weighted * normed).reshape(-1, feature_count), axis=0)
    shift_grad = jnp.sum(weighted.reshape(-1, feature_count), axis=0)
    first_mean = jnp.mean(grad_norm, axis=-1, keepdims=True)
    second_mean = jnp.mean(grad_norm * normed, axis=-1, keepdims=True)
    return (invstd * (grad_norm - first_mean - normed * second_mean), gain_grad, shift_grad)


def qkv_shift(pair):
    return jnp.stack([pair[0], jnp.zeros_like(pair[0]), pair[1]], axis=0).reshape(-1)


def pair_sums(grad_qkv, local_width):
    sums = jnp.sum(grad_qkv.astype(FLOAT).reshape(-1, 3, local_width), axis=0)
    return jnp.stack([sums[0], sums[2]], axis=0)


def gelu_slope(pre):
    normal_cdf = 0.5 * (1.0 + jax.scipy.special.erf(pre * 0.7071067811865476))
    return normal_cdf + pre * jnp.exp(-0.5 * pre * pre) * 0.3989422804014327


def band_stack(values, band_reach):
    frames = values.shape[0]
    padded = jnp.pad(values, ((band_reach, band_reach),) + ((0, 0),) * (values.ndim - 1))
    return jnp.stack(
        [padded[offset : offset + frames] for offset in range(2 * band_reach + 1)], axis=2
    )


def band_return(contrib, band_reach):
    frames = contrib.shape[0]
    padded = jnp.pad(contrib, ((band_reach, band_reach),) + ((0, 0),) * (contrib.ndim - 1))
    total = jnp.zeros((frames,) + contrib.shape[1:2] + contrib.shape[3:], FLOAT)
    for offset in range(2 * band_reach + 1):
        start = 2 * band_reach - offset
        total = total + padded[start : start + frames, :, offset]
    return total


def to_positions(frame_major):
    frames_dev, patches, columns = frame_major.shape
    seq_count = lax.axis_size("seq")
    pos_dev = (patches + seq_count - 1) // seq_count
    padded = jnp.pad(frame_major, ((0, 0), (0, pos_dev * seq_count - patches), (0, 0)))
    moved = lax.all_to_all(
        padded.reshape(frames_dev, seq_count, pos_dev, columns),
        "seq",
        split_axis=1,
        concat_axis=0,
        tiled=True,
    )
    return moved.reshape(frames_dev * seq_count, pos_dev, columns)


def to_frames(pos_major):
    frames_all, pos_dev, columns = pos_major.shape
    seq_count = lax.axis_size("seq")
    moved = lax.all_to_all(
        pos_major.reshape(frames_all, 1, pos_dev, columns),
        "seq",
        split_axis=0,
        concat_axis=1,
        tiled=True,
    )
    return moved.reshape(frames_all // seq_count, seq_count * pos_dev, columns)[:, :PATCH]


def head_cols(pieces):
    return lax.all_gather(pieces, "head", axis=2, tiled=True)


def time_scores(queries, key_band, valid, score_scale):
    raw = (
        jnp.einsum("fphd,fpohd->fpho", queries, key_band, preferred_element_type=FLOAT)
        * score_scale
    )
    return jnp.where(valid[:, None, None, :], raw, NEG)


def time_forward(queries, key_band, value_band, valid, score_scale):
    scores = time_scores(queries, key_band, valid, score_scale)
    largest = jnp.max(scores, axis=-1, keepdims=True)
    exponent = jnp.exp(scores - largest)
    totals = jnp.sum(exponent, axis=-1, keepdims=True)
    attend = (exponent / totals).astype(BHALF)
    result = jnp.einsum("fpho,fpohd->fphd", attend, value_band, preferred_element_type=FLOAT)
    return (result, largest + jnp.log(totals))


def time_backward(
    queries, key_band, value_band, valid, log_total, grad_out, score_scale, band_reach
):
    scores = time_scores(queries, key_band, valid, score_scale)
    attend = jnp.exp(scores - log_total)
    grad_attend = jnp.einsum("fphd,fpohd->fpho", grad_out, value_band, preferred_element_type=FLOAT)
    row_dot = jnp.sum(attend * grad_attend, axis=-1, keepdims=True)
    grad_score = (attend * (grad_attend - row_dot)).astype(BHALF)
    grad_query = (
        jnp.einsum("fpho,fpohd->fphd", grad_score, key_band, preferred_element_type=FLOAT)
        * score_scale
    )
    key_part = (
        jnp.einsum("fpho,fphd->fpohd", grad_score, queries, preferred_element_type=FLOAT)
        * score_scale
    )
    value_part = jnp.einsum(
        "fpho,fphd->fpohd", attend.astype(BHALF), grad_out, preferred_element_type=FLOAT
    )
    return (grad_query, band_return(key_part, band_reach), band_return(value_part, band_reach))


def space_forward(queries, key_rows, value_rows, score_scale):
    scores = (
        jnp.einsum("fqhd,fkhd->fhqk", queries, key_rows, preferred_element_type=FLOAT) * score_scale
    )
    largest = jnp.max(scores, axis=-1, keepdims=True)
    exponent = jnp.exp(scores - largest)
    totals = jnp.sum(exponent, axis=-1, keepdims=True)
    attend = (exponent / totals).astype(BHALF)
    result = jnp.einsum("fhqk,fkhd->fqhd", attend, value_rows, preferred_element_type=FLOAT)
    return (result, largest + jnp.log(totals))


def space_backward(queries, key_rows, value_rows, log_total, grad_out, score_scale):
    scores = (
        jnp.einsum("fqhd,fkhd->fhqk", queries, key_rows, preferred_element_type=FLOAT) * score_scale
    )
    attend = jnp.exp(scores - log_total)
    grad_attend = jnp.einsum("fqhd,fkhd->fhqk", grad_out, value_rows, preferred_element_type=FLOAT)
    row_dot = jnp.sum(attend * grad_attend, axis=-1, keepdims=True)
    grad_score = (attend * (grad_attend - row_dot)).astype(BHALF)
    grad_query = (
        jnp.einsum("fhqk,fkhd->fqhd", grad_score, key_rows, preferred_element_type=FLOAT)
        * score_scale
    )
    grad_key = (
        jnp.einsum("fhqk,fqhd->fkhd", grad_score, queries, preferred_element_type=FLOAT)
        * score_scale
    )
    grad_value = jnp.einsum(
        "fhqk,fqhd->fkhd", attend.astype(BHALF), grad_out, preferred_element_type=FLOAT
    )
    return (grad_query, grad_key, grad_value)


def body(
    tokens,
    cls_tokens,
    clip_lengths,
    time_gain,
    time_beta,
    time_proj_in,
    time_qv_bias,
    time_proj_out,
    time_out_bias,
    time_linear,
    time_linear_bias,
    space_gain,
    space_beta,
    space_proj_in,
    space_qv_bias,
    space_proj_out,
    space_out_bias,
    mlp_gain,
    mlp_beta,
    mlp_up,
    mlp_up_bias,
    mlp_down,
    mlp_down_bias,
    out_grad,
    cls_grad,
):
    frames_dev, patches, model_width = tokens.shape
    seq_count = lax.axis_size("seq")
    frames_all = frames_dev * seq_count
    clip_count = clip_lengths.shape[0]
    local_width = time_proj_in.shape[2]
    local_heads = local_width // HEAD_DIM
    band_reach = MAXLEN - 1
    score_scale = HEAD_DIM ** (-0.5)
    seq_rank = lax.axis_index("seq")
    head_rank = lax.axis_index("head")
    clip_ends = jnp.sum(
        jnp.where(jnp.tri(clip_lengths.shape[0], dtype=bool), clip_lengths[None, :], 0), axis=1
    )
    frame_ids = jnp.arange(frames_all, dtype=jnp.int32)
    clip_of = jnp.sum((frame_ids[:, None] >= clip_ends[None, :]).astype(jnp.int32), axis=1)
    clip_pad = jnp.pad(clip_of, (band_reach, band_reach), constant_values=-1)
    valid = jnp.stack(
        [clip_pad[offset : offset + frames_all] == clip_of for offset in range(2 * band_reach + 1)],
        axis=1,
    )
    local_clip = lax.dynamic_slice_in_dim(clip_of, seq_rank * frames_dev, frames_dev)
    onehot = (local_clip[:, None] == jnp.arange(clip_count, dtype=jnp.int32)[None, :]).astype(FLOAT)
    lengths = clip_lengths.astype(FLOAT)
    time_in = to_positions(tokens)
    pos_dev = time_in.shape[1]
    time_rows = frames_all * pos_dev
    time_normed, time_stat, time_inv = layer_norm(time_in.astype(FLOAT), time_gain, time_beta)
    time_normed = time_normed.astype(BHALF).reshape(time_rows, model_width)
    time_in_mat = time_proj_in.reshape(model_width, 3 * local_width)
    time_qkv = (
        (matmul_plain(time_normed, time_in_mat) + qkv_shift(time_qv_bias))
        .astype(BHALF)
        .reshape(frames_all, pos_dev, 3, local_heads, HEAD_DIM)
    )
    time_query = time_qkv[:, :, 0]
    time_keys = band_stack(time_qkv[:, :, 1], band_reach)
    time_values = band_stack(time_qkv[:, :, 2], band_reach)
    time_att, time_log = time_forward(time_query, time_keys, time_values, valid, score_scale)
    time_att = time_att.astype(BHALF).reshape(time_rows, local_width)
    time_mid = (
        lax.psum(matmul_plain(time_att, time_proj_out).astype(jnp.bfloat16), "head").astype(
            jnp.float32
        )
        + time_out_bias
    ).astype(BHALF)
    col_start = head_rank * local_width
    linear_cols = lax.dynamic_slice_in_dim(time_linear, col_start, local_width, 1)
    linear_shift = lax.dynamic_slice_in_dim(time_linear_bias, col_start, local_width)
    time_part = (
        (matmul_plain(time_mid, linear_cols) + linear_shift)
        .astype(BHALF)
        .reshape(frames_all, pos_dev, local_width)
    )
    time_res = to_frames(head_cols(time_part))
    mid = tokens.astype(FLOAT) + time_res.astype(FLOAT)
    span_rows = patches + 1
    space_rows = frames_dev * span_rows
    cls_rows = matmul_plain(onehot.astype(BHALF), cls_tokens)
    space_in = jnp.concatenate([cls_rows[:, None, :], mid], axis=1)
    space_normed, space_stat, space_inv = layer_norm(space_in, space_gain, space_beta)
    space_normed = space_normed.astype(BHALF).reshape(space_rows, model_width)
    space_in_mat = space_proj_in.reshape(model_width, 3 * local_width)
    space_qkv = (
        (matmul_plain(space_normed, space_in_mat) + qkv_shift(space_qv_bias))
        .astype(BHALF)
        .reshape(frames_dev, span_rows, 3, local_heads, HEAD_DIM)
    )
    space_query = space_qkv[:, :, 0]
    space_keys = space_qkv[:, :, 1]
    space_values = space_qkv[:, :, 2]
    space_att, space_log = space_forward(space_query, space_keys, space_values, score_scale)
    space_att = space_att.astype(BHALF).reshape(space_rows, local_width)
    space_sum = (
        lax.psum(matmul_plain(space_att, space_proj_out).astype(jnp.bfloat16), "head").astype(
            jnp.float32
        )
        + space_out_bias
    ).reshape(frames_dev, span_rows, model_width)
    after = mid + space_sum[:, 1:]
    cls_part = exact_tn(onehot, space_sum[:, 0])
    cls_mid = cls_tokens.astype(FLOAT) + lax.psum(cls_part, "seq") / lengths[:, None]
    tok_rows = frames_dev * patches
    rows = jnp.concatenate([after.reshape(tok_rows, model_width), cls_mid], axis=0)
    mlp_normed, mlp_stat, mlp_inv = layer_norm(rows, mlp_gain, mlp_beta)
    mlp_normed = mlp_normed.astype(BHALF)
    pre = matmul_plain(mlp_normed, mlp_up) + mlp_up_bias
    act = jax.nn.gelu(pre, approximate=False).astype(BHALF)
    result = (
        rows
        + lax.psum(matmul_plain(act, mlp_down).astype(jnp.bfloat16), "head").astype(jnp.float32)
        + mlp_down_bias
    )
    block_out = result[:tok_rows].reshape(frames_dev, patches, model_width).astype(BHALF)
    cls_out = result[tok_rows:].astype(BHALF)
    first_seq = (seq_rank == 0).astype(FLOAT)
    keep_rows = jnp.concatenate(
        [jnp.ones((tok_rows, 1), FLOAT), jnp.ones((clip_count, 1), FLOAT) * first_seq], axis=0
    )
    keep_half = keep_rows.astype(BHALF)
    grad_rows = jnp.concatenate([out_grad.reshape(tok_rows, model_width), cls_grad], axis=0)
    down_grad = matmul_tn(act * keep_half, grad_rows)
    down_shift_grad = jnp.sum(grad_rows.astype(FLOAT) * keep_rows, axis=0)
    grad_pre = (matmul_nt(grad_rows, mlp_down) * gelu_slope(pre)).astype(BHALF)
    up_grad = matmul_tn(mlp_normed * keep_half, grad_pre)
    up_shift_grad = jnp.sum(grad_pre.astype(FLOAT) * keep_rows, axis=0)
    grad_mlp_norm = lax.psum(matmul_nt(grad_pre, mlp_up).astype(jnp.bfloat16), "head").astype(
        jnp.float32
    )
    grad_mlp_in, mlp_gain_grad, mlp_beta_grad = norm_back(
        grad_mlp_norm, mlp_gain, mlp_stat, mlp_inv, keep_rows
    )
    grad_total = grad_rows.astype(FLOAT) + grad_mlp_in
    grad_after = grad_total[:tok_rows].reshape(frames_dev, patches, model_width)
    grad_cls_mid = grad_total[tok_rows:]
    cls_share = exact_nn(onehot, grad_cls_mid / lengths[:, None])
    grad_space_sum = (
        jnp.concatenate([cls_share[:, None, :], grad_after], axis=1)
        .astype(BHALF)
        .reshape(space_rows, model_width)
    )
    space_out_grad = matmul_tn(space_att, grad_space_sum)
    space_shift_grad = jnp.sum(grad_space_sum.astype(FLOAT), axis=0)
    grad_space_att = (
        matmul_nt(grad_space_sum, space_proj_out)
        .astype(BHALF)
        .reshape(frames_dev, span_rows, local_heads, HEAD_DIM)
    )
    space_grad_query, space_grad_key, space_grad_value = space_backward(
        space_query, space_keys, space_values, space_log, grad_space_att, score_scale
    )
    grad_space_qkv = (
        jnp.stack([space_grad_query, space_grad_key, space_grad_value], axis=2)
        .astype(BHALF)
        .reshape(space_rows, 3 * local_width)
    )
    space_in_grad = matmul_tn(space_normed, grad_space_qkv).reshape(model_width, 3, local_width)
    space_pair_grad = pair_sums(grad_space_qkv, local_width)
    grad_space_norm = (
        lax.psum(matmul_nt(grad_space_qkv, space_in_mat).astype(jnp.bfloat16), "head")
        .astype(jnp.float32)
        .reshape(frames_dev, span_rows, model_width)
    )
    grad_space_in, space_gain_grad, space_beta_grad = norm_back(
        grad_space_norm, space_gain, space_stat, space_inv, 1.0
    )
    grad_mid = grad_after + grad_space_in[:, 1:]
    cls_in_part = exact_tn(onehot, grad_space_in[:, 0])
    grad_time_res = to_positions(grad_mid.astype(BHALF)).reshape(time_rows, model_width)
    linear_grad = matmul_tn(
        time_mid, lax.dynamic_slice_in_dim(grad_time_res, col_start, local_width, 1)
    )
    linear_shift_grad = jnp.sum(grad_time_res.astype(FLOAT), axis=0)
    grad_time_mid = matmul_nt(grad_time_res, time_linear).astype(BHALF)
    time_out_grad = matmul_tn(time_att, grad_time_mid)
    time_shift_grad = jnp.sum(grad_time_mid.astype(FLOAT), axis=0)
    grad_time_att = (
        matmul_nt(grad_time_mid, time_proj_out)
        .astype(BHALF)
        .reshape(frames_all, pos_dev, local_heads, HEAD_DIM)
    )
    time_grad_query, time_grad_key, time_grad_value = time_backward(
        time_query, time_keys, time_values, valid, time_log, grad_time_att, score_scale, band_reach
    )
    grad_time_qkv = (
        jnp.stack([time_grad_query, time_grad_key, time_grad_value], axis=2)
        .astype(BHALF)
        .reshape(time_rows, 3 * local_width)
    )
    time_in_grad = matmul_tn(time_normed, grad_time_qkv).reshape(model_width, 3, local_width)
    time_pair_grad = pair_sums(grad_time_qkv, local_width)
    grad_time_norm = (
        lax.psum(matmul_nt(grad_time_qkv, time_in_mat).astype(jnp.bfloat16), "head")
        .astype(jnp.float32)
        .reshape(frames_all, pos_dev, model_width)
    )
    grad_time_in, time_gain_grad, time_beta_grad = norm_back(
        grad_time_norm, time_gain, time_stat, time_inv, 1.0
    )
    grad_tokens_time = to_frames(grad_time_in.astype(BHALF))
    tokens_grad = (grad_mid + grad_tokens_time.astype(FLOAT)).astype(BHALF)
    summed = (
        lax.psum_scatter(time_gain_grad, "seq", scatter_dimension=0, tiled=True),
        lax.psum_scatter(time_in_grad, "seq", scatter_dimension=0, tiled=True),
        lax.psum_scatter(time_out_grad, "seq", scatter_dimension=1, tiled=True),
        lax.psum_scatter(linear_grad, "seq", scatter_dimension=0, tiled=True),
        lax.psum_scatter(space_gain_grad, "seq", scatter_dimension=0, tiled=True),
        lax.psum_scatter(space_in_grad, "seq", scatter_dimension=0, tiled=True),
        lax.psum_scatter(space_out_grad, "seq", scatter_dimension=1, tiled=True),
        lax.psum_scatter(mlp_gain_grad, "seq", scatter_dimension=0, tiled=True),
        lax.psum_scatter(up_grad, "seq", scatter_dimension=0, tiled=True),
        lax.psum_scatter(down_grad, "seq", scatter_dimension=1, tiled=True),
        lax.psum_scatter(cls_in_part, "seq", scatter_dimension=1, tiled=True),
    )
    shifts = lax.psum(
        (
            time_beta_grad,
            time_pair_grad,
            time_shift_grad,
            linear_shift_grad,
            space_beta_grad,
            space_pair_grad,
            space_shift_grad,
            mlp_beta_grad,
            up_shift_grad,
            down_shift_grad,
        ),
        "seq",
    )
    col_width = model_width // seq_count
    cls_direct = lax.dynamic_slice_in_dim(grad_cls_mid, seq_rank * col_width, col_width, 1)
    cls_tokens_grad = summed[10] + cls_direct
    return (
        block_out,
        cls_out,
        tokens_grad,
        cls_tokens_grad,
        summed[0],
        shifts[0],
        summed[1],
        shifts[1],
        summed[2],
        shifts[2],
        summed[3],
        shifts[3],
        summed[4],
        shifts[4],
        summed[5],
        shifts[5],
        summed[6],
        shifts[6],
        summed[7],
        shifts[7],
        summed[8],
        shifts[8],
        summed[9],
        shifts[9],
    )


MESH = pl.DeviceIdType.MESH
ROWS = 208
HALF = 16
SLOTS = 2 * HALF
BLOCK = 32


def dot_nn(left, right):
    return jnp.dot(left, right, preferred_element_type=FLOAT)


def dot_nt(left, right):
    return lax.dot_general(left, right, (((1,), (1,)), ((), ())), preferred_element_type=FLOAT)


def dot_tn(left, right):
    return lax.dot_general(left, right, (((0,), (0,)), ((), ())), preferred_element_type=FLOAT)


def iota(shape, axis):
    return lax.broadcasted_iota(jnp.int32, shape, axis)


def scratch_shapes(dims):
    frames, seq, width, model, hidden = dims["frames"], dims["seq"], dims["width"], dims["model"], dims["hidden"]
    rows, every, heads = frames * ROWS, frames * seq, width // HEAD_DIM
    half, low = model // 2, BHALF
    vm = pltpu.VMEM
    shapes = dict(
        tok=vm((frames, dims["patches"], model), low),
        out_grad=vm((frames, dims["patches"], model), low),
        w_ti=vm((model, 3 * width), low),
        w_si=vm((model, 3 * width), low),
        w_tl=vm((model, model), low),
        w_up=vm((model, hidden), low),
        w_dn=vm((hidden, model), low),
        w_to=vm((2, 2, width, model), low),
        w_so=vm((2, 2, width, model), low),
        x32=vm((rows, model), FLOAT),
        gr32=vm((rows, model), FLOAT),
        t32=vm((rows, model), FLOAT),
        u32=vm((rows, model), FLOAT),
        dact=vm((rows, hidden), FLOAT),
        xh_t=vm((rows, model), FLOAT),
        xh_s=vm((rows, model), FLOAT),
        xh_m=vm((rows, model), FLOAT),
        inv=vm((3, rows, 128), FLOAT),
        n_t=vm((rows, model), low),
        n_s=vm((rows, model), low),
        n_m=vm((rows, model), low),
        gr16=vm((rows, model), low),
        mid16=vm((rows, model), low),
        act=vm((rows, hidden), low),
        act_k=vm((rows, hidden), low),
        gpre=vm((rows, hidden), low),
        gpre_k=vm((rows, hidden), low),
        gss=vm((rows, model), low),
        gtr=vm((rows, model), low),
        gtm=vm((rows, model), low),
        sqkv=vm((rows, 3 * width), low),
        dsq=vm((rows, 3 * width), low),
        dtq=vm((rows, 3 * width), low),
        gatt=vm((rows, width), low),
        sel=vm((seq * SLOTS, ROWS), low),
        les=vm((ROWS, seq * SLOTS), low),
        tmask=vm((every * HALF, every * HALF), FLOAT),
        p_t=vm((2 * heads, every * HALF, every * HALF), FLOAT),
        p_s=vm((frames * heads, ROWS, ROWS), FLOAT),
        q_send=vm((seq, 2, frames, HALF, 3 * width), low),
        q_pos=vm((2, every, HALF, 3 * width), low),
        a_pos=vm((2, every, HALF, width), low),
        a_recv=vm((seq, 2, frames, HALF, width), low),
        g_send=vm((seq, 2, frames, HALF, width), low),
        g_pos=vm((2, every, HALF, width), low),
        d_pos=vm((2, every, HALF, 3 * width), low),
        d_recv=vm((seq, 2, frames, HALF, 3 * width), low),
        att_t=vm((2, 2, rows, width), low),
        att_s=vm((2, 2, rows, width), low),
        part=vm((4, 2, rows, half), low),
        pair=vm((4, rows, half), low),
        other=vm((4, rows, half), low),
        total=vm((4, 2, rows, half), low),
        cls_send=vm((8, model), FLOAT),
        cls_recv=vm((seq, 8, model), FLOAT),
        gcm=vm((8, model), FLOAT),
        v_send=vm((3, 8, model), FLOAT),
        v_recv=vm((3, seq, 8, model), FLOAT),
    )
    for name, columns in grad_columns(dims):
        shapes["g_" + name] = vm((seq // 2, 2, model // seq, columns), low)
        shapes["y_" + name] = vm((seq // 2, model // seq, columns), low)
        shapes["z_" + name] = vm((seq // 2, model // seq, columns), low)
    shapes["load"] = pltpu.SemaphoreType.DMA((16,))
    shapes["sent"] = pltpu.SemaphoreType.DMA((160,))
    shapes["got"] = pltpu.SemaphoreType.DMA((160,))
    return shapes


def grad_columns(dims):
    width, model, hidden = dims["width"], dims["model"], dims["hidden"]
    return (
        ("dn", hidden),
        ("up", hidden),
        ("si", 3 * width),
        ("so", width),
        ("tl", width),
        ("to", width),
        ("ti", 3 * width),
    )


INPUTS = ("lens", "cls", "cls_grad", "vec", "h_tok", "h_og", "h_ti", "h_to", "h_tl", "h_si", "h_so", "h_up", "h_dn")
OUTPUTS = ("o_blk", "o_cls", "o_tok", "o_vec")


class Refs:
    pass


def layer_kernel(dims, names, *refs):
    k = Refs()
    for name, ref in zip(names, refs):
        setattr(k, name, ref)
    frames, seq, width, model, hidden = dims["frames"], dims["seq"], dims["width"], dims["model"], dims["hidden"]
    patches, clips, pos = dims["patches"], dims["clips"], dims["pos"]
    rows, every, heads, half = frames * ROWS, frames * seq, width // HEAD_DIM, model // 2
    zs = seq // 2
    scale = HEAD_DIM ** (-0.5)
    s, h = lax.axis_index("seq"), lax.axis_index("head")
    z, y = s // 2, s % 2
    x, c = h // 2, h % 2
    other_c = 1 - c
    sister, across = (s, x * 2 + other_c), (s, (1 - x) * 2 + c)
    y_peer = (z * 2 + 1 - y, h)
    z_peers = [((z + i) % zs) for i in range(1, zs)]
    peers = [((z + i) % zs) * 2 + (y + j) % 2 for i in range(zs) for j in range(2) if i or j]
    used = [0]

    def send(src, dst, device):
        index = used[0]
        used[0] += 1
        copy = pltpu.make_async_remote_copy(
            src_ref=src,
            dst_ref=dst,
            send_sem=k.sent.at[index],
            recv_sem=k.got.at[index],
            device_id=device,
            device_id_type=MESH,
        )
        copy.start()
        unsent.append(copy)
        return copy

    unsent = []
    loads = [0]

    def load(src, dst):
        copy = pltpu.make_async_copy(src, dst, k.load.at[loads[0]])
        loads[0] += 1
        copy.start()
        return copy

    def blocks(body, unroll=False):
        if unroll:
            for i in range(rows // BLOCK):
                body(pl.ds(i * BLOCK, BLOCK))
        else:

            def step(i, carry):
                body(pl.ds(pl.multiple_of(i * BLOCK, BLOCK), BLOCK))
                return carry

            lax.fori_loop(0, rows // BLOCK, step, 0)

    l_tok = load(k.h_tok, k.tok)
    l_ti = load(k.h_ti, k.w_ti)
    l_to = load(k.h_to, k.w_to.at[0, c])
    l_so = load(k.h_so, k.w_so.at[0, c])
    l_og = load(k.h_og, k.out_grad)
    l_dn = load(k.h_dn, k.w_dn)
    l_tl = load(k.h_tl, k.w_tl)
    l_si = load(k.h_si, k.w_si)
    l_up = load(k.h_up, k.w_up)
    barrier = pltpu.get_barrier_semaphore()
    everyone = [(p, h) for p in peers] + [sister, across]
    for device in everyone:
        pl.semaphore_signal(barrier, inc=1, device_id=device, device_id_type=MESH)

    def vec(i):
        return k.vec[i : i + 1, :]

    t_gain, t_beta, t_ob, t_lb, s_gain, s_beta, s_ob, m_gain, m_beta, m_db, m_ub = [vec(i) for i in range(11)]
    t_qb, s_qb = vec(11)[:, : 3 * width], vec(12)[:, : 3 * width]

    slot, row = iota((seq * SLOTS, ROWS), 0), iota((seq * SLOTS, ROWS), 1)
    place = (slot // SLOTS) * pos + slot % SLOTS
    k.sel[...] = jnp.where((place == row) & (slot % SLOTS < pos) & (row < patches), 1.0, 0.0).astype(BHALF)
    row, slot = iota((ROWS, seq * SLOTS), 0), iota((ROWS, seq * SLOTS), 1)
    place = (slot // SLOTS) * pos + slot % SLOTS
    k.les[...] = jnp.where((place == row) & (slot % SLOTS < pos) & (row < patches), 1.0, 0.0).astype(BHALF)
    ends = []
    for i in range(clips):
        ends.append(k.lens[i] + (ends[-1] if i else 0))

    def clip_of(frame):
        total = (frame >= ends[0]).astype(jnp.int32)
        for end in ends[1:]:
            total = total + (frame >= end).astype(jnp.int32)
        return total

    span = every * HALF
    left, right = iota((span, span), 0), iota((span, span), 1)
    same = (left % HALF == right % HALF) & (clip_of(left // HALF) == clip_of(right // HALF))
    near = jnp.abs(left // HALF - right // HALF) < MAXLEN
    k.tmask[...] = jnp.where(same & near, 0.0, NEG)
    onehot = []
    for f in range(frames):
        own = clip_of(jnp.full((1, model), s * frames + f, jnp.int32))
        onehot.append([(own == i).astype(FLOAT) for i in range(clips)])
    per_len = [1.0 / jnp.full((1, model), k.lens[i], jnp.int32).astype(FLOAT) for i in range(clips)]
    cls32 = k.cls[...].astype(FLOAT)
    cls_row = [sum(onehot[f][i] * cls32[i : i + 1] for i in range(clips)) for f in range(frames)]
    tail = ROWS - patches

    def set_tail(ref, f, first):
        used_rows = sum(r.shape[0] for r in first)
        fill = [jnp.zeros((tail - used_rows, model), FLOAT)] if used_rows < tail else []
        ref[f * ROWS + patches : (f + 1) * ROWS, :] = jnp.concatenate(list(first) + fill, axis=0)

    def eight(values):
        missing = 8 - sum(v.shape[0] for v in values)
        fill = [jnp.zeros((missing, model), FLOAT)] if missing else []
        return jnp.concatenate(list(values) + fill, axis=0)

    def norm(src, which, gain, shift, xhat, out):
        def body(r):
            v = src[r, :]
            center = v - jnp.mean(v, axis=-1, keepdims=True)
            invstd = lax.rsqrt(jnp.mean(center * center, axis=-1, keepdims=True) + EPS)
            n = center * invstd
            xhat[r, :] = n
            k.inv[which, r, :] = jnp.broadcast_to(invstd, (BLOCK, 128))
            out[r, :] = (n * gain + shift).astype(BHALF)

        blocks(body, unroll=dims["unroll"])

    l_tok.wait()
    for f in range(frames):
        k.x32[f * ROWS : f * ROWS + patches, :] = k.tok[f].astype(FLOAT)
        set_tail(k.x32, f, [])
    norm(k.x32, 0, t_gain, t_beta, k.xh_t, k.n_t)
    l_ti.wait()

    def to_slots(f, value, dst):
        columns = value.shape[-1]
        moved = dot_nn(k.sel[...], value).astype(BHALF)
        dst[:, :, f] = moved.reshape(seq, 2, HALF, columns)

    def from_slots(f, src):
        columns = src.shape[-1]
        return dot_nn(k.les[...], src[:, :, f].reshape(seq * SLOTS, columns))

    for f in range(frames):
        r = slice(f * ROWS, (f + 1) * ROWS)
        qkv = (dot_nn(k.n_t[r, :], k.w_ti[...]) + t_qb).astype(BHALF)
        to_slots(f, qkv, k.q_send)
    l_to.wait()
    l_so.wait()
    pl.semaphore_wait(barrier, len(everyone))
    mine = pl.ds(frames * s, frames)

    def scatter(src, dst):
        copies = [send(src.at[p], dst.at[:, mine], (p, h)) for p in peers]
        dst[:, mine] = src[s]
        return copies

    def gather(src, dst):
        copies = [send(src.at[:, pl.ds(frames * p, frames)], dst.at[s], (p, h)) for p in peers]
        dst[s] = src[:, mine]
        return copies

    def arrived(copies):
        for copy in copies:
            copy.wait_recv()

    q_copies = scatter(k.q_send, k.q_pos)

    def share(ref):
        return send(ref.at[0, c], ref.at[0, c], sister), send(ref.at[0, c], ref.at[1, c], across)

    def pass_on(ref):
        return send(ref.at[1, c], ref.at[1, c], sister)

    w_to_near, w_to_far = share(k.w_to)
    w_so_near, w_so_far = share(k.w_so)

    l_og.wait()
    cls_g = k.cls_grad[...].astype(FLOAT)
    for f in range(frames):
        k.gr32[f * ROWS : f * ROWS + patches, :] = k.out_grad[f].astype(FLOAT)
        set_tail(k.gr32, f, [cls_g] if f == 0 else [])

    def cast_rows(src, dst):
        def body(r):
            dst[r, :] = src[r, :].astype(BHALF)

        blocks(body)

    cast_rows(k.gr32, k.gr16)
    l_dn.wait()
    k.dact[...] = dot_nt(k.gr16[...], k.w_dn[...])
    w_to_far.wait_recv()
    w_to_last = pass_on(k.w_to)
    w_so_far.wait_recv()
    w_so_last = pass_on(k.w_so)

    def attend(q, key, value, mask, p_ref):
        scores = dot_nt(q, key) * scale + mask
        e = jnp.exp(scores - jnp.max(scores, axis=-1, keepdims=True))
        p = e * (1.0 / jnp.sum(e, axis=-1, keepdims=True))
        p_ref[...] = p
        return dot_nn(p.astype(BHALF), value).astype(BHALF)

    def attend_back(q, key, value, grad, p_ref):
        p = p_ref[...]
        grad_p = p * dot_nt(grad, value)
        grad_s = (grad_p - p * jnp.sum(grad_p, axis=-1, keepdims=True)).astype(BHALF)
        grad_q = (dot_nn(grad_s, key) * scale).astype(BHALF)
        grad_k = (dot_tn(grad_s, q) * scale).astype(BHALF)
        grad_v = dot_tn(p.astype(BHALF), grad).astype(BHALF)
        return grad_q, grad_k, grad_v

    def head_of(value, part, j):
        at = part * width + j * HEAD_DIM
        return value[:, at : at + HEAD_DIM]

    arrived(q_copies)
    for b in range(2):
        qkv = k.q_pos[b].reshape(span, 3 * width)
        out = [
            attend(head_of(qkv, 0, j), head_of(qkv, 1, j), head_of(qkv, 2, j), k.tmask[...], k.p_t.at[b * heads + j])
            for j in range(heads)
        ]
        k.a_pos[b] = jnp.concatenate(out, axis=-1).reshape(every, HALF, width)
    a_copies = gather(k.a_pos, k.a_recv)
    arrived(a_copies)
    for f in range(frames):
        k.att_t[0, c, f * ROWS : (f + 1) * ROWS, :] = from_slots(f, k.a_recv).astype(BHALF)

    def project(att, weight):
        near, far = share(att)
        near.wait_recv()
        k.t32[...] = dot_nn(att[0, 0], weight[0, 0]) + dot_nn(att[0, 1], weight[0, 1])
        far.wait_recv()
        last = pass_on(att)
        last.wait_recv()
        k.u32[...] = dot_nn(att[1, 0], weight[1, 0]) + dot_nn(att[1, 1], weight[1, 1])

    arrived([w_to_near, w_to_last])
    project(k.att_t, k.w_to)

    def mid_rows(r):
        k.mid16[r, :] = (k.t32[r, :] + k.u32[r, :] + t_ob).astype(BHALF)

    blocks(mid_rows)
    l_tl.wait()
    k.t32[...] = dot_nn(k.mid16[...], k.w_tl[...])

    def add_res(r):
        k.x32[r, :] = k.x32[r, :] + (k.t32[r, :] + t_lb).astype(BHALF).astype(FLOAT)

    blocks(add_res)
    for f in range(frames):
        set_tail(k.x32, f, [cls_row[f]])

    norm(k.x32, 1, s_gain, s_beta, k.xh_s, k.n_s)
    l_si.wait()
    k.sqkv[...] = (dot_nn(k.n_s[...], k.w_si[...]) + s_qb).astype(BHALF)
    in_frame = jnp.where(iota((1, ROWS), 1) < patches + 1, 0.0, NEG)
    for f in range(frames):
        r = slice(f * ROWS, (f + 1) * ROWS)
        qkv = k.sqkv[r, :]
        out = [
            attend(head_of(qkv, 0, j), head_of(qkv, 1, j), head_of(qkv, 2, j), in_frame, k.p_s.at[f * heads + j])
            for j in range(heads)
        ]
        k.att_s[0, c, r, :] = jnp.concatenate(out, axis=-1)
    arrived([w_so_near, w_so_last])
    project(k.att_s, k.w_so)
    at = [slice(f * ROWS + patches, f * ROWS + patches + 1) for f in range(frames)]
    space_cls = [k.t32[r, :] + k.u32[r, :] + s_ob for r in at]
    parts = [sum(onehot[f][i] * space_cls[f] for f in range(frames)) for i in range(clips)]
    k.cls_send[...] = eight(parts)
    cls_copies = [send(k.cls_send, k.cls_recv.at[s], (p, h)) for p in peers]
    k.cls_recv[s] = k.cls_send[...]

    def add_space(r):
        k.x32[r, :] = k.x32[r, :] + (k.t32[r, :] + k.u32[r, :] + s_ob)

    blocks(add_space)
    arrived(cls_copies)
    cls_sum = k.cls_recv[0]
    for i in range(1, seq):
        cls_sum = cls_sum + k.cls_recv[i]
    cls_mid = [cls32[i : i + 1] + cls_sum[i : i + 1] * per_len[i] for i in range(clips)]
    for f in range(frames):
        set_tail(k.x32, f, cls_mid if f == 0 else [])

    norm(k.x32, 2, m_gain, m_beta, k.xh_m, k.n_m)
    l_up.wait()
    k.t32[...] = dot_nn(k.n_m[...], k.w_up[...])
    first_seq = jnp.where(s == 0, 1.0, 0.0)

    def kept(r):
        at = r.start + iota((BLOCK, 1), 0)
        return jnp.where((at >= patches) & (at < ROWS), first_seq, 1.0)

    def gelu_rows(r):
        pre = k.t32[r, :] + m_ub
        cdf = 0.5 * (1.0 + lax.erf(pre * 0.7071067811865476))
        slope = cdf + pre * jnp.exp(-0.5 * pre * pre) * 0.3989422804014327
        act = pre * cdf
        grad = k.dact[r, :] * slope
        keep = kept(r)
        k.act[r, :] = act.astype(BHALF)
        k.act_k[r, :] = (act * keep).astype(BHALF)
        k.gpre[r, :] = grad.astype(BHALF)
        k.gpre_k[r, :] = (grad * keep).astype(BHALF)

    blocks(gelu_rows)

    def sum_open(i, lhs, rhs, dot):
        for b in range(2):
            cut = slice(b * half, (b + 1) * half)
            k.part[i, b] = dot(lhs[...], rhs[cut, :] if dot is dot_nt else rhs[:, cut]).astype(BHALF)
        return send(k.part.at[i, other_c], k.pair.at[i], sister)

    def sum_across(i, copy):
        copy.wait_recv()
        k.part[i, c] = (k.part[i, c].astype(FLOAT) + k.pair[i].astype(FLOAT)).astype(BHALF)
        return send(k.part.at[i, c], k.other.at[i], across)

    def sum_close(i, copy):
        copy.wait_recv()
        k.total[i, c] = (k.part[i, c].astype(FLOAT) + k.other[i].astype(FLOAT)).astype(BHALF)
        return send(k.total.at[i, c], k.total.at[i, c], sister)

    def sum_rows(i, r):
        return jnp.concatenate([k.total[i, 0, r, :], k.total[i, 1, r, :]], axis=-1).astype(FLOAT)

    def grad_open(name, lhs, rhs):
        g, got = getattr(k, "g_" + name), getattr(k, "y_" + name)
        g[...] = dot_tn(lhs, rhs).astype(BHALF).reshape(g.shape)
        return name, send(g.at[:, 1 - y], got, y_peer)

    def grad_along(job):
        name, copy = job
        g, got, last = [getattr(k, kind + name) for kind in ("g_", "y_", "z_")]
        copy.wait_recv()
        g[:, y] = (g[:, y].astype(FLOAT) + got[...].astype(FLOAT)).astype(BHALF)
        last[z] = g[z, y]
        return name, [send(g.at[p, y], last.at[z], (p * 2 + y, h)) for p in z_peers]

    def grad_close(job):
        name, copies = job
        last, out = getattr(k, "z_" + name), getattr(k, "o_" + name)
        arrived(copies)
        out[...] = sum(last[i].astype(FLOAT) for i in range(zs))

    def vectors_send(which, values):
        value = eight(values)
        k.v_send[which] = value
        k.v_recv[which, s] = value
        return [send(k.v_send.at[which], k.v_recv.at[which, s], (p, h)) for p in peers]

    def vectors_close(which, copies):
        arrived(copies)
        value = k.v_recv[which, 0]
        for i in range(1, seq):
            value = value + k.v_recv[which, i]
        return value

    ones = jnp.ones((8, rows), BHALF)
    at = iota((8, rows), 1)
    ones_kept = jnp.where((at >= patches) & (at < ROWS), first_seq, 1.0).astype(BHALF)

    def col_sums(ref, weights=None):
        out = dot_nn(ones if weights is None else weights, ref[...])[0:1]
        if out.shape[1] < model:
            out = jnp.concatenate([out, jnp.zeros((1, model - out.shape[1]), FLOAT)], axis=-1)
        return out

    def norm_back(i, which, gain, xhat, keep, use):
        def body(r, sums):
            g = sum_rows(i, r)
            n = xhat[r, :]
            gh = g * gain
            m1 = jnp.mean(gh, axis=-1, keepdims=True)
            m2 = jnp.mean(gh * n, axis=-1, keepdims=True)
            use(r, k.inv[which, r, 0:1] * (gh - m1 - n * m2))
            w = g * kept(r) if keep else g
            fold = lambda v: jnp.sum(v.reshape(BLOCK // 8, 8, model), axis=0)
            return sums[0] + fold(w * n), sums[1] + fold(w)

        zero = jnp.zeros((8, model), FLOAT)
        sums = (zero, zero)
        if dims["unroll"]:
            for b in range(rows // BLOCK):
                sums = body(pl.ds(b * BLOCK, BLOCK), sums)
        else:
            sums = lax.fori_loop(
                0, rows // BLOCK, lambda b, v: body(pl.ds(pl.multiple_of(b * BLOCK, BLOCK), BLOCK), v), sums
            )
        return [jnp.sum(v, axis=0, keepdims=True) for v in sums]

    m_sum = sum_open(0, k.gpre, k.w_up, dot_nt)
    j_dn = grad_open("dn", k.gr16[...], k.act_k[...])
    m_sum = sum_across(0, m_sum)
    j_up = grad_open("up", k.n_m[...], k.gpre_k[...])
    o_sum = sum_open(1, k.act, k.w_dn, dot_nn)
    j_dn = grad_along(j_dn)
    o_sum = sum_across(1, o_sum)
    ub_grad, db_grad = col_sums(k.gpre_k), col_sums(k.gr16, ones_kept)
    j_up = grad_along(j_up)
    last = sum_close(0, m_sum)
    last.wait_recv()

    def use_m(r, dx):
        k.gr32[r, :] = k.gr32[r, :] + dx

    sums = norm_back(0, 2, m_gain, k.xh_m, True, use_m)
    v_m = vectors_send(0, [sums[0], sums[1], ub_grad, db_grad])
    grad_cls_mid = k.gr32[patches : patches + clips, :]
    k.gcm[...] = eight([grad_cls_mid])
    for f in range(frames):
        shared = sum(onehot[f][i] * (grad_cls_mid[i : i + 1] * per_len[i]) for i in range(clips))
        set_tail(k.gr32, f, [shared])
    cast_rows(k.gr32, k.gss)
    for f in range(frames):
        set_tail(k.gr32, f, [])

    k.gatt[...] = dot_nt(k.gss[...], k.w_so[0, c]).astype(BHALF)
    for f in range(frames):
        r = slice(f * ROWS, (f + 1) * ROWS)
        qkv, grad = k.sqkv[r, :], k.gatt[r, :]
        out = [
            attend_back(*[head_of(qkv, i, j) for i in range(3)], head_of(grad, 0, j), k.p_s.at[f * heads + j])
            for j in range(heads)
        ]
        k.dsq[r, :] = jnp.concatenate([out[j][i] for i in range(3) for j in range(heads)], axis=-1)
    s_sum = sum_open(2, k.dsq, k.w_si, dot_nt)
    j_si = grad_open("si", k.n_s[...], k.dsq[...])
    s_sum = sum_across(2, s_sum)
    last = sum_close(1, o_sum)
    j_so = grad_open("so", k.gss[...], k.att_s[0, c])
    j_si = grad_along(j_si)
    last.wait_recv()

    def out_rows(r):
        k.t32[r, :] = k.x32[r, :] + sum_rows(1, r) + m_db

    blocks(out_rows)
    for f in range(frames):
        k.o_blk[f] = k.t32[f * ROWS : f * ROWS + patches, :].astype(BHALF)
    k.o_cls[...] = k.t32[patches : patches + clips, :].astype(BHALF)
    s_rows = [col_sums(k.gss), col_sums(k.dsq)]
    j_so = grad_along(j_so)
    last = sum_close(2, s_sum)
    last.wait_recv()
    sums = norm_back(2, 1, s_gain, k.xh_s, False, use_m)
    cls_in = [k.gr32[f * ROWS + patches : f * ROWS + patches + 1, :] for f in range(frames)]
    cls_parts = [sum(onehot[f][i] * cls_in[f] for f in range(frames)) for i in range(clips)]
    for f in range(frames):
        set_tail(k.gr32, f, [])
    v_s = vectors_send(1, [sums[0], sums[1]] + s_rows + cls_parts)
    cast_rows(k.gr32, k.gtr)

    k.gtm[...] = dot_nt(k.gtr[...], k.w_tl[...]).astype(BHALF)
    k.gatt[...] = dot_nt(k.gtm[...], k.w_to[0, c]).astype(BHALF)
    for f in range(frames):
        to_slots(f, k.gatt[f * ROWS : (f + 1) * ROWS, :], k.g_send)
    g_copies = scatter(k.g_send, k.g_pos)
    pick = (iota((model, width), 0) == h * width + iota((model, width), 1)).astype(FLOAT).astype(BHALF)
    j_tl = grad_open("tl", k.mid16[...], dot_nn(k.gtr[...], pick).astype(BHALF))
    j_to = grad_open("to", k.gtm[...], k.att_t[0, c])
    t_rows = [col_sums(k.gtm), col_sums(k.gtr)]
    arrived(g_copies)
    for b in range(2):
        qkv, grad = k.q_pos[b].reshape(span, 3 * width), k.g_pos[b].reshape(span, width)
        out = [
            attend_back(*[head_of(qkv, i, j) for i in range(3)], head_of(grad, 0, j), k.p_t.at[b * heads + j])
            for j in range(heads)
        ]
        value = jnp.concatenate([out[j][i] for i in range(3) for j in range(heads)], axis=-1)
        k.d_pos[b] = value.reshape(every, HALF, 3 * width)
    d_copies = gather(k.d_pos, k.d_recv)
    j_tl = grad_along(j_tl)
    j_to = grad_along(j_to)
    grad_close(j_dn)
    grad_close(j_up)
    m_vec = vectors_close(0, v_m)
    s_vec = vectors_close(1, v_s)
    arrived(d_copies)
    for f in range(frames):
        k.dtq[f * ROWS : (f + 1) * ROWS, :] = from_slots(f, k.d_recv).astype(BHALF)
    t_sum = sum_open(3, k.dtq, k.w_ti, dot_nt)
    j_ti = grad_open("ti", k.n_t[...], k.dtq[...])
    t_sum = sum_across(3, t_sum)
    pair_row = col_sums(k.dtq)
    grad_close(j_si)
    grad_close(j_so)
    j_ti = grad_along(j_ti)
    grad_close(j_tl)
    grad_close(j_to)
    last = sum_close(3, t_sum)
    last.wait_recv()

    def use_t(r, dx):
        k.t32[r, :] = k.gr32[r, :] + dx.astype(BHALF).astype(FLOAT)

    sums = norm_back(3, 0, t_gain, k.xh_t, False, use_t)
    v_t = vectors_send(2, [sums[0], sums[1], t_rows[0], pair_row, t_rows[1]])
    for f in range(frames):
        k.o_tok[f] = k.t32[f * ROWS : f * ROWS + patches, :].astype(BHALF)
    k.o_vec[0:8, :] = m_vec
    k.o_vec[8:16, :] = s_vec + jnp.concatenate([jnp.zeros((4, model), FLOAT), k.gcm[0:4, :]], axis=0)
    k.o_vec[16:24, :] = vectors_close(2, v_t)
    grad_close(j_ti)
    for copy in unsent:
        copy.wait_send()


def finish_kernel(dims, vec, g_dn, g_up, g_si, g_so, g_tl, g_to, g_ti, *outs):
    width, model, seq = dims["width"], dims["model"], dims["seq"]
    share, clips = model // seq, dims["clips"]
    cls, tg, tb, ti, tp, to, tob, tl, tlb, sg, sb, si, sp, so, sob, mg, mb, up, ub, dn, db = outs
    s = lax.axis_index("seq")
    v = vec[...]
    mine = pltpu.roll(v, (model - share * s) % model, 1)[:, :share]
    mg[...], mb[...], ub[...], db[...] = mine[0:1], v[1:2], v[2:3], v[3:4]
    sg[...], sb[...], sob[...] = mine[8:9], v[9:10], v[10:11]
    tg[...], tb[...], tob[...], tlb[...] = mine[16:17], v[17:18], v[18:19], v[20:21]
    cls[...] = mine[12 : 12 + clips]
    for out, row in ((sp, 11), (tp, 19)):
        out[0:1, :] = v[row : row + 1, :width]
        out[1:2, :] = v[row : row + 1, 2 * width : 3 * width]
    for out, g in ((si, g_si), (ti, g_ti)):
        for i in range(3):
            out[:, i, :] = g[:, i * width : (i + 1) * width]
    tl[...] = g_tl[...]
    up[...] = g_up[...]
    to[...] = g_to[...].T
    so[...] = g_so[...].T
    dn[...] = g_dn[...].T


def fused_body(
    tokens,
    cls_tokens,
    clip_lengths,
    time_gain,
    time_beta,
    time_proj_in,
    time_qv_bias,
    time_proj_out,
    time_out_bias,
    time_linear,
    time_linear_bias,
    space_gain,
    space_beta,
    space_proj_in,
    space_qv_bias,
    space_proj_out,
    space_out_bias,
    mlp_gain,
    mlp_beta,
    mlp_up,
    mlp_up_bias,
    mlp_down,
    mlp_down_bias,
    out_grad,
    cls_grad,
):
    frames, patches, model = tokens.shape
    seq = lax.axis_size("seq")
    width, hidden, clips = time_proj_in.shape[2], mlp_up.shape[1], clip_lengths.shape[0]
    dims = dict(
        frames=frames,
        patches=patches,
        model=model,
        seq=seq,
        width=width,
        hidden=hidden,
        clips=clips,
        pos=-(-patches // seq),
        unroll=False,
    )

    def wide(v):
        return jnp.pad(v, (0, model - v.shape[0]))

    vec = jnp.stack(
        [
            time_gain,
            time_beta,
            time_out_bias,
            time_linear_bias,
            space_gain,
            space_beta,
            space_out_bias,
            mlp_gain,
            mlp_beta,
            mlp_down_bias,
            mlp_up_bias,
            wide(qkv_shift(time_qv_bias)),
            wide(qkv_shift(space_qv_bias)),
        ]
    )
    scratch = scratch_shapes(dims)
    grads = grad_columns(dims)
    share = model // seq
    shape = jax.ShapeDtypeStruct
    vmem, anywhere = pl.BlockSpec(memory_space=pltpu.VMEM), pl.BlockSpec(memory_space=pl.ANY)
    outs = [
        shape(tokens.shape, BHALF),
        shape(cls_tokens.shape, BHALF),
        shape(tokens.shape, BHALF),
        shape((24, model), FLOAT),
    ] + [shape((share, columns), FLOAT) for _, columns in grads]
    names = list(INPUTS) + list(OUTPUTS) + ["o_" + name for name, _ in grads] + list(scratch)
    results = pl.pallas_call(
        functools.partial(layer_kernel, dims, names),
        out_shape=outs,
        in_specs=[pl.BlockSpec(memory_space=pltpu.SMEM)] + [vmem] * 3 + [anywhere] * 9,
        out_specs=[vmem] * len(outs),
        scratch_shapes=list(scratch.values()),
        compiler_params=pltpu.CompilerParams(
            collective_id=0, has_side_effects=True, vmem_limit_bytes=62 * 1024 * 1024
        ),
        name="layer",
    )(
        clip_lengths,
        cls_tokens,
        cls_grad,
        vec,
        tokens,
        out_grad,
        time_proj_in.reshape(model, 3 * width),
        time_proj_out,
        time_linear,
        space_proj_in.reshape(model, 3 * width),
        space_proj_out,
        mlp_up,
        mlp_down,
    )
    block_out, cls_out, tokens_grad = results[:3]
    row, gain = shape((1, model), FLOAT), shape((1, share), FLOAT)
    proj, pair = shape((share, 3, width), FLOAT), shape((2, width), FLOAT)
    out_shape = [
        shape((clips, share), FLOAT),
        gain,
        row,
        proj,
        pair,
        shape((width, share), FLOAT),
        row,
        shape((share, width), FLOAT),
        row,
        gain,
        row,
        proj,
        pair,
        shape((width, share), FLOAT),
        row,
        gain,
        row,
        shape((share, hidden), FLOAT),
        shape((1, hidden), FLOAT),
        shape((hidden, share), FLOAT),
        row,
    ]
    last = pl.pallas_call(
        functools.partial(finish_kernel, dims),
        out_shape=out_shape,
        in_specs=[vmem] * 8,
        out_specs=[vmem] * len(out_shape),
        compiler_params=pltpu.CompilerParams(vmem_limit_bytes=32 * 1024 * 1024),
        name="finish",
    )(*results[3:])
    last = [v.reshape(-1) if v.shape[0] == 1 else v for v in last]
    return (block_out, cls_out, tokens_grad, *last)


def solution(mesh):
    placed = (
        P("seq", None, None),
        P(),
        P(),
        P(),
        P(),
        P(None, None, "head"),
        P(None, "head"),
        P("head", None),
        P(),
        P(),
        P(),
        P(),
        P(),
        P(None, None, "head"),
        P(None, "head"),
        P("head", None),
        P(),
        P(),
        P(),
        P(None, "head"),
        P("head"),
        P("head", None),
        P(),
        P("seq", None, None),
        P(),
    )
    fused = mesh.shape["seq"] == 8 and mesh.shape["head"] == 4
    return jax.shard_map(
        fused_body if fused else body,
        mesh=mesh,
        in_specs=placed,
        out_specs=(
            P("seq", None, None),
            P(),
            P("seq", None, None),
            P(None, "seq"),
            P("seq"),
            P(),
            P("seq", None, "head"),
            P(None, "head"),
            P("head", "seq"),
            P(),
            P("seq", "head"),
            P(),
            P("seq"),
            P(),
            P("seq", None, "head"),
            P(None, "head"),
            P("head", "seq"),
            P(),
            P("seq"),
            P(),
            P("seq", "head"),
            P("head"),
            P("head", "seq"),
            P(),
        ),
        check_vma=False,
    )
```

```python
import functools

import jax
import jax.numpy as jnp
from jax import lax
from jax.experimental import pallas as pl
from jax.experimental.pallas import tpu as pltpu
from jax.sharding import PartitionSpec as P

HEAD_DIM = 64
PATCH = 196
MAXLEN = 8


EPS = 1e-06
NEG = -1e30
FLOAT = jnp.float32
BHALF = jnp.bfloat16


def matmul_plain(left, right):
    return jnp.dot(left, right, preferred_element_type=FLOAT)


def matmul_tn(left, right):
    return lax.dot_general(left, right, (((0,), (0,)), ((), ())), preferred_element_type=FLOAT)


def matmul_nt(left, right):
    return lax.dot_general(left, right, (((1,), (1,)), ((), ())), preferred_element_type=FLOAT)


def exact_tn(left, right):
    return lax.dot_general(
        left,
        right,
        (((0,), (0,)), ((), ())),
        precision=lax.Precision.HIGHEST,
        preferred_element_type=FLOAT,
    )


def exact_nn(left, right):
    return jnp.dot(left, right, precision=lax.Precision.HIGHEST, preferred_element_type=FLOAT)


def layer_norm(rows, gain, shift):
    center = rows - jnp.mean(rows, axis=-1, keepdims=True)
    invstd = lax.rsqrt(jnp.mean(center * center, axis=-1, keepdims=True) + EPS)
    normed = center * invstd
    return (normed * gain + shift, normed, invstd)


def norm_back(grad_out, gain, normed, invstd, row_weight):
    feature_count = grad_out.shape[-1]
    grad_norm = grad_out * gain
    weighted = grad_out * row_weight
    gain_grad = jnp.sum((weighted * normed).reshape(-1, feature_count), axis=0)
    shift_grad = jnp.sum(weighted.reshape(-1, feature_count), axis=0)
    first_mean = jnp.mean(grad_norm, axis=-1, keepdims=True)
    second_mean = jnp.mean(grad_norm * normed, axis=-1, keepdims=True)
    return (invstd * (grad_norm - first_mean - normed * second_mean), gain_grad, shift_grad)


def qkv_shift(pair):
    return jnp.stack([pair[0], jnp.zeros_like(pair[0]), pair[1]], axis=0).reshape(-1)


def pair_sums(grad_qkv, local_width):
    sums = jnp.sum(grad_qkv.astype(FLOAT).reshape(-1, 3, local_width), axis=0)
    return jnp.stack([sums[0], sums[2]], axis=0)


def gelu_slope(pre):
    normal_cdf = 0.5 * (1.0 + jax.scipy.special.erf(pre * 0.7071067811865476))
    return normal_cdf + pre * jnp.exp(-0.5 * pre * pre) * 0.3989422804014327


def band_stack(values, band_reach):
    frames = values.shape[0]
    padded = jnp.pad(values, ((band_reach, band_reach),) + ((0, 0),) * (values.ndim - 1))
    return jnp.stack(
        [padded[offset : offset + frames] for offset in range(2 * band_reach + 1)], axis=2
    )


def band_return(contrib, band_reach):
    frames = contrib.shape[0]
    padded = jnp.pad(contrib, ((band_reach, band_reach),) + ((0, 0),) * (contrib.ndim - 1))
    total = jnp.zeros((frames,) + contrib.shape[1:2] + contrib.shape[3:], FLOAT)
    for offset in range(2 * band_reach + 1):
        start = 2 * band_reach - offset
        total = total + padded[start : start + frames, :, offset]
    return total


def to_positions(frame_major):
    frames_dev, patches, columns = frame_major.shape
    seq_count = lax.axis_size("seq")
    pos_dev = (patches + seq_count - 1) // seq_count
    padded = jnp.pad(frame_major, ((0, 0), (0, pos_dev * seq_count - patches), (0, 0)))
    moved = lax.all_to_all(
        padded.reshape(frames_dev, seq_count, pos_dev, columns),
        "seq",
        split_axis=1,
        concat_axis=0,
        tiled=True,
    )
    return moved.reshape(frames_dev * seq_count, pos_dev, columns)


def to_frames(pos_major):
    frames_all, pos_dev, columns = pos_major.shape
    seq_count = lax.axis_size("seq")
    moved = lax.all_to_all(
        pos_major.reshape(frames_all, 1, pos_dev, columns),
        "seq",
        split_axis=0,
        concat_axis=1,
        tiled=True,
    )
    return moved.reshape(frames_all // seq_count, seq_count * pos_dev, columns)[:, :PATCH]


def head_cols(pieces):
    return lax.all_gather(pieces, "head", axis=2, tiled=True)


def time_scores(queries, key_band, valid, score_scale):
    raw = (
        jnp.einsum("fphd,fpohd->fpho", queries, key_band, preferred_element_type=FLOAT)
        * score_scale
    )
    return jnp.where(valid[:, None, None, :], raw, NEG)


def time_forward(queries, key_band, value_band, valid, score_scale):
    scores = time_scores(queries, key_band, valid, score_scale)
    largest = jnp.max(scores, axis=-1, keepdims=True)
    exponent = jnp.exp(scores - largest)
    totals = jnp.sum(exponent, axis=-1, keepdims=True)
    attend = (exponent / totals).astype(BHALF)
    result = jnp.einsum("fpho,fpohd->fphd", attend, value_band, preferred_element_type=FLOAT)
    return (result, largest + jnp.log(totals))


def time_backward(
    queries, key_band, value_band, valid, log_total, grad_out, score_scale, band_reach
):
    scores = time_scores(queries, key_band, valid, score_scale)
    attend = jnp.exp(scores - log_total)
    grad_attend = jnp.einsum("fphd,fpohd->fpho", grad_out, value_band, preferred_element_type=FLOAT)
    row_dot = jnp.sum(attend * grad_attend, axis=-1, keepdims=True)
    grad_score = (attend * (grad_attend - row_dot)).astype(BHALF)
    grad_query = (
        jnp.einsum("fpho,fpohd->fphd", grad_score, key_band, preferred_element_type=FLOAT)
        * score_scale
    )
    key_part = (
        jnp.einsum("fpho,fphd->fpohd", grad_score, queries, preferred_element_type=FLOAT)
        * score_scale
    )
    value_part = jnp.einsum(
        "fpho,fphd->fpohd", attend.astype(BHALF), grad_out, preferred_element_type=FLOAT
    )
    return (grad_query, band_return(key_part, band_reach), band_return(value_part, band_reach))


def space_forward(queries, key_rows, value_rows, score_scale):
    scores = (
        jnp.einsum("fqhd,fkhd->fhqk", queries, key_rows, preferred_element_type=FLOAT) * score_scale
    )
    largest = jnp.max(scores, axis=-1, keepdims=True)
    exponent = jnp.exp(scores - largest)
    totals = jnp.sum(exponent, axis=-1, keepdims=True)
    attend = (exponent / totals).astype(BHALF)
    result = jnp.einsum("fhqk,fkhd->fqhd", attend, value_rows, preferred_element_type=FLOAT)
    return (result, largest + jnp.log(totals))


def space_backward(queries, key_rows, value_rows, log_total, grad_out, score_scale):
    scores = (
        jnp.einsum("fqhd,fkhd->fhqk", queries, key_rows, preferred_element_type=FLOAT) * score_scale
    )
    attend = jnp.exp(scores - log_total)
    grad_attend = jnp.einsum("fqhd,fkhd->fhqk", grad_out, value_rows, preferred_element_type=FLOAT)
    row_dot = jnp.sum(attend * grad_attend, axis=-1, keepdims=True)
    grad_score = (attend * (grad_attend - row_dot)).astype(BHALF)
    grad_query = (
        jnp.einsum("fhqk,fkhd->fqhd", grad_score, key_rows, preferred_element_type=FLOAT)
        * score_scale
    )
    grad_key = (
        jnp.einsum("fhqk,fqhd->fkhd", grad_score, queries, preferred_element_type=FLOAT)
        * score_scale
    )
    grad_value = jnp.einsum(
        "fhqk,fqhd->fkhd", attend.astype(BHALF), grad_out, preferred_element_type=FLOAT
    )
    return (grad_query, grad_key, grad_value)


def body(
    tokens,
    cls_tokens,
    clip_lengths,
    time_gain,
    time_beta,
    time_proj_in,
    time_qv_bias,
    time_proj_out,
    time_out_bias,
    time_linear,
    time_linear_bias,
    space_gain,
    space_beta,
    space_proj_in,
    space_qv_bias,
    space_proj_out,
    space_out_bias,
    mlp_gain,
    mlp_beta,
    mlp_up,
    mlp_up_bias,
    mlp_down,
    mlp_down_bias,
    out_grad,
    cls_grad,
):
    frames_dev, patches, model_width = tokens.shape
    seq_count = lax.axis_size("seq")
    frames_all = frames_dev * seq_count
    clip_count = clip_lengths.shape[0]
    local_width = time_proj_in.shape[2]
    local_heads = local_width // HEAD_DIM
    band_reach = MAXLEN - 1
    score_scale = HEAD_DIM ** (-0.5)
    seq_rank = lax.axis_index("seq")
    head_rank = lax.axis_index("head")
    clip_ends = jnp.sum(
        jnp.where(jnp.tri(clip_lengths.shape[0], dtype=bool), clip_lengths[None, :], 0), axis=1
    )
    frame_ids = jnp.arange(frames_all, dtype=jnp.int32)
    clip_of = jnp.sum((frame_ids[:, None] >= clip_ends[None, :]).astype(jnp.int32), axis=1)
    clip_pad = jnp.pad(clip_of, (band_reach, band_reach), constant_values=-1)
    valid = jnp.stack(
        [clip_pad[offset : offset + frames_all] == clip_of for offset in range(2 * band_reach + 1)],
        axis=1,
    )
    local_clip = lax.dynamic_slice_in_dim(clip_of, seq_rank * frames_dev, frames_dev)
    onehot = (local_clip[:, None] == jnp.arange(clip_count, dtype=jnp.int32)[None, :]).astype(FLOAT)
    lengths = clip_lengths.astype(FLOAT)
    time_in = to_positions(tokens)
    pos_dev = time_in.shape[1]
    time_rows = frames_all * pos_dev
    time_normed, time_stat, time_inv = layer_norm(time_in.astype(FLOAT), time_gain, time_beta)
    time_normed = time_normed.astype(BHALF).reshape(time_rows, model_width)
    time_in_mat = time_proj_in.reshape(model_width, 3 * local_width)
    time_qkv = (
        (matmul_plain(time_normed, time_in_mat) + qkv_shift(time_qv_bias))
        .astype(BHALF)
        .reshape(frames_all, pos_dev, 3, local_heads, HEAD_DIM)
    )
    time_query = time_qkv[:, :, 0]
    time_keys = band_stack(time_qkv[:, :, 1], band_reach)
    time_values = band_stack(time_qkv[:, :, 2], band_reach)
    time_att, time_log = time_forward(time_query, time_keys, time_values, valid, score_scale)
    time_att = time_att.astype(BHALF).reshape(time_rows, local_width)
    time_mid = (
        lax.psum(matmul_plain(time_att, time_proj_out).astype(jnp.bfloat16), "head").astype(
            jnp.float32
        )
        + time_out_bias
    ).astype(BHALF)
    col_start = head_rank * local_width
    linear_cols = lax.dynamic_slice_in_dim(time_linear, col_start, local_width, 1)
    linear_shift = lax.dynamic_slice_in_dim(time_linear_bias, col_start, local_width)
    time_part = (
        (matmul_plain(time_mid, linear_cols) + linear_shift)
        .astype(BHALF)
        .reshape(frames_all, pos_dev, local_width)
    )
    time_res = to_frames(head_cols(time_part))
    mid = tokens.astype(FLOAT) + time_res.astype(FLOAT)
    span_rows = patches + 1
    space_rows = frames_dev * span_rows
    cls_rows = matmul_plain(onehot.astype(BHALF), cls_tokens)
    space_in = jnp.concatenate([cls_rows[:, None, :], mid], axis=1)
    space_normed, space_stat, space_inv = layer_norm(space_in, space_gain, space_beta)
    space_normed = space_normed.astype(BHALF).reshape(space_rows, model_width)
    space_in_mat = space_proj_in.reshape(model_width, 3 * local_width)
    space_qkv = (
        (matmul_plain(space_normed, space_in_mat) + qkv_shift(space_qv_bias))
        .astype(BHALF)
        .reshape(frames_dev, span_rows, 3, local_heads, HEAD_DIM)
    )
    space_query = space_qkv[:, :, 0]
    space_keys = space_qkv[:, :, 1]
    space_values = space_qkv[:, :, 2]
    space_att, space_log = space_forward(space_query, space_keys, space_values, score_scale)
    space_att = space_att.astype(BHALF).reshape(space_rows, local_width)
    space_sum = (
        lax.psum(matmul_plain(space_att, space_proj_out).astype(jnp.bfloat16), "head").astype(
            jnp.float32
        )
        + space_out_bias
    ).reshape(frames_dev, span_rows, model_width)
    after = mid + space_sum[:, 1:]
    cls_part = exact_tn(onehot, space_sum[:, 0])
    cls_mid = cls_tokens.astype(FLOAT) + lax.psum(cls_part, "seq") / lengths[:, None]
    tok_rows = frames_dev * patches
    rows = jnp.concatenate([after.reshape(tok_rows, model_width), cls_mid], axis=0)
    mlp_normed, mlp_stat, mlp_inv = layer_norm(rows, mlp_gain, mlp_beta)
    mlp_normed = mlp_normed.astype(BHALF)
    pre = matmul_plain(mlp_normed, mlp_up) + mlp_up_bias
    act = jax.nn.gelu(pre, approximate=False).astype(BHALF)
    result = (
        rows
        + lax.psum(matmul_plain(act, mlp_down).astype(jnp.bfloat16), "head").astype(jnp.float32)
        + mlp_down_bias
    )
    block_out = result[:tok_rows].reshape(frames_dev, patches, model_width).astype(BHALF)
    cls_out = result[tok_rows:].astype(BHALF)
    first_seq = (seq_rank == 0).astype(FLOAT)
    keep_rows = jnp.concatenate(
        [jnp.ones((tok_rows, 1), FLOAT), jnp.ones((clip_count, 1), FLOAT) * first_seq], axis=0
    )
    keep_half = keep_rows.astype(BHALF)
    grad_rows = jnp.concatenate([out_grad.reshape(tok_rows, model_width), cls_grad], axis=0)
    down_grad = matmul_tn(act * keep_half, grad_rows)
    down_shift_grad = jnp.sum(grad_rows.astype(FLOAT) * keep_rows, axis=0)
    grad_pre = (matmul_nt(grad_rows, mlp_down) * gelu_slope(pre)).astype(BHALF)
    up_grad = matmul_tn(mlp_normed * keep_half, grad_pre)
    up_shift_grad = jnp.sum(grad_pre.astype(FLOAT) * keep_rows, axis=0)
    grad_mlp_norm = lax.psum(matmul_nt(grad_pre, mlp_up).astype(jnp.bfloat16), "head").astype(
        jnp.float32
    )
    grad_mlp_in, mlp_gain_grad, mlp_beta_grad = norm_back(
        grad_mlp_norm, mlp_gain, mlp_stat, mlp_inv, keep_rows
    )
    grad_total = grad_rows.astype(FLOAT) + grad_mlp_in
    grad_after = grad_total[:tok_rows].reshape(frames_dev, patches, model_width)
    grad_cls_mid = grad_total[tok_rows:]
    cls_share = exact_nn(onehot, grad_cls_mid / lengths[:, None])
    grad_space_sum = (
        jnp.concatenate([cls_share[:, None, :], grad_after], axis=1)
        .astype(BHALF)
        .reshape(space_rows, model_width)
    )
    space_out_grad = matmul_tn(space_att, grad_space_sum)
    space_shift_grad = jnp.sum(grad_space_sum.astype(FLOAT), axis=0)
    grad_space_att = (
        matmul_nt(grad_space_sum, space_proj_out)
        .astype(BHALF)
        .reshape(frames_dev, span_rows, local_heads, HEAD_DIM)
    )
    space_grad_query, space_grad_key, space_grad_value = space_backward(
        space_query, space_keys, space_values, space_log, grad_space_att, score_scale
    )
    grad_space_qkv = (
        jnp.stack([space_grad_query, space_grad_key, space_grad_value], axis=2)
        .astype(BHALF)
        .reshape(space_rows, 3 * local_width)
    )
    space_in_grad = matmul_tn(space_normed, grad_space_qkv).reshape(model_width, 3, local_width)
    space_pair_grad = pair_sums(grad_space_qkv, local_width)
    grad_space_norm = (
        lax.psum(matmul_nt(grad_space_qkv, space_in_mat).astype(jnp.bfloat16), "head")
        .astype(jnp.float32)
        .reshape(frames_dev, span_rows, model_width)
    )
    grad_space_in, space_gain_grad, space_beta_grad = norm_back(
        grad_space_norm, space_gain, space_stat, space_inv, 1.0
    )
    grad_mid = grad_after + grad_space_in[:, 1:]
    cls_in_part = exact_tn(onehot, grad_space_in[:, 0])
    grad_time_res = to_positions(grad_mid.astype(BHALF)).reshape(time_rows, model_width)
    linear_grad = matmul_tn(
        time_mid, lax.dynamic_slice_in_dim(grad_time_res, col_start, local_width, 1)
    )
    linear_shift_grad = jnp.sum(grad_time_res.astype(FLOAT), axis=0)
    grad_time_mid = matmul_nt(grad_time_res, time_linear).astype(BHALF)
    time_out_grad = matmul_tn(time_att, grad_time_mid)
    time_shift_grad = jnp.sum(grad_time_mid.astype(FLOAT), axis=0)
    grad_time_att = (
        matmul_nt(grad_time_mid, time_proj_out)
        .astype(BHALF)
        .reshape(frames_all, pos_dev, local_heads, HEAD_DIM)
    )
    time_grad_query, time_grad_key, time_grad_value = time_backward(
        time_query, time_keys, time_values, valid, time_log, grad_time_att, score_scale, band_reach
    )
    grad_time_qkv = (
        jnp.stack([time_grad_query, time_grad_key, time_grad_value], axis=2)
        .astype(BHALF)
        .reshape(time_rows, 3 * local_width)
    )
    time_in_grad = matmul_tn(time_normed, grad_time_qkv).reshape(model_width, 3, local_width)
    time_pair_grad = pair_sums(grad_time_qkv, local_width)
    grad_time_norm = (
        lax.psum(matmul_nt(grad_time_qkv, time_in_mat).astype(jnp.bfloat16), "head")
        .astype(jnp.float32)
        .reshape(frames_all, pos_dev, model_width)
    )
    grad_time_in, time_gain_grad, time_beta_grad = norm_back(
        grad_time_norm, time_gain, time_stat, time_inv, 1.0
    )
    grad_tokens_time = to_frames(grad_time_in.astype(BHALF))
    tokens_grad = (grad_mid + grad_tokens_time.astype(FLOAT)).astype(BHALF)
    summed = (
        lax.psum_scatter(time_gain_grad, "seq", scatter_dimension=0, tiled=True),
        lax.psum_scatter(time_in_grad, "seq", scatter_dimension=0, tiled=True),
        lax.psum_scatter(time_out_grad, "seq", scatter_dimension=1, tiled=True),
        lax.psum_scatter(linear_grad, "seq", scatter_dimension=0, tiled=True),
        lax.psum_scatter(space_gain_grad, "seq", scatter_dimension=0, tiled=True),
        lax.psum_scatter(space_in_grad, "seq", scatter_dimension=0, tiled=True),
        lax.psum_scatter(space_out_grad, "seq", scatter_dimension=1, tiled=True),
        lax.psum_scatter(mlp_gain_grad, "seq", scatter_dimension=0, tiled=True),
        lax.psum_scatter(up_grad, "seq", scatter_dimension=0, tiled=True),
        lax.psum_scatter(down_grad, "seq", scatter_dimension=1, tiled=True),
        lax.psum_scatter(cls_in_part, "seq", scatter_dimension=1, tiled=True),
    )
    shifts = lax.psum(
        (
            time_beta_grad,
            time_pair_grad,
            time_shift_grad,
            linear_shift_grad,
            space_beta_grad,
            space_pair_grad,
            space_shift_grad,
            mlp_beta_grad,
            up_shift_grad,
            down_shift_grad,
        ),
        "seq",
    )
    col_width = model_width // seq_count
    cls_direct = lax.dynamic_slice_in_dim(grad_cls_mid, seq_rank * col_width, col_width, 1)
    cls_tokens_grad = summed[10] + cls_direct
    return (
        block_out,
        cls_out,
        tokens_grad,
        cls_tokens_grad,
        summed[0],
        shifts[0],
        summed[1],
        shifts[1],
        summed[2],
        shifts[2],
        summed[3],
        shifts[3],
        summed[4],
        shifts[4],
        summed[5],
        shifts[5],
        summed[6],
        shifts[6],
        summed[7],
        shifts[7],
        summed[8],
        shifts[8],
        summed[9],
        shifts[9],
    )


MESH = pl.DeviceIdType.MESH
ROWS = 208
HALF = 16
SLOTS = 2 * HALF
BLOCK = 32


def dot_nn(left, right):
    return jnp.dot(left, right, preferred_element_type=FLOAT)


def dot_nt(left, right):
    return lax.dot_general(left, right, (((1,), (1,)), ((), ())), preferred_element_type=FLOAT)


def dot_tn(left, right):
    return lax.dot_general(left, right, (((0,), (0,)), ((), ())), preferred_element_type=FLOAT)


def iota(shape, axis):
    return lax.broadcasted_iota(jnp.int32, shape, axis)


def scratch_shapes(dims):
    frames, seq, width, model, hidden = dims["frames"], dims["seq"], dims["width"], dims["model"], dims["hidden"]
    rows, every, heads = frames * ROWS, frames * seq, width // HEAD_DIM
    half, low = model // 2, BHALF
    vm = pltpu.VMEM
    shapes = dict(
        tok=vm((dims["patches"], frames, model), low),
        out_grad=vm((dims["patches"], frames, model), low),
        w_ti=vm((3 * width, model), low),
        w_si=vm((3 * width, model), low),
        w_tl=vm((model, model), low),
        w_up=vm((model, hidden), low),
        w_dn=vm((hidden, model), low),
        w_to=vm((2, 2, width, model), low),
        w_so=vm((2, 2, width, model), low),
        x32=vm((rows, model), FLOAT),
        gr32=vm((rows, model), FLOAT),
        t32=vm((rows, model), FLOAT),
        u32=vm((rows, model), FLOAT),
        dact=vm((rows, hidden), FLOAT),
        xh_t=vm((rows, model), FLOAT),
        xh_s=vm((rows, model), FLOAT),
        xh_m=vm((rows, model), FLOAT),
        inv=vm((3, rows, 128), FLOAT),
        n_t=vm((rows, model), low),
        n_s=vm((rows, model), low),
        n_m=vm((rows, model), low),
        gr16=vm((rows, model), low),
        mid16=vm((rows, model), low),
        act=vm((rows, hidden), low),
        act_k=vm((rows, hidden), low),
        gpre=vm((rows, hidden), low),
        gpre_k=vm((rows, hidden), low),
        gss=vm((rows, model), low),
        gtr=vm((rows, model), low),
        gtm=vm((rows, model), low),
        sqkv=vm((rows, 3 * width), low),
        dsq=vm((rows, 3 * width), low),
        dtq=vm((rows, 3 * width), low),
        gatt=vm((rows, width), low),
        sel=vm((seq * SLOTS, ROWS), low),
        les=vm((ROWS, seq * SLOTS), low),
        tmask=vm((every * HALF, every * HALF), FLOAT),
        p_t=vm((2 * heads, every * HALF, every * HALF), FLOAT),
        p_s=vm((frames * heads, ROWS, ROWS), FLOAT),
        q_send=vm((frames, seq, 2, HALF, 3 * width), low),
        q_pos=vm((2, every, HALF, 3 * width), low),
        a_pos=vm((2, every, HALF, width), low),
        a_recv=vm((2, seq, frames, HALF, width), low),
        g_send=vm((frames, seq, 2, HALF, width), low),
        g_pos=vm((2, every, HALF, width), low),
        d_pos=vm((2, every, HALF, 3 * width), low),
        d_recv=vm((2, seq, frames, HALF, 3 * width), low),
        att_t=vm((2, 2, rows, width), low),
        att_s=vm((2, 2, rows, width), low),
        part=vm((4, 2, rows, half), low),
        pair=vm((4, rows, half), low),
        other=vm((4, rows, half), low),
        total=vm((4, 2, rows, half), low),
        cls_send=vm((8, model), FLOAT),
        cls_recv=vm((seq, 8, model), FLOAT),
        gcm=vm((8, model), FLOAT),
        v_send=vm((3, 8, model), FLOAT),
        v_recv=vm((3, seq, 8, model), FLOAT),
        v_head=vm((4, 8, model), FLOAT),
    )
    for name, columns in grad_columns(dims):
        shapes["g_" + name] = vm((seq // 2, 2, model // seq, columns), low)
        shapes["y_" + name] = vm((seq // 2, model // seq, columns), low)
        shapes["z_" + name] = vm((seq // 2, model // seq, columns), low)
    for name in VECTORS:
        shapes[name] = vm((hidden if name == "m_ub" else model,), FLOAT)
    for name in PAIRS:
        shapes[name] = vm((2, width), FLOAT)
    shapes["load"] = pltpu.SemaphoreType.DMA((32,))
    shapes["sent"] = pltpu.SemaphoreType.DMA((240,))
    shapes["got"] = pltpu.SemaphoreType.DMA((240,))
    return shapes


def grad_columns(dims):
    width, model, hidden = dims["width"], dims["model"], dims["hidden"]
    return (
        ("dn", hidden),
        ("up", hidden),
        ("si", 3 * width),
        ("so", width),
        ("tl", width),
        ("to", width),
        ("ti", 3 * width),
    )


VECTORS = ("t_gain", "t_beta", "t_ob", "t_lb", "s_gain", "s_beta", "s_ob", "m_gain", "m_beta", "m_db", "m_ub")
PAIRS = ("t_qv", "s_qv")
MATRICES = ("tok", "out_grad", "w_ti", "w_to", "w_tl", "w_si", "w_so", "w_up", "w_dn")
INPUTS = ("lens", "cls", "cls_grad") + tuple("h_" + name for name in VECTORS + PAIRS + MATRICES)
OUTPUTS = ("o_blk", "o_cls", "o_tok", "o_vec")


class Refs:
    pass


def layer_kernel(dims, names, *refs):
    k = Refs()
    for name, ref in zip(names, refs):
        setattr(k, name, ref)
    frames, seq, width, model, hidden = dims["frames"], dims["seq"], dims["width"], dims["model"], dims["hidden"]
    patches, clips, pos = dims["patches"], dims["clips"], dims["pos"]
    rows, every, heads, half = frames * ROWS, frames * seq, width // HEAD_DIM, model // 2
    zs = seq // 2
    scale = HEAD_DIM ** (-0.5)
    s, h = lax.axis_index("seq"), lax.axis_index("head")
    z, y = s // 2, s % 2
    x, c = h // 2, h % 2
    other_c = 1 - c
    sister, across, diagonal = (s, x * 2 + other_c), (s, (1 - x) * 2 + c), (s, (1 - x) * 2 + other_c)
    y_peer = (z * 2 + 1 - y, h)
    z_peers = [((z + i) % zs) for i in range(1, zs)]
    peers = [((z + i) % zs) * 2 + (y + j) % 2 for i in range(zs) for j in range(2) if i or j]
    used = [0]

    def send(src, dst, device):
        index = used[0]
        used[0] += 1
        copy = pltpu.make_async_remote_copy(
            src_ref=src,
            dst_ref=dst,
            send_sem=k.sent.at[index],
            recv_sem=k.got.at[index],
            device_id=device,
            device_id_type=MESH,
        )
        copy.start()
        unsent.append(copy)
        return copy

    unsent = []
    loads = [0]

    def load(src, dst):
        copy = pltpu.make_async_copy(src, dst, k.load.at[loads[0]])
        loads[0] += 1
        copy.start()
        return copy

    def blocks(body, unroll=False):
        if unroll:
            for i in range(rows // BLOCK):
                body(pl.ds(i * BLOCK, BLOCK))
        else:

            def step(i, carry):
                body(pl.ds(pl.multiple_of(i * BLOCK, BLOCK), BLOCK))
                return carry

            lax.fori_loop(0, rows // BLOCK, step, 0)

    places = {"w_to": k.w_to.at[0, c], "w_so": k.w_so.at[0, c]}
    order = ("tok", "t_gain", "t_beta", "w_ti", "t_qv", "w_to", "w_so", "out_grad", "w_dn") + VECTORS[2:] + ("s_qv", "w_tl", "w_si", "w_up")
    loading = {name: load(getattr(k, "h_" + name), places.get(name, getattr(k, name))) for name in order}

    def need(*wanted):
        for name in wanted:
            loading.pop(name).wait()

    barrier = pltpu.get_barrier_semaphore()
    everyone = [(p, h) for p in peers] + [sister, across, diagonal]
    for device in everyone:
        pl.semaphore_signal(barrier, inc=1, device_id=device, device_id_type=MESH)

    def vec(name):
        if name in loading:
            need(name)
        return getattr(k, name)[...].reshape(1, -1)

    def qkv_row(name):
        need(name)
        pair = getattr(k, name)
        return jnp.concatenate([pair[0:1, :], jnp.zeros((1, width), FLOAT), pair[1:2, :]], axis=-1)

    def chosen(slot, row, outer):
        if outer:
            device, place = slot // SLOTS, slot % SLOTS
        else:
            device, place = slot // HALF % seq, slot // (HALF * seq) * HALF + slot % HALF
        hit = (device * pos + place == row) & (place < pos) & (row < patches)
        return jnp.where(hit, 1.0, 0.0).astype(BHALF)

    k.sel[...] = chosen(iota((seq * SLOTS, ROWS), 0), iota((seq * SLOTS, ROWS), 1), True)
    ends = []
    for i in range(clips):
        ends.append(k.lens[i] + (ends[-1] if i else 0))

    def clip_of(frame):
        total = (frame >= ends[0]).astype(jnp.int32)
        for end in ends[1:]:
            total = total + (frame >= end).astype(jnp.int32)
        return total

    onehot = []
    for f in range(frames):
        own = clip_of(jnp.full((1, model), s * frames + f, jnp.int32))
        onehot.append([(own == i).astype(FLOAT) for i in range(clips)])
    per_len = [1.0 / jnp.full((1, model), k.lens[i], jnp.int32).astype(FLOAT) for i in range(clips)]
    cls32 = k.cls[...].astype(FLOAT)
    cls_row = [sum(onehot[f][i] * cls32[i : i + 1] for i in range(clips)) for f in range(frames)]
    tail = ROWS - patches

    def set_tail(ref, f, first):
        used_rows = sum(r.shape[0] for r in first)
        fill = [jnp.zeros((tail - used_rows, model), FLOAT)] if used_rows < tail else []
        ref[f * ROWS + patches : (f + 1) * ROWS, :] = jnp.concatenate(list(first) + fill, axis=0)

    def eight(values):
        missing = 8 - sum(v.shape[0] for v in values)
        fill = [jnp.zeros((missing, model), FLOAT)] if missing else []
        return jnp.concatenate(list(values) + fill, axis=0)

    def norm_rows(src, which, gain, shift, xhat, out, r):
        v = src[r, :]
        center = v - jnp.mean(v, axis=-1, keepdims=True)
        invstd = lax.rsqrt(jnp.mean(center * center, axis=-1, keepdims=True) + EPS)
        n = center * invstd
        xhat[r, :] = n
        k.inv[which, r, :] = jnp.broadcast_to(invstd, (v.shape[0], 128))
        out[r, :] = (n * gain + shift).astype(BHALF)

    def norm(src, which, gain, shift, xhat, out):
        blocks(lambda r: norm_rows(src, which, gain, shift, xhat, out, r), unroll=dims["unroll"])

    need("tok")
    for f in range(frames):
        k.x32[f * ROWS : f * ROWS + patches, :] = k.tok[:, f, :].astype(FLOAT)
        set_tail(k.x32, f, [])
    t_gain = vec("t_gain")
    norm(k.x32, 0, t_gain, vec("t_beta"), k.xh_t, k.n_t)
    need("w_ti")
    t_qb = qkv_row("t_qv")

    def frame(f):
        return slice(f * ROWS, (f + 1) * ROWS)

    def scatter(f, value, src, dst):
        moved = dot_nn(k.sel[...], value).astype(BHALF)
        src[f] = moved.reshape(seq, 2, HALF, value.shape[-1])
        to = frames * s + f
        copies = [send(src.at[f, p], dst.at[:, to], (p, h)) for p in peers]
        dst[:, to] = src[f, s]
        return copies

    def gather(b, src, dst):
        copies = [send(src.at[b, pl.ds(frames * p, frames)], dst.at[b, s], (p, h)) for p in peers]
        dst[b, s] = src[b, pl.ds(frames * s, frames)]
        return copies

    def gathered(f, src):
        return dot_nn(k.les[...], src[:, :, f].reshape(seq * SLOTS, src.shape[-1])).astype(BHALF)

    def arrived(copies):
        for copy in copies:
            copy.wait_recv()

    q_copies = []
    for f in range(frames):
        qkv = (dot_nt(k.n_t[frame(f), :], k.w_ti[...]) + t_qb).astype(BHALF)
        if f == 0:
            pl.semaphore_wait(barrier, len(everyone))
        q_copies += scatter(f, qkv, k.q_send, k.q_pos)

    def share(ref):
        return send(ref.at[0, c], ref.at[0, c], sister), send(ref.at[0, c], ref.at[1, c], across)

    def pass_on(ref):
        return send(ref.at[1, c], ref.at[1, c], sister)

    need("w_to", "w_so")
    w_to_near, w_to_far = share(k.w_to)
    w_so_near, w_so_far = share(k.w_so)

    k.les[...] = chosen(iota((ROWS, seq * SLOTS), 1), iota((ROWS, seq * SLOTS), 0), False)
    span = every * HALF
    left, right = iota((span, span), 0), iota((span, span), 1)
    same = (left % HALF == right % HALF) & (clip_of(left // HALF) == clip_of(right // HALF))
    near = jnp.abs(left // HALF - right // HALF) < MAXLEN
    k.tmask[...] = jnp.where(same & near, 0.0, NEG)
    need("out_grad")
    cls_g = k.cls_grad[...].astype(FLOAT)
    for f in range(frames):
        k.gr32[f * ROWS : f * ROWS + patches, :] = k.out_grad[:, f, :].astype(FLOAT)
        set_tail(k.gr32, f, [cls_g] if f == 0 else [])

    def cast_rows(src, dst):
        def body(r):
            dst[r, :] = src[r, :].astype(BHALF)

        blocks(body)

    cast_rows(k.gr32, k.gr16)
    need("w_dn")
    k.dact[...] = dot_nt(k.gr16[...], k.w_dn[...])
    w_to_far.wait_recv()
    w_to_last = pass_on(k.w_to)
    w_so_far.wait_recv()
    w_so_last = pass_on(k.w_so)

    def attend(q, key, value, mask, p_ref):
        scores = dot_nt(q, key) * scale + mask
        e = jnp.exp(scores - jnp.max(scores, axis=-1, keepdims=True))
        p = e * (1.0 / jnp.sum(e, axis=-1, keepdims=True))
        p_ref[...] = p
        return dot_nn(p.astype(BHALF), value).astype(BHALF)

    def attend_back(q, key, value, grad, p_ref):
        p = p_ref[...]
        grad_p = p * dot_nt(grad, value)
        grad_s = (grad_p - p * jnp.sum(grad_p, axis=-1, keepdims=True)).astype(BHALF)
        grad_q = (dot_nn(grad_s, key) * scale).astype(BHALF)
        grad_k = (dot_tn(grad_s, q) * scale).astype(BHALF)
        grad_v = dot_tn(p.astype(BHALF), grad).astype(BHALF)
        return grad_q, grad_k, grad_v

    def head_of(value, part, j):
        at = part * width + j * HEAD_DIM
        return value[:, at : at + HEAD_DIM]

    def attend_all(qkv, mask, p_ref, first):
        out = [
            attend(*[head_of(qkv, i, j) for i in range(3)], mask, p_ref.at[first + j]) for j in range(heads)
        ]
        return jnp.concatenate(out, axis=-1)

    def attend_back_all(qkv, grad, p_ref, first):
        out = [
            attend_back(*[head_of(qkv, i, j) for i in range(3)], head_of(grad, 0, j), p_ref.at[first + j])
            for j in range(heads)
        ]
        return jnp.concatenate([out[j][i] for i in range(3) for j in range(heads)], axis=-1)

    arrived(q_copies)
    a_copies = []
    for b in range(2):
        out = attend_all(k.q_pos[b].reshape(span, 3 * width), k.tmask[...], k.p_t, b * heads)
        k.a_pos[b] = out.reshape(every, HALF, width)
        a_copies += gather(b, k.a_pos, k.a_recv)
    arrived(a_copies)
    for f in range(frames):
        k.att_t[0, c, frame(f), :] = gathered(f, k.a_recv)

    def project(att, weight):
        near, far = share(att)
        near.wait_recv()
        k.t32[...] = dot_nn(att[0, 0], weight[0, 0]) + dot_nn(att[0, 1], weight[0, 1])
        far.wait_recv()
        last = pass_on(att)
        last.wait_recv()
        k.u32[...] = dot_nn(att[1, 0], weight[1, 0]) + dot_nn(att[1, 1], weight[1, 1])

    arrived([w_to_near, w_to_last])
    project(k.att_t, k.w_to)
    t_ob, t_lb = vec("t_ob"), vec("t_lb")

    def mid_rows(r):
        k.mid16[r, :] = (k.t32[r, :] + k.u32[r, :] + t_ob).astype(BHALF)

    blocks(mid_rows)
    need("w_tl")
    k.t32[...] = dot_nn(k.mid16[...], k.w_tl[...])

    def add_res(r):
        k.x32[r, :] = k.x32[r, :] + (k.t32[r, :] + t_lb).astype(BHALF).astype(FLOAT)

    blocks(add_res)
    for f in range(frames):
        set_tail(k.x32, f, [cls_row[f]])

    s_gain = vec("s_gain")
    norm(k.x32, 1, s_gain, vec("s_beta"), k.xh_s, k.n_s)
    need("w_si")
    k.sqkv[...] = (dot_nt(k.n_s[...], k.w_si[...]) + qkv_row("s_qv")).astype(BHALF)
    in_frame = jnp.where(iota((1, ROWS), 1) < patches + 1, 0.0, NEG)
    for f in range(frames):
        k.att_s[0, c, frame(f), :] = attend_all(k.sqkv[frame(f), :], in_frame, k.p_s, f * heads)
    arrived([w_so_near, w_so_last])
    project(k.att_s, k.w_so)
    s_ob = vec("s_ob")
    cls_at = [slice(f * ROWS + patches, f * ROWS + patches + 1) for f in range(frames)]
    space_cls = [k.t32[r, :] + k.u32[r, :] + s_ob for r in cls_at]
    parts = [sum(onehot[f][i] * space_cls[f] for f in range(frames)) for i in range(clips)]
    k.cls_send[...] = eight(parts)
    cls_copies = [send(k.cls_send, k.cls_recv.at[s], (p, h)) for p in peers]
    k.cls_recv[s] = k.cls_send[...]

    def add_space(r):
        k.x32[r, :] = k.x32[r, :] + (k.t32[r, :] + k.u32[r, :] + s_ob)

    blocks(add_space)
    for f in range(frames):
        set_tail(k.x32, f, [])

    m_gain, m_beta = vec("m_gain"), vec("m_beta")
    norm(k.x32, 2, m_gain, m_beta, k.xh_m, k.n_m)
    need("w_up")
    k.t32[...] = dot_nn(k.n_m[...], k.w_up[...])
    arrived(cls_copies)
    cls_sum = k.cls_recv[0]
    for i in range(1, seq):
        cls_sum = cls_sum + k.cls_recv[i]
    set_tail(k.x32, 0, [cls32[i : i + 1] + cls_sum[i : i + 1] * per_len[i] for i in range(clips)])
    last_block = slice(ROWS - HALF, ROWS)
    norm_rows(k.x32, 2, m_gain, m_beta, k.xh_m, k.n_m, last_block)
    k.t32[last_block, :] = dot_nn(k.n_m[last_block, :], k.w_up[...])
    first_seq = jnp.where(s == 0, 1.0, 0.0)
    m_ub = vec("m_ub")

    def kept(r):
        at = r.start + iota((BLOCK, 1), 0)
        return jnp.where((at >= patches) & (at < ROWS), first_seq, 1.0)

    def gelu_rows(r):
        pre = k.t32[r, :] + m_ub
        cdf = 0.5 * (1.0 + lax.erf(pre * 0.7071067811865476))
        slope = cdf + pre * jnp.exp(-0.5 * pre * pre) * 0.3989422804014327
        act = pre * cdf
        grad = k.dact[r, :] * slope
        keep = kept(r)
        k.act[r, :] = act.astype(BHALF)
        k.act_k[r, :] = (act * keep).astype(BHALF)
        k.gpre[r, :] = grad.astype(BHALF)
        k.gpre_k[r, :] = (grad * keep).astype(BHALF)

    blocks(gelu_rows)

    def sum_make(i, lhs, rhs, dot):
        for b in range(2):
            cut = slice(b * half, (b + 1) * half)
            k.part[i, b] = dot(lhs[...], rhs[cut, :] if dot is dot_nt else rhs[:, cut]).astype(BHALF)

    def sum_open(i):
        return send(k.part.at[i, other_c], k.pair.at[i], sister)

    def sum_across(i, copy):
        copy.wait_recv()
        k.part[i, c] = (k.part[i, c].astype(FLOAT) + k.pair[i].astype(FLOAT)).astype(BHALF)
        return send(k.part.at[i, c], k.other.at[i], across)

    def sum_close(i, copy):
        copy.wait_recv()
        k.total[i, c] = (k.part[i, c].astype(FLOAT) + k.other[i].astype(FLOAT)).astype(BHALF)
        return send(k.total.at[i, c], k.total.at[i, c], sister)

    def rows_of(ref, r):
        return jnp.concatenate([ref[0, r, :], ref[1, r, :]], axis=-1).astype(FLOAT)

    def grad_make(name, lhs, rhs):
        g = getattr(k, "g_" + name)
        g[...] = dot_tn(lhs, rhs).astype(BHALF).reshape(g.shape)

    def grad_open(name):
        g, got = getattr(k, "g_" + name), getattr(k, "y_" + name)
        return name, [send(g.at[p, 1 - y], got.at[p], y_peer) for p in z_peers + [z]]

    def grad_along(job):
        name, opened = job
        g, got, last = [getattr(k, kind + name) for kind in ("g_", "y_", "z_")]
        copies = []
        for p, copy in zip(z_peers, opened):
            copy.wait_recv()
            g[p, y] = (g[p, y].astype(FLOAT) + got[p].astype(FLOAT)).astype(BHALF)
            copies.append(send(g.at[p, y], last.at[z], (p * 2 + y, h)))
        opened[-1].wait_recv()
        last[z] = (g[z, y].astype(FLOAT) + got[z].astype(FLOAT)).astype(BHALF)
        return name, copies

    def grad_close(job):
        name, copies = job
        last, out = getattr(k, "z_" + name), getattr(k, "o_" + name)
        arrived(copies)
        out[...] = sum(last[i].astype(FLOAT) for i in range(zs))

    def vectors_send(which, values):
        value = eight(values)
        k.v_send[which] = value
        k.v_recv[which, s] = value
        return [send(k.v_send.at[which], k.v_recv.at[which, s], (p, h)) for p in peers]

    def vectors_close(which, copies):
        arrived(copies)
        value = k.v_recv[which, 0]
        for i in range(1, seq):
            value = value + k.v_recv[which, i]
        return value

    ones = jnp.ones((8, rows), BHALF)
    at = iota((8, rows), 1)
    ones_kept = jnp.where((at >= patches) & (at < ROWS), first_seq, 1.0).astype(BHALF)

    def col_sums(ref, weights=None):
        out = dot_nn(ones if weights is None else weights, ref[...])[0:1]
        if out.shape[1] < model:
            out = jnp.concatenate([out, jnp.zeros((1, model - out.shape[1]), FLOAT)], axis=-1)
        return out

    def block_sums(body):
        def step(b, sums):
            pair = body(pl.ds(pl.multiple_of(b * BLOCK, BLOCK), BLOCK))
            return tuple(t + jnp.sum(v.reshape(BLOCK // 8, 8, model), axis=0) for t, v in zip(sums, pair))

        zero = jnp.zeros((8, model), FLOAT)
        sums = lax.fori_loop(0, rows // BLOCK, step, (zero, zero))
        return [jnp.sum(v, axis=0, keepdims=True) for v in sums]

    def norm_back(i, which, gain, xhat, keep, use):
        def body(r):
            g = rows_of(k.total.at[i], r)
            n = xhat[r, :]
            gh = g * gain
            m1 = jnp.mean(gh, axis=-1, keepdims=True)
            m2 = jnp.mean(gh * n, axis=-1, keepdims=True)
            use(r, k.inv[which, r, 0:1] * (gh - m1 - n * m2))
            w = g * kept(r) if keep else g
            return w * n, w

        return block_sums(body)

    sum_make(0, k.gpre, k.w_up, dot_nt)
    m_sum = sum_open(0)
    grad_make("dn", k.gr16[...], k.act_k[...])
    m_sum = sum_across(0, m_sum)
    j_dn = grad_open("dn")
    grad_make("up", k.n_m[...], k.gpre_k[...])
    j_up = grad_open("up")
    sum_make(1, k.act, k.w_dn, dot_nn)
    o_sum = sum_open(1)
    ub_grad, db_grad = col_sums(k.gpre_k), col_sums(k.gr16, ones_kept)
    m_last = sum_close(0, m_sum)
    o_sum = sum_across(1, o_sum)
    m_last.wait_recv()

    def use_m(r, dx):
        k.gr32[r, :] = k.gr32[r, :] + dx

    sums = norm_back(0, 2, m_gain, k.xh_m, True, use_m)
    v_m = vectors_send(0, [sums[0], sums[1], ub_grad, db_grad])
    grad_cls_mid = k.gr32[patches : patches + clips, :]
    k.gcm[...] = eight([grad_cls_mid])
    for f in range(frames):
        shared = sum(onehot[f][i] * (grad_cls_mid[i : i + 1] * per_len[i]) for i in range(clips))
        set_tail(k.gr32, f, [shared])
    cast_rows(k.gr32, k.gss)
    for f in range(frames):
        set_tail(k.gr32, f, [])

    k.gatt[...] = dot_nt(k.gss[...], k.w_so[0, c]).astype(BHALF)
    for f in range(frames):
        k.dsq[frame(f), :] = attend_back_all(k.sqkv[frame(f), :], k.gatt[frame(f), :], k.p_s, f * heads)
    sum_make(2, k.dsq, k.w_si, dot_nn)
    s_sum = sum_open(2)
    j_dn = grad_along(j_dn)
    s_sum = sum_across(2, s_sum)
    grad_make("si", k.n_s[...], k.dsq[...])
    j_si = grad_open("si")
    grad_make("so", k.gss[...], k.att_s[0, c])
    j_so = grad_open("so")
    o_last = sum_close(1, o_sum)
    s_rows = [col_sums(k.gss), col_sums(k.dsq)]
    j_up = grad_along(j_up)
    o_last.wait_recv()
    m_db = vec("m_db")

    def out_rows(r):
        k.t32[r, :] = k.x32[r, :] + rows_of(k.total.at[1], r) + m_db

    blocks(out_rows)
    for f in range(frames):
        k.o_blk[:, f, :] = k.t32[f * ROWS : f * ROWS + patches, :].astype(BHALF)
    k.o_cls[...] = k.t32[patches : patches + clips, :].astype(BHALF)
    s_last = sum_close(2, s_sum)
    s_last.wait_recv()
    sums = norm_back(2, 1, s_gain, k.xh_s, False, use_m)
    cls_in = [k.gr32[r, :] for r in cls_at]
    cls_parts = [sum(onehot[f][i] * cls_in[f] for f in range(frames)) for i in range(clips)]
    for f in range(frames):
        set_tail(k.gr32, f, [])
    cast_rows(k.gr32, k.gtr)

    k.gtm[...] = dot_nt(k.gtr[...], k.w_tl[...]).astype(BHALF)
    k.gatt[...] = dot_nt(k.gtm[...], k.w_to[0, c]).astype(BHALF)
    g_copies = []
    for f in range(frames):
        g_copies += scatter(f, k.gatt[frame(f), :], k.g_send, k.g_pos)
    v_s = vectors_send(1, [sums[0], sums[1]] + s_rows + cls_parts)
    pick = (iota((model, width), 0) == h * width + iota((model, width), 1)).astype(FLOAT).astype(BHALF)
    grad_make("tl", k.mid16[...], dot_nn(k.gtr[...], pick).astype(BHALF))
    grad_make("to", k.gtm[...], k.att_t[0, c])
    t_rows = [col_sums(k.gtm), col_sums(k.gtr)]
    arrived(g_copies)
    d_copies = []
    for b in range(2):
        value = attend_back_all(
            k.q_pos[b].reshape(span, 3 * width), k.g_pos[b].reshape(span, width), k.p_t, b * heads
        )
        k.d_pos[b] = value.reshape(every, HALF, 3 * width)
        d_copies += gather(b, k.d_pos, k.d_recv)
    j_tl = grad_open("tl")
    j_to = grad_open("to")
    j_si = grad_along(j_si)
    j_so = grad_along(j_so)
    grad_close(j_dn)
    m_vec = vectors_close(0, v_m)
    s_vec = vectors_close(1, v_s)
    k.o_vec[0:8, :] = m_vec
    k.o_vec[8:16, :] = s_vec + jnp.concatenate([jnp.zeros((4, model), FLOAT), k.gcm[0:4, :]], axis=0)
    arrived(d_copies)
    for f in range(frames):
        k.dtq[frame(f), :] = gathered(f, k.d_recv)
    sum_make(3, k.dtq, k.w_ti, dot_nn)
    t_sum = sum_open(3)
    grad_make("ti", k.n_t[...], k.dtq[...])
    j_ti = grad_open("ti")

    def partial(r):
        g = rows_of(k.part.at[3], r)
        return g * k.xh_t[r, :], g

    sums = block_sums(partial)
    t_sum = sum_across(3, t_sum)
    v_t = vectors_send(2, [sums[0], sums[1], t_rows[0], col_sums(k.dtq), t_rows[1]])
    j_tl = grad_along(j_tl)
    j_to = grad_along(j_to)
    grad_close(j_up)
    grad_close(j_si)
    grad_close(j_so)
    t_vec = vectors_close(2, v_t)
    k.v_head[h] = t_vec
    h_copies = [send(k.v_head.at[h], k.v_head.at[h], device) for device in (sister, across, diagonal)]
    j_ti = grad_along(j_ti)
    t_last = sum_close(3, t_sum)
    grad_close(j_tl)
    grad_close(j_to)
    t_last.wait_recv()

    def use_t(r, dx):
        k.t32[r, :] = k.gr32[r, :] + dx.astype(BHALF).astype(FLOAT)

    norm_back(3, 0, t_gain, k.xh_t, False, use_t)
    for f in range(frames):
        k.o_tok[:, f, :] = k.t32[f * ROWS : f * ROWS + patches, :].astype(BHALF)
    arrived(h_copies)
    over_head = k.v_head[0] + k.v_head[1] + k.v_head[2] + k.v_head[3]
    k.o_vec[16:24, :] = jnp.concatenate([over_head[0:2], t_vec[2:8]], axis=0)
    grad_close(j_ti)
    for copy in unsent:
        copy.wait_send()


def finish_kernel(dims, h_blk, h_tok, vec, cls_out, g_dn, g_up, g_si, g_so, g_tl, g_to, g_ti, *refs):
    width, model, seq = dims["width"], dims["model"], dims["seq"]
    share, clips = model // seq, dims["clips"]
    o_blk, o_cls, o_tok, cls, tg, tb, ti, tp, to, tob, tl, tlb, sg, sb, si, sp, so, sob, mg, mb, up, ub, dn, db = refs
    o_blk[...] = h_blk[...]
    o_tok[...] = h_tok[...]
    s = lax.axis_index("seq")
    v = vec[...]
    mine = pltpu.roll(v, (model - share * s) % model, 1)[:, :share]
    for out, row in ((mg, 0), (sg, 8), (tg, 16)):
        out[...] = mine[row : row + 1].reshape(share)
    for out, row in ((mb, 1), (ub, 2), (db, 3), (sb, 9), (sob, 10), (tb, 17), (tob, 18), (tlb, 20)):
        out[...] = v[row : row + 1].reshape(model)
    cls[...] = mine[12 : 12 + clips]
    o_cls[...] = cls_out[...]
    for out, row in ((sp, 11), (tp, 19)):
        out[0:1, :] = v[row : row + 1, :width]
        out[1:2, :] = v[row : row + 1, 2 * width : 3 * width]
    for out, g in ((si, g_si), (ti, g_ti)):
        for i in range(3):
            out[i] = g[:, i * width : (i + 1) * width]
    tl[...] = g_tl[...]
    up[...] = g_up[...]
    dn[...] = g_dn[...]
    to[...] = g_to[...].T
    so[...] = g_so[...].T


def fused_body(
    tokens,
    cls_tokens,
    clip_lengths,
    time_gain,
    time_beta,
    time_proj_in,
    time_qv_bias,
    time_proj_out,
    time_out_bias,
    time_linear,
    time_linear_bias,
    space_gain,
    space_beta,
    space_proj_in,
    space_qv_bias,
    space_proj_out,
    space_out_bias,
    mlp_gain,
    mlp_beta,
    mlp_up,
    mlp_up_bias,
    mlp_down,
    mlp_down_bias,
    out_grad,
    cls_grad,
):
    frames, patches, model = tokens.shape
    seq = lax.axis_size("seq")
    width, hidden, clips = time_proj_in.shape[2], mlp_up.shape[1], clip_lengths.shape[0]
    dims = dict(
        frames=frames,
        patches=patches,
        model=model,
        seq=seq,
        width=width,
        hidden=hidden,
        clips=clips,
        pos=-(-patches // seq),
        unroll=False,
    )

    def frames_inner(v):
        return jnp.transpose(v, (1, 0, 2))

    def outputs_first(v):
        return jnp.transpose(v, (1, 2, 0)).reshape(3 * width, model)

    scratch = scratch_shapes(dims)
    grads = grad_columns(dims)
    share = model // seq
    shape = jax.ShapeDtypeStruct
    vmem, anywhere = pl.BlockSpec(memory_space=pltpu.VMEM), pl.BlockSpec(memory_space=pl.ANY)
    inner = (patches, frames, model)
    outs = [
        shape(inner, BHALF),
        shape(cls_tokens.shape, BHALF),
        shape(inner, BHALF),
        shape((24, model), FLOAT),
    ] + [shape((share, columns), FLOAT) for _, columns in grads]
    names = list(INPUTS) + list(OUTPUTS) + ["o_" + name for name, _ in grads] + list(scratch)
    results = pl.pallas_call(
        functools.partial(layer_kernel, dims, names),
        out_shape=outs,
        in_specs=[pl.BlockSpec(memory_space=pltpu.SMEM)] + [vmem] * 2 + [anywhere] * (len(INPUTS) - 3),
        out_specs=[vmem] * len(outs),
        scratch_shapes=list(scratch.values()),
        compiler_params=pltpu.CompilerParams(
            collective_id=0, has_side_effects=True, vmem_limit_bytes=62 * 1024 * 1024
        ),
        name="layer",
    )(
        clip_lengths,
        cls_tokens,
        cls_grad,
        time_gain,
        time_beta,
        time_out_bias,
        time_linear_bias,
        space_gain,
        space_beta,
        space_out_bias,
        mlp_gain,
        mlp_beta,
        mlp_down_bias,
        mlp_up_bias,
        time_qv_bias,
        space_qv_bias,
        frames_inner(tokens),
        frames_inner(out_grad),
        outputs_first(time_proj_in),
        time_proj_out,
        time_linear,
        outputs_first(space_proj_in),
        space_proj_out,
        mlp_up,
        mlp_down,
    )
    blk, cls_out, tok, vectors = results[:4]
    row, gain = shape((model,), FLOAT), shape((share,), FLOAT)
    proj, pair = shape((3, share, width), FLOAT), shape((2, width), FLOAT)
    out_shape = [
        shape(inner, BHALF),
        shape(cls_tokens.shape, BHALF),
        shape(inner, BHALF),
        shape((clips, share), FLOAT),
        gain,
        row,
        proj,
        pair,
        shape((width, share), FLOAT),
        row,
        shape((share, width), FLOAT),
        row,
        gain,
        row,
        proj,
        pair,
        shape((width, share), FLOAT),
        row,
        gain,
        row,
        shape((share, hidden), FLOAT),
        shape((hidden,), FLOAT),
        shape((share, hidden), FLOAT),
        row,
    ]
    last = pl.pallas_call(
        functools.partial(finish_kernel, dims),
        out_shape=out_shape,
        in_specs=[vmem] * 11,
        out_specs=[vmem] * len(out_shape),
        compiler_params=pltpu.CompilerParams(vmem_limit_bytes=62 * 1024 * 1024),
        name="finish",
    )(blk, tok, vectors, cls_out, *results[4:])
    last = list(last)
    for i in (0, 2, 6, 14):
        last[i] = jnp.transpose(last[i], (1, 0, 2))
    last[22] = last[22].T
    return tuple(last)


def solution(mesh):
    placed = (
        P("seq", None, None),
        P(),
        P(),
        P(),
        P(),
        P(None, None, "head"),
        P(None, "head"),
        P("head", None),
        P(),
        P(),
        P(),
        P(),
        P(),
        P(None, None, "head"),
        P(None, "head"),
        P("head", None),
        P(),
        P(),
        P(),
        P(None, "head"),
        P("head"),
        P("head", None),
        P(),
        P("seq", None, None),
        P(),
    )
    fused = mesh.shape["seq"] == 8 and mesh.shape["head"] == 4
    return jax.shard_map(
        fused_body if fused else body,
        mesh=mesh,
        in_specs=placed,
        out_specs=(
            P("seq", None, None),
            P(),
            P("seq", None, None),
            P(None, "seq"),
            P("seq"),
            P(),
            P("seq", None, "head"),
            P(None, "head"),
            P("head", "seq"),
            P(),
            P("seq", "head"),
            P(),
            P("seq"),
            P(),
            P("seq", None, "head"),
            P(None, "head"),
            P("head", "seq"),
            P(),
            P("seq"),
            P(),
            P("seq", "head"),
            P("head"),
            P("head", "seq"),
            P(),
        ),
        check_vma=False,
    )
```

```python
import functools

import jax
import jax.numpy as jnp
from jax import lax
from jax.experimental import pallas as pl
from jax.experimental.pallas import tpu as pltpu
from jax.sharding import PartitionSpec as P

HEAD_DIM = 64
PATCH = 196
MAXLEN = 8


EPS = 1e-06
NEG = -1e30
FLOAT = jnp.float32
BHALF = jnp.bfloat16


def matmul_plain(left, right):
    return jnp.dot(left, right, preferred_element_type=FLOAT)


def matmul_tn(left, right):
    return lax.dot_general(left, right, (((0,), (0,)), ((), ())), preferred_element_type=FLOAT)


def matmul_nt(left, right):
    return lax.dot_general(left, right, (((1,), (1,)), ((), ())), preferred_element_type=FLOAT)


def exact_tn(left, right):
    return lax.dot_general(
        left,
        right,
        (((0,), (0,)), ((), ())),
        precision=lax.Precision.HIGHEST,
        preferred_element_type=FLOAT,
    )


def exact_nn(left, right):
    return jnp.dot(left, right, precision=lax.Precision.HIGHEST, preferred_element_type=FLOAT)


def layer_norm(rows, gain, shift):
    center = rows - jnp.mean(rows, axis=-1, keepdims=True)
    invstd = lax.rsqrt(jnp.mean(center * center, axis=-1, keepdims=True) + EPS)
    normed = center * invstd
    return (normed * gain + shift, normed, invstd)


def norm_back(grad_out, gain, normed, invstd, row_weight):
    feature_count = grad_out.shape[-1]
    grad_norm = grad_out * gain
    weighted = grad_out * row_weight
    gain_grad = jnp.sum((weighted * normed).reshape(-1, feature_count), axis=0)
    shift_grad = jnp.sum(weighted.reshape(-1, feature_count), axis=0)
    first_mean = jnp.mean(grad_norm, axis=-1, keepdims=True)
    second_mean = jnp.mean(grad_norm * normed, axis=-1, keepdims=True)
    return (invstd * (grad_norm - first_mean - normed * second_mean), gain_grad, shift_grad)


def qkv_shift(pair):
    return jnp.stack([pair[0], jnp.zeros_like(pair[0]), pair[1]], axis=0).reshape(-1)


def pair_sums(grad_qkv, local_width):
    sums = jnp.sum(grad_qkv.astype(FLOAT).reshape(-1, 3, local_width), axis=0)
    return jnp.stack([sums[0], sums[2]], axis=0)


def gelu_slope(pre):
    normal_cdf = 0.5 * (1.0 + jax.scipy.special.erf(pre * 0.7071067811865476))
    return normal_cdf + pre * jnp.exp(-0.5 * pre * pre) * 0.3989422804014327


def band_stack(values, band_reach):
    frames = values.shape[0]
    padded = jnp.pad(values, ((band_reach, band_reach),) + ((0, 0),) * (values.ndim - 1))
    return jnp.stack(
        [padded[offset : offset + frames] for offset in range(2 * band_reach + 1)], axis=2
    )


def band_return(contrib, band_reach):
    frames = contrib.shape[0]
    padded = jnp.pad(contrib, ((band_reach, band_reach),) + ((0, 0),) * (contrib.ndim - 1))
    total = jnp.zeros((frames,) + contrib.shape[1:2] + contrib.shape[3:], FLOAT)
    for offset in range(2 * band_reach + 1):
        start = 2 * band_reach - offset
        total = total + padded[start : start + frames, :, offset]
    return total


def to_positions(frame_major):
    frames_dev, patches, columns = frame_major.shape
    seq_count = lax.axis_size("seq")
    pos_dev = (patches + seq_count - 1) // seq_count
    padded = jnp.pad(frame_major, ((0, 0), (0, pos_dev * seq_count - patches), (0, 0)))
    moved = lax.all_to_all(
        padded.reshape(frames_dev, seq_count, pos_dev, columns),
        "seq",
        split_axis=1,
        concat_axis=0,
        tiled=True,
    )
    return moved.reshape(frames_dev * seq_count, pos_dev, columns)


def to_frames(pos_major):
    frames_all, pos_dev, columns = pos_major.shape
    seq_count = lax.axis_size("seq")
    moved = lax.all_to_all(
        pos_major.reshape(frames_all, 1, pos_dev, columns),
        "seq",
        split_axis=0,
        concat_axis=1,
        tiled=True,
    )
    return moved.reshape(frames_all // seq_count, seq_count * pos_dev, columns)[:, :PATCH]


def head_cols(pieces):
    return lax.all_gather(pieces, "head", axis=2, tiled=True)


def time_scores(queries, key_band, valid, score_scale):
    raw = (
        jnp.einsum("fphd,fpohd->fpho", queries, key_band, preferred_element_type=FLOAT)
        * score_scale
    )
    return jnp.where(valid[:, None, None, :], raw, NEG)


def time_forward(queries, key_band, value_band, valid, score_scale):
    scores = time_scores(queries, key_band, valid, score_scale)
    largest = jnp.max(scores, axis=-1, keepdims=True)
    exponent = jnp.exp(scores - largest)
    totals = jnp.sum(exponent, axis=-1, keepdims=True)
    attend = (exponent / totals).astype(BHALF)
    result = jnp.einsum("fpho,fpohd->fphd", attend, value_band, preferred_element_type=FLOAT)
    return (result, largest + jnp.log(totals))


def time_backward(
    queries, key_band, value_band, valid, log_total, grad_out, score_scale, band_reach
):
    scores = time_scores(queries, key_band, valid, score_scale)
    attend = jnp.exp(scores - log_total)
    grad_attend = jnp.einsum("fphd,fpohd->fpho", grad_out, value_band, preferred_element_type=FLOAT)
    row_dot = jnp.sum(attend * grad_attend, axis=-1, keepdims=True)
    grad_score = (attend * (grad_attend - row_dot)).astype(BHALF)
    grad_query = (
        jnp.einsum("fpho,fpohd->fphd", grad_score, key_band, preferred_element_type=FLOAT)
        * score_scale
    )
    key_part = (
        jnp.einsum("fpho,fphd->fpohd", grad_score, queries, preferred_element_type=FLOAT)
        * score_scale
    )
    value_part = jnp.einsum(
        "fpho,fphd->fpohd", attend.astype(BHALF), grad_out, preferred_element_type=FLOAT
    )
    return (grad_query, band_return(key_part, band_reach), band_return(value_part, band_reach))


def space_forward(queries, key_rows, value_rows, score_scale):
    scores = (
        jnp.einsum("fqhd,fkhd->fhqk", queries, key_rows, preferred_element_type=FLOAT) * score_scale
    )
    largest = jnp.max(scores, axis=-1, keepdims=True)
    exponent = jnp.exp(scores - largest)
    totals = jnp.sum(exponent, axis=-1, keepdims=True)
    attend = (exponent / totals).astype(BHALF)
    result = jnp.einsum("fhqk,fkhd->fqhd", attend, value_rows, preferred_element_type=FLOAT)
    return (result, largest + jnp.log(totals))


def space_backward(queries, key_rows, value_rows, log_total, grad_out, score_scale):
    scores = (
        jnp.einsum("fqhd,fkhd->fhqk", queries, key_rows, preferred_element_type=FLOAT) * score_scale
    )
    attend = jnp.exp(scores - log_total)
    grad_attend = jnp.einsum("fqhd,fkhd->fhqk", grad_out, value_rows, preferred_element_type=FLOAT)
    row_dot = jnp.sum(attend * grad_attend, axis=-1, keepdims=True)
    grad_score = (attend * (grad_attend - row_dot)).astype(BHALF)
    grad_query = (
        jnp.einsum("fhqk,fkhd->fqhd", grad_score, key_rows, preferred_element_type=FLOAT)
        * score_scale
    )
    grad_key = (
        jnp.einsum("fhqk,fqhd->fkhd", grad_score, queries, preferred_element_type=FLOAT)
        * score_scale
    )
    grad_value = jnp.einsum(
        "fhqk,fqhd->fkhd", attend.astype(BHALF), grad_out, preferred_element_type=FLOAT
    )
    return (grad_query, grad_key, grad_value)


def body(
    tokens,
    cls_tokens,
    clip_lengths,
    time_gain,
    time_beta,
    time_proj_in,
    time_qv_bias,
    time_proj_out,
    time_out_bias,
    time_linear,
    time_linear_bias,
    space_gain,
    space_beta,
    space_proj_in,
    space_qv_bias,
    space_proj_out,
    space_out_bias,
    mlp_gain,
    mlp_beta,
    mlp_up,
    mlp_up_bias,
    mlp_down,
    mlp_down_bias,
    out_grad,
    cls_grad,
):
    frames_dev, patches, model_width = tokens.shape
    seq_count = lax.axis_size("seq")
    frames_all = frames_dev * seq_count
    clip_count = clip_lengths.shape[0]
    local_width = time_proj_in.shape[2]
    local_heads = local_width // HEAD_DIM
    band_reach = MAXLEN - 1
    score_scale = HEAD_DIM ** (-0.5)
    seq_rank = lax.axis_index("seq")
    head_rank = lax.axis_index("head")
    clip_ends = jnp.sum(
        jnp.where(jnp.tri(clip_lengths.shape[0], dtype=bool), clip_lengths[None, :], 0), axis=1
    )
    frame_ids = jnp.arange(frames_all, dtype=jnp.int32)
    clip_of = jnp.sum((frame_ids[:, None] >= clip_ends[None, :]).astype(jnp.int32), axis=1)
    clip_pad = jnp.pad(clip_of, (band_reach, band_reach), constant_values=-1)
    valid = jnp.stack(
        [clip_pad[offset : offset + frames_all] == clip_of for offset in range(2 * band_reach + 1)],
        axis=1,
    )
    local_clip = lax.dynamic_slice_in_dim(clip_of, seq_rank * frames_dev, frames_dev)
    onehot = (local_clip[:, None] == jnp.arange(clip_count, dtype=jnp.int32)[None, :]).astype(FLOAT)
    lengths = clip_lengths.astype(FLOAT)
    time_in = to_positions(tokens)
    pos_dev = time_in.shape[1]
    time_rows = frames_all * pos_dev
    time_normed, time_stat, time_inv = layer_norm(time_in.astype(FLOAT), time_gain, time_beta)
    time_normed = time_normed.astype(BHALF).reshape(time_rows, model_width)
    time_in_mat = time_proj_in.reshape(model_width, 3 * local_width)
    time_qkv = (
        (matmul_plain(time_normed, time_in_mat) + qkv_shift(time_qv_bias))
        .astype(BHALF)
        .reshape(frames_all, pos_dev, 3, local_heads, HEAD_DIM)
    )
    time_query = time_qkv[:, :, 0]
    time_keys = band_stack(time_qkv[:, :, 1], band_reach)
    time_values = band_stack(time_qkv[:, :, 2], band_reach)
    time_att, time_log = time_forward(time_query, time_keys, time_values, valid, score_scale)
    time_att = time_att.astype(BHALF).reshape(time_rows, local_width)
    time_mid = (
        lax.psum(matmul_plain(time_att, time_proj_out).astype(jnp.bfloat16), "head").astype(
            jnp.float32
        )
        + time_out_bias
    ).astype(BHALF)
    col_start = head_rank * local_width
    linear_cols = lax.dynamic_slice_in_dim(time_linear, col_start, local_width, 1)
    linear_shift = lax.dynamic_slice_in_dim(time_linear_bias, col_start, local_width)
    time_part = (
        (matmul_plain(time_mid, linear_cols) + linear_shift)
        .astype(BHALF)
        .reshape(frames_all, pos_dev, local_width)
    )
    time_res = to_frames(head_cols(time_part))
    mid = tokens.astype(FLOAT) + time_res.astype(FLOAT)
    span_rows = patches + 1
    space_rows = frames_dev * span_rows
    cls_rows = matmul_plain(onehot.astype(BHALF), cls_tokens)
    space_in = jnp.concatenate([cls_rows[:, None, :], mid], axis=1)
    space_normed, space_stat, space_inv = layer_norm(space_in, space_gain, space_beta)
    space_normed = space_normed.astype(BHALF).reshape(space_rows, model_width)
    space_in_mat = space_proj_in.reshape(model_width, 3 * local_width)
    space_qkv = (
        (matmul_plain(space_normed, space_in_mat) + qkv_shift(space_qv_bias))
        .astype(BHALF)
        .reshape(frames_dev, span_rows, 3, local_heads, HEAD_DIM)
    )
    space_query = space_qkv[:, :, 0]
    space_keys = space_qkv[:, :, 1]
    space_values = space_qkv[:, :, 2]
    space_att, space_log = space_forward(space_query, space_keys, space_values, score_scale)
    space_att = space_att.astype(BHALF).reshape(space_rows, local_width)
    space_sum = (
        lax.psum(matmul_plain(space_att, space_proj_out).astype(jnp.bfloat16), "head").astype(
            jnp.float32
        )
        + space_out_bias
    ).reshape(frames_dev, span_rows, model_width)
    after = mid + space_sum[:, 1:]
    cls_part = exact_tn(onehot, space_sum[:, 0])
    cls_mid = cls_tokens.astype(FLOAT) + lax.psum(cls_part, "seq") / lengths[:, None]
    tok_rows = frames_dev * patches
    rows = jnp.concatenate([after.reshape(tok_rows, model_width), cls_mid], axis=0)
    mlp_normed, mlp_stat, mlp_inv = layer_norm(rows, mlp_gain, mlp_beta)
    mlp_normed = mlp_normed.astype(BHALF)
    pre = matmul_plain(mlp_normed, mlp_up) + mlp_up_bias
    act = jax.nn.gelu(pre, approximate=False).astype(BHALF)
    result = (
        rows
        + lax.psum(matmul_plain(act, mlp_down).astype(jnp.bfloat16), "head").astype(jnp.float32)
        + mlp_down_bias
    )
    block_out = result[:tok_rows].reshape(frames_dev, patches, model_width).astype(BHALF)
    cls_out = result[tok_rows:].astype(BHALF)
    first_seq = (seq_rank == 0).astype(FLOAT)
    keep_rows = jnp.concatenate(
        [jnp.ones((tok_rows, 1), FLOAT), jnp.ones((clip_count, 1), FLOAT) * first_seq], axis=0
    )
    keep_half = keep_rows.astype(BHALF)
    grad_rows = jnp.concatenate([out_grad.reshape(tok_rows, model_width), cls_grad], axis=0)
    down_grad = matmul_tn(act * keep_half, grad_rows)
    down_shift_grad = jnp.sum(grad_rows.astype(FLOAT) * keep_rows, axis=0)
    grad_pre = (matmul_nt(grad_rows, mlp_down) * gelu_slope(pre)).astype(BHALF)
    up_grad = matmul_tn(mlp_normed * keep_half, grad_pre)
    up_shift_grad = jnp.sum(grad_pre.astype(FLOAT) * keep_rows, axis=0)
    grad_mlp_norm = lax.psum(matmul_nt(grad_pre, mlp_up).astype(jnp.bfloat16), "head").astype(
        jnp.float32
    )
    grad_mlp_in, mlp_gain_grad, mlp_beta_grad = norm_back(
        grad_mlp_norm, mlp_gain, mlp_stat, mlp_inv, keep_rows
    )
    grad_total = grad_rows.astype(FLOAT) + grad_mlp_in
    grad_after = grad_total[:tok_rows].reshape(frames_dev, patches, model_width)
    grad_cls_mid = grad_total[tok_rows:]
    cls_share = exact_nn(onehot, grad_cls_mid / lengths[:, None])
    grad_space_sum = (
        jnp.concatenate([cls_share[:, None, :], grad_after], axis=1)
        .astype(BHALF)
        .reshape(space_rows, model_width)
    )
    space_out_grad = matmul_tn(space_att, grad_space_sum)
    space_shift_grad = jnp.sum(grad_space_sum.astype(FLOAT), axis=0)
    grad_space_att = (
        matmul_nt(grad_space_sum, space_proj_out)
        .astype(BHALF)
        .reshape(frames_dev, span_rows, local_heads, HEAD_DIM)
    )
    space_grad_query, space_grad_key, space_grad_value = space_backward(
        space_query, space_keys, space_values, space_log, grad_space_att, score_scale
    )
    grad_space_qkv = (
        jnp.stack([space_grad_query, space_grad_key, space_grad_value], axis=2)
        .astype(BHALF)
        .reshape(space_rows, 3 * local_width)
    )
    space_in_grad = matmul_tn(space_normed, grad_space_qkv).reshape(model_width, 3, local_width)
    space_pair_grad = pair_sums(grad_space_qkv, local_width)
    grad_space_norm = (
        lax.psum(matmul_nt(grad_space_qkv, space_in_mat).astype(jnp.bfloat16), "head")
        .astype(jnp.float32)
        .reshape(frames_dev, span_rows, model_width)
    )
    grad_space_in, space_gain_grad, space_beta_grad = norm_back(
        grad_space_norm, space_gain, space_stat, space_inv, 1.0
    )
    grad_mid = grad_after + grad_space_in[:, 1:]
    cls_in_part = exact_tn(onehot, grad_space_in[:, 0])
    grad_time_res = to_positions(grad_mid.astype(BHALF)).reshape(time_rows, model_width)
    linear_grad = matmul_tn(
        time_mid, lax.dynamic_slice_in_dim(grad_time_res, col_start, local_width, 1)
    )
    linear_shift_grad = jnp.sum(grad_time_res.astype(FLOAT), axis=0)
    grad_time_mid = matmul_nt(grad_time_res, time_linear).astype(BHALF)
    time_out_grad = matmul_tn(time_att, grad_time_mid)
    time_shift_grad = jnp.sum(grad_time_mid.astype(FLOAT), axis=0)
    grad_time_att = (
        matmul_nt(grad_time_mid, time_proj_out)
        .astype(BHALF)
        .reshape(frames_all, pos_dev, local_heads, HEAD_DIM)
    )
    time_grad_query, time_grad_key, time_grad_value = time_backward(
        time_query, time_keys, time_values, valid, time_log, grad_time_att, score_scale, band_reach
    )
    grad_time_qkv = (
        jnp.stack([time_grad_query, time_grad_key, time_grad_value], axis=2)
        .astype(BHALF)
        .reshape(time_rows, 3 * local_width)
    )
    time_in_grad = matmul_tn(time_normed, grad_time_qkv).reshape(model_width, 3, local_width)
    time_pair_grad = pair_sums(grad_time_qkv, local_width)
    grad_time_norm = (
        lax.psum(matmul_nt(grad_time_qkv, time_in_mat).astype(jnp.bfloat16), "head")
        .astype(jnp.float32)
        .reshape(frames_all, pos_dev, model_width)
    )
    grad_time_in, time_gain_grad, time_beta_grad = norm_back(
        grad_time_norm, time_gain, time_stat, time_inv, 1.0
    )
    grad_tokens_time = to_frames(grad_time_in.astype(BHALF))
    tokens_grad = (grad_mid + grad_tokens_time.astype(FLOAT)).astype(BHALF)
    summed = (
        lax.psum_scatter(time_gain_grad, "seq", scatter_dimension=0, tiled=True),
        lax.psum_scatter(time_in_grad, "seq", scatter_dimension=0, tiled=True),
        lax.psum_scatter(time_out_grad, "seq", scatter_dimension=1, tiled=True),
        lax.psum_scatter(linear_grad, "seq", scatter_dimension=0, tiled=True),
        lax.psum_scatter(space_gain_grad, "seq", scatter_dimension=0, tiled=True),
        lax.psum_scatter(space_in_grad, "seq", scatter_dimension=0, tiled=True),
        lax.psum_scatter(space_out_grad, "seq", scatter_dimension=1, tiled=True),
        lax.psum_scatter(mlp_gain_grad, "seq", scatter_dimension=0, tiled=True),
        lax.psum_scatter(up_grad, "seq", scatter_dimension=0, tiled=True),
        lax.psum_scatter(down_grad, "seq", scatter_dimension=1, tiled=True),
        lax.psum_scatter(cls_in_part, "seq", scatter_dimension=1, tiled=True),
    )
    shifts = lax.psum(
        (
            time_beta_grad,
            time_pair_grad,
            time_shift_grad,
            linear_shift_grad,
            space_beta_grad,
            space_pair_grad,
            space_shift_grad,
            mlp_beta_grad,
            up_shift_grad,
            down_shift_grad,
        ),
        "seq",
    )
    col_width = model_width // seq_count
    cls_direct = lax.dynamic_slice_in_dim(grad_cls_mid, seq_rank * col_width, col_width, 1)
    cls_tokens_grad = summed[10] + cls_direct
    return (
        block_out,
        cls_out,
        tokens_grad,
        cls_tokens_grad,
        summed[0],
        shifts[0],
        summed[1],
        shifts[1],
        summed[2],
        shifts[2],
        summed[3],
        shifts[3],
        summed[4],
        shifts[4],
        summed[5],
        shifts[5],
        summed[6],
        shifts[6],
        summed[7],
        shifts[7],
        summed[8],
        shifts[8],
        summed[9],
        shifts[9],
    )


MESH = pl.DeviceIdType.MESH
ROWS = 208
HALF = 16
SLOTS = 2 * HALF


def dot_nn(left, right):
    return jnp.dot(left, right, preferred_element_type=FLOAT)


def dot_nt(left, right):
    return lax.dot_general(left, right, (((1,), (1,)), ((), ())), preferred_element_type=FLOAT)


def dot_tn(left, right):
    return lax.dot_general(left, right, (((0,), (0,)), ((), ())), preferred_element_type=FLOAT)


def iota(shape, axis):
    return lax.broadcasted_iota(jnp.int32, shape, axis)


def scratch_shapes(dims):
    frames, seq, width, model, hidden = dims["frames"], dims["seq"], dims["width"], dims["model"], dims["hidden"]
    rows, every, heads = frames * ROWS, frames * seq, width // HEAD_DIM
    half, low = model // 2, BHALF
    vm = pltpu.VMEM
    shapes = dict(
        tok=vm((dims["patches"], frames, model), low),
        out_grad=vm((dims["patches"], frames, model), low),
        w_ti=vm((3 * width, model), low),
        w_si=vm((3 * width, model), low),
        w_tl=vm((model, model), low),
        w_up=vm((model, hidden), low),
        w_dn=vm((hidden, model), low),
        w_to=vm((2, 2, width, model), low),
        w_so=vm((2, 2, width, model), low),
        x32=vm((rows, model), FLOAT),
        gr32=vm((rows, model), FLOAT),
        t32=vm((rows, model), FLOAT),
        u32=vm((rows, model), FLOAT),
        dact=vm((rows, hidden), FLOAT),
        xh_t=vm((rows, model), FLOAT),
        xh_s=vm((rows, model), FLOAT),
        xh_m=vm((rows, model), FLOAT),
        inv=vm((3, rows, 128), FLOAT),
        n_t=vm((rows, model), low),
        n_s=vm((rows, model), low),
        n_m=vm((rows, model), low),
        gr16=vm((rows, model), low),
        mid16=vm((rows, model), low),
        act=vm((rows, hidden), low),
        act_k=vm((rows, hidden), low),
        gpre=vm((rows, hidden), low),
        gpre_k=vm((rows, hidden), low),
        gss=vm((rows, model), low),
        gtr=vm((rows, model), low),
        gtm=vm((rows, model), low),
        sqkv=vm((rows, 3 * width), low),
        dsq=vm((rows, 3 * width), low),
        dtq=vm((rows, 3 * width), low),
        gatt=vm((rows, width), low),
        sel=vm((seq * SLOTS, ROWS), low),
        les=vm((ROWS, seq * SLOTS), low),
        tmask=vm((every * HALF, every * HALF), FLOAT),
        p_t=vm((2 * heads, every * HALF, every * HALF), FLOAT),
        p_s=vm((frames * heads, ROWS, ROWS), FLOAT),
        q_send=vm((frames, seq, 2, HALF, 3 * width), low),
        q_pos=vm((2, every, HALF, 3 * width), low),
        a_pos=vm((2, every, HALF, width), low),
        a_recv=vm((2, seq, frames, HALF, width), low),
        g_send=vm((frames, seq, 2, HALF, width), low),
        g_pos=vm((2, every, HALF, width), low),
        d_pos=vm((2, every, HALF, 3 * width), low),
        d_recv=vm((2, seq, frames, HALF, 3 * width), low),
        att_t=vm((2, 2, rows, width), low),
        att_s=vm((2, 2, rows, width), low),
        part=vm((4, 2, rows, half), low),
        pair=vm((4, rows, half), low),
        other=vm((4, rows, half), low),
        total=vm((4, 2, rows, half), low),
        cls_send=vm((8, model), FLOAT),
        cls_recv=vm((seq, 8, model), FLOAT),
        gcm=vm((8, model), FLOAT),
        v_send=vm((3, 8, model), FLOAT),
        v_recv=vm((3, seq, 8, model), FLOAT),
        v_head=vm((4, 8, model), FLOAT),
    )
    for name, columns in grad_columns(dims):
        share = model // seq
        shapes["g_" + name] = vm((seq // 4, 2, 2, share, columns), low)
        shapes["y_" + name] = vm((2, seq // 4, share, columns), low)
        shapes["z_" + name] = vm((seq // 4, share, columns), low)
        shapes["x_" + name] = vm((share, columns), low)
    for name in VECTORS:
        shapes[name] = vm((hidden if name == "m_ub" else model,), FLOAT)
    for name in PAIRS:
        shapes[name] = vm((2, width), FLOAT)
    shapes["load"] = pltpu.SemaphoreType.DMA((32,))
    shapes["sent"] = pltpu.SemaphoreType.DMA((280,))
    shapes["got"] = pltpu.SemaphoreType.DMA((280,))
    return shapes


def grad_columns(dims):
    width, model, hidden = dims["width"], dims["model"], dims["hidden"]
    return (
        ("dn", hidden),
        ("up", hidden),
        ("s", 4 * width),
        ("l", 2 * width),
        ("ta", 2 * width),
        ("tb", width),
    )


VECTORS = ("t_gain", "t_beta", "t_ob", "t_lb", "s_gain", "s_beta", "s_ob", "m_gain", "m_beta", "m_db", "m_ub")
PAIRS = ("t_qv", "s_qv")
MATRICES = ("tok", "out_grad", "w_ti", "w_to", "w_tl", "w_si", "w_so", "w_up", "w_dn")
INPUTS = ("lens", "cls", "cls_grad") + tuple("h_" + name for name in VECTORS + PAIRS + MATRICES)
OUTPUTS = ("o_blk", "o_cls", "o_tok", "o_vec")


class Refs:
    pass


class Exchange:
    def __init__(self, out, into):
        self.wait_send, self.wait_recv = out.wait_send, into.wait_recv


def layer_kernel(dims, names, *refs):
    k = Refs()
    for name, ref in zip(names, refs):
        setattr(k, name, ref)
    frames, seq, width, model, hidden = dims["frames"], dims["seq"], dims["width"], dims["model"], dims["hidden"]
    patches, clips, pos = dims["patches"], dims["clips"], dims["pos"]
    rows, every, heads, half = frames * ROWS, frames * seq, width // HEAD_DIM, model // 2
    zs = seq // 2
    share_rows = model // seq
    scale = HEAD_DIM ** (-0.5)
    s, h = lax.axis_index("seq"), lax.axis_index("head")
    z, y = s // 2, s % 2
    x, c = h // 2, h % 2
    other_c = 1 - c
    sister, across, diagonal = (s, x * 2 + other_c), (s, (1 - x) * 2 + c), (s, (1 - x) * 2 + other_c)
    y_peer = (z * 2 + 1 - y, h)
    peers = [((z + i) % zs) * 2 + (y + j) % 2 for i in range(zs) for j in range(2) if i or j]
    givers = [((z + zs - i) % zs) * 2 + (y + j) % 2 for i in range(zs) for j in range(2) if i or j]
    used = [0]

    def send(src, dst, device, lands):
        index = used[0]
        used[0] += 1
        sems = dict(send_sem=k.sent.at[index], recv_sem=k.got.at[index], device_id=device, device_id_type=MESH)
        copy = pltpu.make_async_remote_copy(src_ref=src, dst_ref=dst, **sems)
        copy.start()
        copy = Exchange(copy, pltpu.make_async_remote_copy(src_ref=src, dst_ref=lands, **sems))
        unsent.append(copy)
        return copy

    unsent = []
    loads = [0]

    def load(src, dst):
        copy = pltpu.make_async_copy(src, dst, k.load.at[loads[0]])
        loads[0] += 1
        copy.start()
        return copy

    places = {"w_to": k.w_to.at[0, c], "w_so": k.w_so.at[0, c]}
    order = ("tok", "t_gain", "t_beta", "w_ti", "t_qv", "w_to", "w_so", "out_grad", "w_dn") + VECTORS[2:] + ("s_qv", "w_tl", "w_si", "w_up")
    loading = {name: load(getattr(k, "h_" + name), places.get(name, getattr(k, name))) for name in order}

    def need(*wanted):
        for name in wanted:
            loading.pop(name).wait()

    barrier = pltpu.get_barrier_semaphore()
    everyone = [(p, h) for p in peers] + [sister, across, diagonal]
    for device in everyone:
        pl.semaphore_signal(barrier, inc=1, device_id=device, device_id_type=MESH)

    def vec(name):
        if name in loading:
            need(name)
        return getattr(k, name)[...].reshape(1, -1)

    def qkv_row(name):
        need(name)
        pair = getattr(k, name)
        return jnp.concatenate([pair[0:1, :], jnp.zeros((1, width), FLOAT), pair[1:2, :]], axis=-1)

    def chosen(slot, row, outer):
        if outer:
            device, place = slot // SLOTS, slot % SLOTS
        else:
            device, place = slot // HALF % seq, slot // (HALF * seq) * HALF + slot % HALF
        hit = (device * pos + place == row) & (place < pos) & (row < patches)
        return jnp.where(hit, 1.0, 0.0).astype(BHALF)

    k.sel[...] = chosen(iota((seq * SLOTS, ROWS), 0), iota((seq * SLOTS, ROWS), 1), True)
    ends = []
    for i in range(clips):
        ends.append(k.lens[i] + (ends[-1] if i else 0))

    def clip_of(frame):
        total = (frame >= ends[0]).astype(jnp.int32)
        for end in ends[1:]:
            total = total + (frame >= end).astype(jnp.int32)
        return total

    onehot = []
    for f in range(frames):
        own = clip_of(jnp.full((1, model), s * frames + f, jnp.int32))
        onehot.append([(own == i).astype(FLOAT) for i in range(clips)])
    per_len = [1.0 / jnp.full((1, model), k.lens[i], jnp.int32).astype(FLOAT) for i in range(clips)]
    cls32 = k.cls[...].astype(FLOAT)
    cls_row = [sum(onehot[f][i] * cls32[i : i + 1] for i in range(clips)) for f in range(frames)]
    tail = ROWS - patches

    def set_tail(ref, f, first):
        used_rows = sum(r.shape[0] for r in first)
        fill = [jnp.zeros((tail - used_rows, model), FLOAT)] if used_rows < tail else []
        ref[f * ROWS + patches : (f + 1) * ROWS, :] = jnp.concatenate(list(first) + fill, axis=0)

    def eight(values):
        missing = 8 - sum(v.shape[0] for v in values)
        fill = [jnp.zeros((missing, model), FLOAT)] if missing else []
        return jnp.concatenate(list(values) + fill, axis=0)

    def frame(f):
        return slice(f * ROWS, (f + 1) * ROWS)

    def norm(src, which, gain, shift, xhat, out, r):
        v = src[r, :]
        center = v - jnp.mean(v, axis=-1, keepdims=True)
        invstd = lax.rsqrt(jnp.mean(center * center, axis=-1, keepdims=True) + EPS)
        n = center * invstd
        xhat[r, :] = n
        k.inv[which, r, :] = jnp.broadcast_to(invstd, (v.shape[0], 128))
        out[r, :] = (n * gain + shift).astype(BHALF)

    def arrived(copies):
        for copy in copies:
            copy.wait_recv()

    def scatter(f, value, src, dst):
        moved = dot_nn(k.sel[...], value).astype(BHALF)
        src[f] = moved.reshape(seq, 2, HALF, value.shape[-1])
        to = frames * s + f
        copies = [
            [send(src.at[f, p, b], dst.at[b, to], (p, h), dst.at[b, frames * q + f]) for p, q in zip(peers, givers)]
            for b in range(2)
        ]
        dst[:, to] = src[f, s]
        return copies

    def gather(b, src, dst):
        copies = [
            send(src.at[b, pl.ds(frames * p, frames)], dst.at[b, s], (p, h), dst.at[b, q]) for p, q in zip(peers, givers)
        ]
        dst[b, s] = src[b, pl.ds(frames * s, frames)]
        return copies

    def gathered(f, src):
        return dot_nn(k.les[...], src[:, :, f].reshape(seq * SLOTS, src.shape[-1])).astype(BHALF)

    need("tok")
    t_gain, t_beta, t_qb = vec("t_gain"), vec("t_beta"), qkv_row("t_qv")
    q_copies = []
    for f in range(frames):
        k.x32[f * ROWS : f * ROWS + patches, :] = k.tok[:, f, :].astype(FLOAT)
        set_tail(k.x32, f, [])
        norm(k.x32, 0, t_gain, t_beta, k.xh_t, k.n_t, frame(f))
        if f == 0:
            need("w_ti")
        qkv = (dot_nt(k.n_t[frame(f), :], k.w_ti[...]) + t_qb).astype(BHALF)
        if f == 0:
            pl.semaphore_wait(barrier, len(everyone))
        q_copies.append(scatter(f, qkv, k.q_send, k.q_pos))

    def share(ref):
        return (
            send(ref.at[0, c], ref.at[0, c], sister, ref.at[0, other_c]),
            send(ref.at[0, c], ref.at[1, c], across, ref.at[1, c]),
        )

    def pass_on(ref):
        return send(ref.at[1, c], ref.at[1, c], sister, ref.at[1, other_c])

    need("w_to", "w_so")
    w_to_near, w_to_far = share(k.w_to)
    w_so_near, w_so_far = share(k.w_so)

    k.les[...] = chosen(iota((ROWS, seq * SLOTS), 1), iota((ROWS, seq * SLOTS), 0), False)
    span = every * HALF
    left, right = iota((span, span), 0), iota((span, span), 1)
    same = (left % HALF == right % HALF) & (clip_of(left // HALF) == clip_of(right // HALF))
    near = jnp.abs(left // HALF - right // HALF) < MAXLEN
    k.tmask[...] = jnp.where(same & near, 0.0, NEG)
    need("out_grad")
    cls_g = k.cls_grad[...].astype(FLOAT)
    for f in range(frames):
        k.gr32[f * ROWS : f * ROWS + patches, :] = k.out_grad[:, f, :].astype(FLOAT)
        set_tail(k.gr32, f, [cls_g] if f == 0 else [])
        k.gr16[frame(f), :] = k.gr32[frame(f), :].astype(BHALF)
    need("w_dn")
    k.dact[...] = dot_nt(k.gr16[...], k.w_dn[...])
    w_to_far.wait_recv()
    w_to_last = pass_on(k.w_to)
    w_so_far.wait_recv()
    w_so_last = pass_on(k.w_so)

    def attend(q, key, value, mask, p_ref):
        scores = dot_nt(q, key) * scale + mask
        e = jnp.exp(scores - jnp.max(scores, axis=-1, keepdims=True))
        p = e * (1.0 / jnp.sum(e, axis=-1, keepdims=True))
        p_ref[...] = p
        return dot_nn(p.astype(BHALF), value).astype(BHALF)

    def attend_back(q, key, value, grad, p_ref):
        p = p_ref[...]
        grad_p = p * dot_nt(grad, value)
        grad_s = (grad_p - p * jnp.sum(grad_p, axis=-1, keepdims=True)).astype(BHALF)
        grad_q = (dot_nn(grad_s, key) * scale).astype(BHALF)
        grad_k = (dot_tn(grad_s, q) * scale).astype(BHALF)
        grad_v = dot_tn(p.astype(BHALF), grad).astype(BHALF)
        return grad_q, grad_k, grad_v

    def head_of(value, part, j):
        at = part * width + j * HEAD_DIM
        return value[:, at : at + HEAD_DIM]

    def attend_all(qkv, mask, p_ref, first):
        out = [
            attend(*[head_of(qkv, i, j) for i in range(3)], mask, p_ref.at[first + j]) for j in range(heads)
        ]
        return jnp.concatenate(out, axis=-1)

    def attend_back_all(qkv, grad, p_ref, first):
        out = [
            attend_back(*[head_of(qkv, i, j) for i in range(3)], head_of(grad, 0, j), p_ref.at[first + j])
            for j in range(heads)
        ]
        return jnp.concatenate([out[j][i] for i in range(3) for j in range(heads)], axis=-1)

    a_copies = []
    for b in range(2):
        for copies in q_copies:
            arrived(copies[b])
        out = attend_all(k.q_pos[b].reshape(span, 3 * width), k.tmask[...], k.p_t, b * heads)
        k.a_pos[b] = out.reshape(every, HALF, width)
        a_copies += gather(b, k.a_pos, k.a_recv)
    arrived(a_copies)

    def features(f, att):
        r = frame(f)
        return (
            send(att.at[0, c, r], att.at[0, c, r], sister, att.at[0, other_c, r]),
            send(att.at[0, c, r], att.at[1, c, r], across, att.at[1, c, r]),
        )

    def own_part(f, att, weight, copies):
        r = frame(f)
        copies[0].wait_recv()
        k.t32[r, :] = dot_nn(att[0, 0, r], weight[0, 0]) + dot_nn(att[0, 1, r], weight[0, 1])

    def features_on(f, att, copies):
        copies[1].wait_recv()
        r = frame(f)
        return send(att.at[1, c, r], att.at[1, c, r], sister, att.at[1, other_c, r])

    def both_parts(f, att, weight, copy):
        r = frame(f)
        copy.wait_recv()
        k.u32[r, :] = dot_nn(att[1, 0, r], weight[1, 0]) + dot_nn(att[1, 1, r], weight[1, 1])
        own, other = k.t32[r, :], k.u32[r, :]
        return jnp.where(x == 0, own, other) + jnp.where(x == 0, other, own)

    ta_copies = []
    for f in range(frames):
        k.att_t[0, c, frame(f), :] = gathered(f, k.a_recv)
        ta_copies.append(features(f, k.att_t))
    arrived([w_to_near, w_to_last])
    t_ob, t_lb, s_gain, s_beta, s_qb = vec("t_ob"), vec("t_lb"), vec("s_gain"), vec("s_beta"), qkv_row("s_qv")
    need("w_tl", "w_si")
    in_frame = jnp.where(iota((1, ROWS), 1) < patches + 1, 0.0, NEG)
    for f in range(frames):
        own_part(f, k.att_t, k.w_to, ta_copies[f])
    ta_last, sa_copies = [], []
    for f in range(frames):
        ta_last.append(features_on(f, k.att_t, ta_copies[f]))
    for f in range(frames):
        r = frame(f)
        k.mid16[r, :] = (both_parts(f, k.att_t, k.w_to, ta_last[f]) + t_ob).astype(BHALF)
        res = (dot_nn(k.mid16[r, :], k.w_tl[...]) + t_lb).astype(BHALF)
        k.x32[r, :] = k.x32[r, :] + res.astype(FLOAT)
        set_tail(k.x32, f, [cls_row[f]])
        norm(k.x32, 1, s_gain, s_beta, k.xh_s, k.n_s, r)
        k.sqkv[r, :] = (dot_nt(k.n_s[r, :], k.w_si[...]) + s_qb).astype(BHALF)
        k.att_s[0, c, r, :] = attend_all(k.sqkv[r, :], in_frame, k.p_s, f * heads)
        sa_copies.append(features(f, k.att_s))
    arrived([w_so_near, w_so_last])
    s_ob, m_gain, m_beta = vec("s_ob"), vec("m_gain"), vec("m_beta")
    for f in range(frames):
        own_part(f, k.att_s, k.w_so, sa_copies[f])
    sa_last = []
    for f in range(frames):
        sa_last.append(features_on(f, k.att_s, sa_copies[f]))
    cls_at = [slice(f * ROWS + patches, f * ROWS + patches + 1) for f in range(frames)]
    space_cls = []
    for f in range(frames):
        r = frame(f)
        k.t32[r, :] = both_parts(f, k.att_s, k.w_so, sa_last[f]) + s_ob
        space_cls.append(k.t32[cls_at[f], :])
        k.x32[r, :] = k.x32[r, :] + k.t32[r, :]
        set_tail(k.x32, f, [])
    parts = [sum(onehot[f][i] * space_cls[f] for f in range(frames)) for i in range(clips)]
    k.cls_send[...] = eight(parts)
    cls_copies = [send(k.cls_send, k.cls_recv.at[s], (p, h), k.cls_recv.at[q]) for p, q in zip(peers, givers)]
    k.cls_recv[s] = k.cls_send[...]

    first_seq = jnp.where(s == 0, 1.0, 0.0)
    m_ub = vec("m_ub")
    need("w_up")

    def up_rows(r):
        norm(k.x32, 2, m_gain, m_beta, k.xh_m, k.n_m, r)
        k.t32[r, :] = dot_nn(k.n_m[r, :], k.w_up[...])

    def kept(r):
        at = r.start + iota((r.stop - r.start, 1), 0)
        return jnp.where((at >= patches) & (at < ROWS), first_seq, 1.0)

    def gelu_rows(r):
        pre = k.t32[r, :] + m_ub
        cdf = 0.5 * (1.0 + lax.erf(pre * 0.7071067811865476))
        slope = cdf + pre * jnp.exp(-0.5 * pre * pre) * 0.3989422804014327
        act = pre * cdf
        grad = k.dact[r, :] * slope
        k.act[r, :] = act.astype(BHALF)
        k.gpre[r, :] = grad.astype(BHALF)
        if r.start == 0:
            act, grad = act * kept(r), grad * kept(r)
        k.act_k[r, :] = act.astype(BHALF)
        k.gpre_k[r, :] = grad.astype(BHALF)

    def sum_open(i, f, lhs, rhs, dot):
        r = frame(f)
        for b in range(2):
            cut = slice(b * half, (b + 1) * half)
            k.part[i, b, r, :] = dot(lhs[r, :], rhs[cut, :] if dot is dot_nt else rhs[:, cut]).astype(BHALF)
        return send(k.part.at[i, other_c, r], k.pair.at[i, r], sister, k.pair.at[i, r])

    def sum_across(i, f, copy):
        r = frame(f)
        copy.wait_recv()
        k.part[i, c, r, :] = (k.part[i, c, r, :].astype(FLOAT) + k.pair[i, r, :].astype(FLOAT)).astype(BHALF)
        return send(k.part.at[i, c, r], k.other.at[i, r], across, k.other.at[i, r])

    def sum_close(i, f, copy):
        r = frame(f)
        copy.wait_recv()
        k.total[i, c, r, :] = (k.part[i, c, r, :].astype(FLOAT) + k.other[i, r, :].astype(FLOAT)).astype(BHALF)
        return send(k.total.at[i, c, r], k.total.at[i, c, r], sister, k.total.at[i, other_c, r])

    def rows_of(ref, i, r):
        return jnp.concatenate([ref[i, 0, r, :], ref[i, 1, r, :]], axis=-1).astype(FLOAT)

    z_hi, z_lo = z // 2, z % 2
    z_near, z_far = ((z + 1 - 2 * z_lo) * 2 + y, h), (((z + 2) % zs) * 2 + y, h)
    z_first = ("up", "l", "tb")

    def grad_make(name, *pairs):
        g = getattr(k, "g_" + name)
        parts = [dot_tn(lhs, rhs).astype(BHALF) for lhs, rhs in pairs]
        value = parts[0] if len(parts) == 1 else jnp.concatenate(parts, axis=-1)
        g[...] = value.reshape(g.shape)

    class Reduction:
        def __init__(self, name):
            self.name, self.g = name, getattr(k, "g_" + name)
            self.first, self.second, self.third = [getattr(k, kind + name) for kind in ("y_", "z_", "x_")]
            ways = [(y, y_peer), (z_lo, z_near)]
            (self.one, self.peer_one), (self.two, self.peer_two) = ways[::-1] if name in z_first else ways

        def at(self, one, two):
            return (slice(None), one, two) if self.name in z_first else (slice(None), two, one)

        def add(self, at, got):
            self.g[at] = (self.g[at].astype(FLOAT) + got.astype(FLOAT)).astype(BHALF)

    def grad_open(name):
        job = Reduction(name)
        job.copies = []
        for two in (1 - job.two, job.two):
            into = job.first.at[two]
            job.copies.append(send(job.g.at[job.at(1 - job.one, two)], into, job.peer_one, into))
        return job

    def grad_near(job):
        job.copies[0].wait_recv()
        away, kept_here = job.at(job.one, 1 - job.two), job.at(job.one, job.two)
        job.add(away, job.first[1 - job.two])
        copy = send(job.g.at[away], job.second, job.peer_two, job.second)
        job.copies[1].wait_recv()
        job.add(kept_here, job.first[job.two])
        job.copies = [copy]
        return job

    def grad_far(job):
        job.copies[0].wait_recv()
        job.add(job.at(job.one, job.two), job.second[...])
        job.copies = [send(job.g.at[1 - z_hi, z_lo, y], job.third, z_far, job.third)]
        return job

    def grad_close(job):
        job.copies[0].wait_recv()
        getattr(k, "o_" + job.name)[...] = job.g[z_hi, z_lo, y].astype(FLOAT) + job.third[...].astype(FLOAT)

    def vectors_send(which, values):
        value = eight(values)
        k.v_send[which] = value
        k.v_recv[which, s] = value
        into = k.v_recv.at[which]
        return [send(k.v_send.at[which], into.at[s], (p, h), into.at[q]) for p, q in zip(peers, givers)]

    def vectors_close(which, copies):
        arrived(copies)
        value = k.v_recv[which, 0]
        for i in range(1, seq):
            value = value + k.v_recv[which, i]
        return value

    ones = jnp.ones((8, rows), BHALF)
    at = iota((8, rows), 1)
    ones_kept = jnp.where((at >= patches) & (at < ROWS), first_seq, 1.0).astype(BHALF)

    def col_sums(ref, weights=None):
        out = dot_nn(ones if weights is None else weights, ref[...])[0:1]
        if out.shape[1] < model:
            out = jnp.concatenate([out, jnp.zeros((1, model - out.shape[1]), FLOAT)], axis=-1)
        return out

    def column_sum(v):
        return jnp.sum(v, axis=0, keepdims=True)

    def add_all(lists):
        return [sum(v) for v in zip(*lists)]

    def norm_back(i, which, gain, xhat, r, keep):
        g = rows_of(k.total, i, r)
        n = xhat[r, :]
        gh = g * gain
        m1 = jnp.mean(gh, axis=-1, keepdims=True)
        m2 = jnp.mean(gh * n, axis=-1, keepdims=True)
        dx = k.inv[which, r, 0:1] * (gh - m1 - n * m2)
        w = g * kept(r) if keep and r.start == 0 else g
        return dx, (column_sum(w * n), column_sum(w))

    m_sum = [None] * frames
    for f in range(1, frames):
        up_rows(frame(f))
        gelu_rows(frame(f))
        m_sum[f] = sum_open(0, f, k.gpre, k.w_up, dot_nt)
    up_rows(frame(0))
    for f in range(1, frames):
        m_sum[f] = sum_across(0, f, m_sum[f])
    arrived(cls_copies)
    cls_sum = k.cls_recv[0]
    for i in range(1, seq):
        cls_sum = cls_sum + k.cls_recv[i]
    set_tail(k.x32, 0, [cls32[i : i + 1] + cls_sum[i : i + 1] * per_len[i] for i in range(clips)])
    up_rows(slice(ROWS - HALF, ROWS))
    gelu_rows(frame(0))
    m_sum[0] = sum_open(0, 0, k.gpre, k.w_up, dot_nt)
    o_sum = [sum_open(1, f, k.act, k.w_dn, dot_nn) for f in range(frames)]
    m_sum[0] = sum_across(0, 0, m_sum[0])
    grad_make("dn", (k.gr16[...], k.act_k[...]))
    j_dn = grad_open("dn")
    grad_make("up", (k.n_m[...], k.gpre_k[...]))
    j_up = grad_open("up")
    ub_grad, db_grad = col_sums(k.gpre_k), col_sums(k.gr16, ones_kept)
    m_last, sums = [None] * frames, [None] * frames
    backwards = list(range(1, frames)) + [0]
    for f in backwards:
        m_last[f] = sum_close(0, f, m_sum[f])
    for f in backwards:
        m_last[f].wait_recv()
        dx, sums[f] = norm_back(0, 2, m_gain, k.xh_m, frame(f), True)
        k.gr32[frame(f), :] = k.gr32[frame(f), :] + dx
    grad_cls_mid = k.gr32[patches : patches + clips, :]
    k.gcm[...] = eight([grad_cls_mid])
    shares = [
        sum(onehot[f][i] * (grad_cls_mid[i : i + 1] * per_len[i]) for i in range(clips)) for f in range(frames)
    ]

    def space_back(f):
        r = frame(f)
        set_tail(k.gr32, f, [shares[f]])
        k.gss[r, :] = k.gr32[r, :].astype(BHALF)
        set_tail(k.gr32, f, [])
        grad = dot_nt(k.gss[r, :], k.w_so[0, c]).astype(BHALF)
        k.dsq[r, :] = attend_back_all(k.sqkv[r, :], grad, k.p_s, f * heads)
        return sum_open(2, f, k.dsq, k.w_si, dot_nn)

    s_sum = []
    for f in range(frames):
        s_sum.append(space_back(f))
        if f:
            s_sum[f - 1] = sum_across(2, f - 1, s_sum[f - 1])
    m_rows = add_all(sums) + [ub_grad, db_grad]
    s_sum[-1] = sum_across(2, frames - 1, s_sum[-1])
    j_dn = grad_near(j_dn)
    j_up = grad_near(j_up)
    v_m = vectors_send(0, m_rows)
    grad_make("s", (k.n_s[...], k.dsq[...]), (k.gss[...], k.att_s[0, c]))
    j_s = grad_open("s")
    s_rows = [col_sums(k.gss), col_sums(k.dsq)]
    s_last = [sum_close(2, f, s_sum[f]) for f in range(frames)]

    g_copies, cls_in = [], []
    for f in range(frames):
        r = frame(f)
        s_last[f].wait_recv()
        dx, sums[f] = norm_back(2, 1, s_gain, k.xh_s, r, False)
        k.gr32[r, :] = k.gr32[r, :] + dx
        cls_in.append(k.gr32[cls_at[f], :])
        set_tail(k.gr32, f, [])
        k.gtr[r, :] = k.gr32[r, :].astype(BHALF)
        k.gtm[r, :] = dot_nt(k.gtr[r, :], k.w_tl[...]).astype(BHALF)
        grad = dot_nt(k.gtm[r, :], k.w_to[0, c]).astype(BHALF)
        g_copies.append(scatter(f, grad, k.g_send, k.g_pos))
    o_sum = [sum_across(1, f, o_sum[f]) for f in range(frames)]
    j_dn = grad_far(j_dn)
    j_up = grad_far(j_up)
    pick = (iota((model, width), 0) == h * width + iota((model, width), 1)).astype(FLOAT).astype(BHALF)
    grad_make("l", (k.mid16[...], dot_nn(k.gtr[...], pick).astype(BHALF)), (k.gtm[...], k.att_t[0, c]))
    j_l = grad_open("l")
    d_copies = []
    for b in range(2):
        for copies in g_copies:
            arrived(copies[b])
            value = attend_back_all(
            k.q_pos[b].reshape(span, 3 * width), k.g_pos[b].reshape(span, width), k.p_t, b * heads
        )
        k.d_pos[b] = value.reshape(every, HALF, 3 * width)
        d_copies += gather(b, k.d_pos, k.d_recv)
    j_s = grad_near(j_s)
    cls_parts = [sum(onehot[f][i] * cls_in[f] for f in range(frames)) for i in range(clips)]
    v_s = vectors_send(1, add_all(sums) + s_rows + cls_parts)
    t_rows = [col_sums(k.gtm), col_sums(k.gtr)]
    o_last = [sum_close(1, f, o_sum[f]) for f in range(frames)]
    m_vec = vectors_close(0, v_m)
    k.o_vec[0:8, :] = m_vec
    m_db = vec("m_db")
    for f in range(frames):
        r = frame(f)
        o_last[f].wait_recv()
        out = k.x32[r, :] + rows_of(k.total, 1, r) + m_db
        k.o_blk[:, f, :] = out[:patches].astype(BHALF)
        if f == 0:
            k.o_cls[...] = out[patches : patches + clips].astype(BHALF)
    grad_close(j_dn)
    grad_close(j_up)
    j_l = grad_near(j_l)
    arrived(d_copies)
    t_sum, shared = [], []
    for f in range(frames):
        k.dtq[frame(f), :] = gathered(f, k.d_recv)
        t_sum.append(sum_open(3, f, k.dtq, k.w_ti, dot_nn))
    grad_make("ta", (k.n_t[...], k.dtq[:, : 2 * width]))
    j_ta = grad_open("ta")
    for f in range(frames):
        g = rows_of(k.part, 3, frame(f))
        shared.append((column_sum(g * k.xh_t[frame(f), :]), column_sum(g)))
        t_sum[f] = sum_across(3, f, t_sum[f])
    grad_make("tb", (k.n_t[...], k.dtq[:, 2 * width :]))
    j_tb = grad_open("tb")
    v_t = vectors_send(2, add_all(shared) + [t_rows[0], col_sums(k.dtq), t_rows[1]])
    j_s = grad_far(j_s)
    s_vec = vectors_close(1, v_s)
    k.o_vec[8:16, :] = s_vec + jnp.concatenate([jnp.zeros((4, model), FLOAT), k.gcm[0:4, :]], axis=0)
    j_l = grad_far(j_l)
    j_ta = grad_near(j_ta)
    t_last = [sum_close(3, 0, t_sum[0])]
    t_vec = vectors_close(2, v_t)
    k.v_head[h] = t_vec
    h_copies = [send(k.v_head.at[h], k.v_head.at[h], d, k.v_head.at[d[1]]) for d in (sister, across, diagonal)]
    t_last += [sum_close(3, f, t_sum[f]) for f in range(1, frames)]
    for f in range(frames):
        r = frame(f)
        t_last[f].wait_recv()
        if f == 0:
            j_tb = grad_near(j_tb)
        dx, _ = norm_back(3, 0, t_gain, k.xh_t, r, False)
        out = k.gr32[r, :] + dx.astype(BHALF).astype(FLOAT)
        k.o_tok[:, f, :] = out[:patches].astype(BHALF)
    j_ta = grad_far(j_ta)
    grad_close(j_s)
    arrived(h_copies)
    over_head = k.v_head[0] + k.v_head[1] + k.v_head[2] + k.v_head[3]
    k.o_vec[16:24, :] = jnp.concatenate([over_head[0:2], t_vec[2:8]], axis=0)
    j_tb = grad_far(j_tb)
    grad_close(j_l)
    grad_close(j_ta)
    grad_close(j_tb)
    for copy in unsent:
        copy.wait_send()


def finish_kernel(dims, h_blk, h_tok, vec, cls_out, g_dn, g_up, g_s, g_l, g_ta, g_tb, *refs):
    width, model, seq = dims["width"], dims["model"], dims["seq"]
    share, clips = model // seq, dims["clips"]
    o_blk, o_cls, o_tok, cls, tg, tb, ti, tp, to, tob, tl, tlb, sg, sb, si, sp, so, sob, mg, mb, up, ub, dn, db = refs
    o_blk[...] = h_blk[...]
    o_tok[...] = h_tok[...]
    s = lax.axis_index("seq")
    v = vec[...]
    mine = pltpu.roll(v, (model - share * s) % model, 1)[:, :share]
    for out, row in ((mg, 0), (sg, 8), (tg, 16)):
        out[...] = mine[row : row + 1].reshape(share)
    for out, row in ((mb, 1), (ub, 2), (db, 3), (sb, 9), (sob, 10), (tb, 17), (tob, 18), (tlb, 20)):
        out[...] = v[row : row + 1].reshape(model)
    cls[...] = mine[12 : 12 + clips]
    o_cls[...] = cls_out[...]
    for out, row in ((sp, 11), (tp, 19)):
        out[0:1, :] = v[row : row + 1, :width]
        out[1:2, :] = v[row : row + 1, 2 * width : 3 * width]
    for i in range(3):
        si[i] = g_s[:, i * width : (i + 1) * width]
    ti[0], ti[1], ti[2] = g_ta[:, :width], g_ta[:, width:], g_tb[...]
    tl[...] = g_l[:, :width]
    up[...] = g_up[...]
    dn[...] = g_dn[...]
    to[...] = g_l[:, width:].T
    so[...] = g_s[:, 3 * width :].T


def fused_body(
    tokens,
    cls_tokens,
    clip_lengths,
    time_gain,
    time_beta,
    time_proj_in,
    time_qv_bias,
    time_proj_out,
    time_out_bias,
    time_linear,
    time_linear_bias,
    space_gain,
    space_beta,
    space_proj_in,
    space_qv_bias,
    space_proj_out,
    space_out_bias,
    mlp_gain,
    mlp_beta,
    mlp_up,
    mlp_up_bias,
    mlp_down,
    mlp_down_bias,
    out_grad,
    cls_grad,
):
    frames, patches, model = tokens.shape
    seq = lax.axis_size("seq")
    width, hidden, clips = time_proj_in.shape[2], mlp_up.shape[1], clip_lengths.shape[0]
    dims = dict(
        frames=frames,
        patches=patches,
        model=model,
        seq=seq,
        width=width,
        hidden=hidden,
        clips=clips,
        pos=-(-patches // seq),
    )

    def frames_inner(v):
        return jnp.transpose(v, (1, 0, 2))

    def outputs_first(v):
        return jnp.transpose(v, (1, 2, 0)).reshape(3 * width, model)

    scratch = scratch_shapes(dims)
    grads = grad_columns(dims)
    share = model // seq
    shape = jax.ShapeDtypeStruct
    vmem, anywhere = pl.BlockSpec(memory_space=pltpu.VMEM), pl.BlockSpec(memory_space=pl.ANY)
    inner = (patches, frames, model)
    outs = [
        shape(inner, BHALF),
        shape(cls_tokens.shape, BHALF),
        shape(inner, BHALF),
        shape((24, model), FLOAT),
    ] + [shape((share, columns), FLOAT) for _, columns in grads]
    names = list(INPUTS) + list(OUTPUTS) + ["o_" + name for name, _ in grads] + list(scratch)
    results = pl.pallas_call(
        functools.partial(layer_kernel, dims, names),
        out_shape=outs,
        in_specs=[pl.BlockSpec(memory_space=pltpu.SMEM)] + [vmem] * 2 + [anywhere] * (len(INPUTS) - 3),
        out_specs=[vmem] * len(outs),
        scratch_shapes=list(scratch.values()),
        compiler_params=pltpu.CompilerParams(
            collective_id=0, has_side_effects=True, vmem_limit_bytes=62 * 1024 * 1024
        ),
        name="layer",
    )(
        clip_lengths,
        cls_tokens,
        cls_grad,
        time_gain,
        time_beta,
        time_out_bias,
        time_linear_bias,
        space_gain,
        space_beta,
        space_out_bias,
        mlp_gain,
        mlp_beta,
        mlp_down_bias,
        mlp_up_bias,
        time_qv_bias,
        space_qv_bias,
        frames_inner(tokens),
        frames_inner(out_grad),
        outputs_first(time_proj_in),
        time_proj_out,
        time_linear,
        outputs_first(space_proj_in),
        space_proj_out,
        mlp_up,
        mlp_down,
    )
    blk, cls_out, tok, vectors = results[:4]
    row, gain = shape((model,), FLOAT), shape((share,), FLOAT)
    proj, pair = shape((3, share, width), FLOAT), shape((2, width), FLOAT)
    out_shape = [
        shape(inner, BHALF),
        shape(cls_tokens.shape, BHALF),
        shape(inner, BHALF),
        shape((clips, share), FLOAT),
        gain,
        row,
        proj,
        pair,
        shape((width, share), FLOAT),
        row,
        shape((share, width), FLOAT),
        row,
        gain,
        row,
        proj,
        pair,
        shape((width, share), FLOAT),
        row,
        gain,
        row,
        shape((share, hidden), FLOAT),
        shape((hidden,), FLOAT),
        shape((share, hidden), FLOAT),
        row,
    ]
    last = pl.pallas_call(
        functools.partial(finish_kernel, dims),
        out_shape=out_shape,
        in_specs=[vmem] * 10,
        out_specs=[vmem] * len(out_shape),
        compiler_params=pltpu.CompilerParams(vmem_limit_bytes=62 * 1024 * 1024),
        name="finish",
    )(blk, tok, vectors, cls_out, *results[4:])
    last = list(last)
    for i in (0, 2, 6, 14):
        last[i] = jnp.transpose(last[i], (1, 0, 2))
    last[22] = last[22].T
    return tuple(last)


def solution(mesh):
    placed = (
        P("seq", None, None),
        P(),
        P(),
        P(),
        P(),
        P(None, None, "head"),
        P(None, "head"),
        P("head", None),
        P(),
        P(),
        P(),
        P(),
        P(),
        P(None, None, "head"),
        P(None, "head"),
        P("head", None),
        P(),
        P(),
        P(),
        P(None, "head"),
        P("head"),
        P("head", None),
        P(),
        P("seq", None, None),
        P(),
    )
    fused = mesh.shape["seq"] == 8 and mesh.shape["head"] == 4
    return jax.shard_map(
        fused_body if fused else body,
        mesh=mesh,
        in_specs=placed,
        out_specs=(
            P("seq", None, None),
            P(),
            P("seq", None, None),
            P(None, "seq"),
            P("seq"),
            P(),
            P("seq", None, "head"),
            P(None, "head"),
            P("head", "seq"),
            P(),
            P("seq", "head"),
            P(),
            P("seq"),
            P(),
            P("seq", None, "head"),
            P(None, "head"),
            P("head", "seq"),
            P(),
            P("seq"),
            P(),
            P("seq", "head"),
            P("head"),
            P("head", "seq"),
            P(),
        ),
        check_vma=False,
    )
```

```python
import functools

import jax
import jax.numpy as jnp
from jax import lax
from jax.experimental import pallas as pl
from jax.experimental.pallas import tpu as pltpu
from jax.sharding import PartitionSpec as P

HEAD_DIM = 64
PATCH = 196
MAXLEN = 8


EPS = 1e-06
NEG = -1e30
FLOAT = jnp.float32
BHALF = jnp.bfloat16


def matmul_plain(left, right):
    return jnp.dot(left, right, preferred_element_type=FLOAT)


def matmul_tn(left, right):
    return lax.dot_general(left, right, (((0,), (0,)), ((), ())), preferred_element_type=FLOAT)


def matmul_nt(left, right):
    return lax.dot_general(left, right, (((1,), (1,)), ((), ())), preferred_element_type=FLOAT)


def exact_tn(left, right):
    return lax.dot_general(
        left,
        right,
        (((0,), (0,)), ((), ())),
        precision=lax.Precision.HIGHEST,
        preferred_element_type=FLOAT,
    )


def exact_nn(left, right):
    return jnp.dot(left, right, precision=lax.Precision.HIGHEST, preferred_element_type=FLOAT)


def layer_norm(rows, gain, shift):
    center = rows - jnp.mean(rows, axis=-1, keepdims=True)
    invstd = lax.rsqrt(jnp.mean(center * center, axis=-1, keepdims=True) + EPS)
    normed = center * invstd
    return (normed * gain + shift, normed, invstd)


def norm_back(grad_out, gain, normed, invstd, row_weight):
    feature_count = grad_out.shape[-1]
    grad_norm = grad_out * gain
    weighted = grad_out * row_weight
    gain_grad = jnp.sum((weighted * normed).reshape(-1, feature_count), axis=0)
    shift_grad = jnp.sum(weighted.reshape(-1, feature_count), axis=0)
    first_mean = jnp.mean(grad_norm, axis=-1, keepdims=True)
    second_mean = jnp.mean(grad_norm * normed, axis=-1, keepdims=True)
    return (invstd * (grad_norm - first_mean - normed * second_mean), gain_grad, shift_grad)


def qkv_shift(pair):
    return jnp.stack([pair[0], jnp.zeros_like(pair[0]), pair[1]], axis=0).reshape(-1)


def pair_sums(grad_qkv, local_width):
    sums = jnp.sum(grad_qkv.astype(FLOAT).reshape(-1, 3, local_width), axis=0)
    return jnp.stack([sums[0], sums[2]], axis=0)


def gelu_slope(pre):
    normal_cdf = 0.5 * (1.0 + jax.scipy.special.erf(pre * 0.7071067811865476))
    return normal_cdf + pre * jnp.exp(-0.5 * pre * pre) * 0.3989422804014327


def band_stack(values, band_reach):
    frames = values.shape[0]
    padded = jnp.pad(values, ((band_reach, band_reach),) + ((0, 0),) * (values.ndim - 1))
    return jnp.stack(
        [padded[offset : offset + frames] for offset in range(2 * band_reach + 1)], axis=2
    )


def band_return(contrib, band_reach):
    frames = contrib.shape[0]
    padded = jnp.pad(contrib, ((band_reach, band_reach),) + ((0, 0),) * (contrib.ndim - 1))
    total = jnp.zeros((frames,) + contrib.shape[1:2] + contrib.shape[3:], FLOAT)
    for offset in range(2 * band_reach + 1):
        start = 2 * band_reach - offset
        total = total + padded[start : start + frames, :, offset]
    return total


def to_positions(frame_major):
    frames_dev, patches, columns = frame_major.shape
    seq_count = lax.axis_size("seq")
    pos_dev = (patches + seq_count - 1) // seq_count
    padded = jnp.pad(frame_major, ((0, 0), (0, pos_dev * seq_count - patches), (0, 0)))
    moved = lax.all_to_all(
        padded.reshape(frames_dev, seq_count, pos_dev, columns),
        "seq",
        split_axis=1,
        concat_axis=0,
        tiled=True,
    )
    return moved.reshape(frames_dev * seq_count, pos_dev, columns)


def to_frames(pos_major):
    frames_all, pos_dev, columns = pos_major.shape
    seq_count = lax.axis_size("seq")
    moved = lax.all_to_all(
        pos_major.reshape(frames_all, 1, pos_dev, columns),
        "seq",
        split_axis=0,
        concat_axis=1,
        tiled=True,
    )
    return moved.reshape(frames_all // seq_count, seq_count * pos_dev, columns)[:, :PATCH]


def head_cols(pieces):
    return lax.all_gather(pieces, "head", axis=2, tiled=True)


def time_scores(queries, key_band, valid, score_scale):
    raw = (
        jnp.einsum("fphd,fpohd->fpho", queries, key_band, preferred_element_type=FLOAT)
        * score_scale
    )
    return jnp.where(valid[:, None, None, :], raw, NEG)


def time_forward(queries, key_band, value_band, valid, score_scale):
    scores = time_scores(queries, key_band, valid, score_scale)
    largest = jnp.max(scores, axis=-1, keepdims=True)
    exponent = jnp.exp(scores - largest)
    totals = jnp.sum(exponent, axis=-1, keepdims=True)
    attend = (exponent / totals).astype(BHALF)
    result = jnp.einsum("fpho,fpohd->fphd", attend, value_band, preferred_element_type=FLOAT)
    return (result, largest + jnp.log(totals))


def time_backward(
    queries, key_band, value_band, valid, log_total, grad_out, score_scale, band_reach
):
    scores = time_scores(queries, key_band, valid, score_scale)
    attend = jnp.exp(scores - log_total)
    grad_attend = jnp.einsum("fphd,fpohd->fpho", grad_out, value_band, preferred_element_type=FLOAT)
    row_dot = jnp.sum(attend * grad_attend, axis=-1, keepdims=True)
    grad_score = (attend * (grad_attend - row_dot)).astype(BHALF)
    grad_query = (
        jnp.einsum("fpho,fpohd->fphd", grad_score, key_band, preferred_element_type=FLOAT)
        * score_scale
    )
    key_part = (
        jnp.einsum("fpho,fphd->fpohd", grad_score, queries, preferred_element_type=FLOAT)
        * score_scale
    )
    value_part = jnp.einsum(
        "fpho,fphd->fpohd", attend.astype(BHALF), grad_out, preferred_element_type=FLOAT
    )
    return (grad_query, band_return(key_part, band_reach), band_return(value_part, band_reach))


def space_forward(queries, key_rows, value_rows, score_scale):
    scores = (
        jnp.einsum("fqhd,fkhd->fhqk", queries, key_rows, preferred_element_type=FLOAT) * score_scale
    )
    largest = jnp.max(scores, axis=-1, keepdims=True)
    exponent = jnp.exp(scores - largest)
    totals = jnp.sum(exponent, axis=-1, keepdims=True)
    attend = (exponent / totals).astype(BHALF)
    result = jnp.einsum("fhqk,fkhd->fqhd", attend, value_rows, preferred_element_type=FLOAT)
    return (result, largest + jnp.log(totals))


def space_backward(queries, key_rows, value_rows, log_total, grad_out, score_scale):
    scores = (
        jnp.einsum("fqhd,fkhd->fhqk", queries, key_rows, preferred_element_type=FLOAT) * score_scale
    )
    attend = jnp.exp(scores - log_total)
    grad_attend = jnp.einsum("fqhd,fkhd->fhqk", grad_out, value_rows, preferred_element_type=FLOAT)
    row_dot = jnp.sum(attend * grad_attend, axis=-1, keepdims=True)
    grad_score = (attend * (grad_attend - row_dot)).astype(BHALF)
    grad_query = (
        jnp.einsum("fhqk,fkhd->fqhd", grad_score, key_rows, preferred_element_type=FLOAT)
        * score_scale
    )
    grad_key = (
        jnp.einsum("fhqk,fqhd->fkhd", grad_score, queries, preferred_element_type=FLOAT)
        * score_scale
    )
    grad_value = jnp.einsum(
        "fhqk,fqhd->fkhd", attend.astype(BHALF), grad_out, preferred_element_type=FLOAT
    )
    return (grad_query, grad_key, grad_value)


def body(
    tokens,
    cls_tokens,
    clip_lengths,
    time_gain,
    time_beta,
    time_proj_in,
    time_qv_bias,
    time_proj_out,
    time_out_bias,
    time_linear,
    time_linear_bias,
    space_gain,
    space_beta,
    space_proj_in,
    space_qv_bias,
    space_proj_out,
    space_out_bias,
    mlp_gain,
    mlp_beta,
    mlp_up,
    mlp_up_bias,
    mlp_down,
    mlp_down_bias,
    out_grad,
    cls_grad,
):
    frames_dev, patches, model_width = tokens.shape
    seq_count = lax.axis_size("seq")
    frames_all = frames_dev * seq_count
    clip_count = clip_lengths.shape[0]
    local_width = time_proj_in.shape[2]
    local_heads = local_width // HEAD_DIM
    band_reach = MAXLEN - 1
    score_scale = HEAD_DIM ** (-0.5)
    seq_rank = lax.axis_index("seq")
    head_rank = lax.axis_index("head")
    clip_ends = jnp.sum(
        jnp.where(jnp.tri(clip_lengths.shape[0], dtype=bool), clip_lengths[None, :], 0), axis=1
    )
    frame_ids = jnp.arange(frames_all, dtype=jnp.int32)
    clip_of = jnp.sum((frame_ids[:, None] >= clip_ends[None, :]).astype(jnp.int32), axis=1)
    clip_pad = jnp.pad(clip_of, (band_reach, band_reach), constant_values=-1)
    valid = jnp.stack(
        [clip_pad[offset : offset + frames_all] == clip_of for offset in range(2 * band_reach + 1)],
        axis=1,
    )
    local_clip = lax.dynamic_slice_in_dim(clip_of, seq_rank * frames_dev, frames_dev)
    onehot = (local_clip[:, None] == jnp.arange(clip_count, dtype=jnp.int32)[None, :]).astype(FLOAT)
    lengths = clip_lengths.astype(FLOAT)
    time_in = to_positions(tokens)
    pos_dev = time_in.shape[1]
    time_rows = frames_all * pos_dev
    time_normed, time_stat, time_inv = layer_norm(time_in.astype(FLOAT), time_gain, time_beta)
    time_normed = time_normed.astype(BHALF).reshape(time_rows, model_width)
    time_in_mat = time_proj_in.reshape(model_width, 3 * local_width)
    time_qkv = (
        (matmul_plain(time_normed, time_in_mat) + qkv_shift(time_qv_bias))
        .astype(BHALF)
        .reshape(frames_all, pos_dev, 3, local_heads, HEAD_DIM)
    )
    time_query = time_qkv[:, :, 0]
    time_keys = band_stack(time_qkv[:, :, 1], band_reach)
    time_values = band_stack(time_qkv[:, :, 2], band_reach)
    time_att, time_log = time_forward(time_query, time_keys, time_values, valid, score_scale)
    time_att = time_att.astype(BHALF).reshape(time_rows, local_width)
    time_mid = (
        lax.psum(matmul_plain(time_att, time_proj_out).astype(jnp.bfloat16), "head").astype(
            jnp.float32
        )
        + time_out_bias
    ).astype(BHALF)
    col_start = head_rank * local_width
    linear_cols = lax.dynamic_slice_in_dim(time_linear, col_start, local_width, 1)
    linear_shift = lax.dynamic_slice_in_dim(time_linear_bias, col_start, local_width)
    time_part = (
        (matmul_plain(time_mid, linear_cols) + linear_shift)
        .astype(BHALF)
        .reshape(frames_all, pos_dev, local_width)
    )
    time_res = to_frames(head_cols(time_part))
    mid = tokens.astype(FLOAT) + time_res.astype(FLOAT)
    span_rows = patches + 1
    space_rows = frames_dev * span_rows
    cls_rows = matmul_plain(onehot.astype(BHALF), cls_tokens)
    space_in = jnp.concatenate([cls_rows[:, None, :], mid], axis=1)
    space_normed, space_stat, space_inv = layer_norm(space_in, space_gain, space_beta)
    space_normed = space_normed.astype(BHALF).reshape(space_rows, model_width)
    space_in_mat = space_proj_in.reshape(model_width, 3 * local_width)
    space_qkv = (
        (matmul_plain(space_normed, space_in_mat) + qkv_shift(space_qv_bias))
        .astype(BHALF)
        .reshape(frames_dev, span_rows, 3, local_heads, HEAD_DIM)
    )
    space_query = space_qkv[:, :, 0]
    space_keys = space_qkv[:, :, 1]
    space_values = space_qkv[:, :, 2]
    space_att, space_log = space_forward(space_query, space_keys, space_values, score_scale)
    space_att = space_att.astype(BHALF).reshape(space_rows, local_width)
    space_sum = (
        lax.psum(matmul_plain(space_att, space_proj_out).astype(jnp.bfloat16), "head").astype(
            jnp.float32
        )
        + space_out_bias
    ).reshape(frames_dev, span_rows, model_width)
    after = mid + space_sum[:, 1:]
    cls_part = exact_tn(onehot, space_sum[:, 0])
    cls_mid = cls_tokens.astype(FLOAT) + lax.psum(cls_part, "seq") / lengths[:, None]
    tok_rows = frames_dev * patches
    rows = jnp.concatenate([after.reshape(tok_rows, model_width), cls_mid], axis=0)
    mlp_normed, mlp_stat, mlp_inv = layer_norm(rows, mlp_gain, mlp_beta)
    mlp_normed = mlp_normed.astype(BHALF)
    pre = matmul_plain(mlp_normed, mlp_up) + mlp_up_bias
    act = jax.nn.gelu(pre, approximate=False).astype(BHALF)
    result = (
        rows
        + lax.psum(matmul_plain(act, mlp_down).astype(jnp.bfloat16), "head").astype(jnp.float32)
        + mlp_down_bias
    )
    block_out = result[:tok_rows].reshape(frames_dev, patches, model_width).astype(BHALF)
    cls_out = result[tok_rows:].astype(BHALF)
    first_seq = (seq_rank == 0).astype(FLOAT)
    keep_rows = jnp.concatenate(
        [jnp.ones((tok_rows, 1), FLOAT), jnp.ones((clip_count, 1), FLOAT) * first_seq], axis=0
    )
    keep_half = keep_rows.astype(BHALF)
    grad_rows = jnp.concatenate([out_grad.reshape(tok_rows, model_width), cls_grad], axis=0)
    down_grad = matmul_tn(act * keep_half, grad_rows)
    down_shift_grad = jnp.sum(grad_rows.astype(FLOAT) * keep_rows, axis=0)
    grad_pre = (matmul_nt(grad_rows, mlp_down) * gelu_slope(pre)).astype(BHALF)
    up_grad = matmul_tn(mlp_normed * keep_half, grad_pre)
    up_shift_grad = jnp.sum(grad_pre.astype(FLOAT) * keep_rows, axis=0)
    grad_mlp_norm = lax.psum(matmul_nt(grad_pre, mlp_up).astype(jnp.bfloat16), "head").astype(
        jnp.float32
    )
    grad_mlp_in, mlp_gain_grad, mlp_beta_grad = norm_back(
        grad_mlp_norm, mlp_gain, mlp_stat, mlp_inv, keep_rows
    )
    grad_total = grad_rows.astype(FLOAT) + grad_mlp_in
    grad_after = grad_total[:tok_rows].reshape(frames_dev, patches, model_width)
    grad_cls_mid = grad_total[tok_rows:]
    cls_share = exact_nn(onehot, grad_cls_mid / lengths[:, None])
    grad_space_sum = (
        jnp.concatenate([cls_share[:, None, :], grad_after], axis=1)
        .astype(BHALF)
        .reshape(space_rows, model_width)
    )
    space_out_grad = matmul_tn(space_att, grad_space_sum)
    space_shift_grad = jnp.sum(grad_space_sum.astype(FLOAT), axis=0)
    grad_space_att = (
        matmul_nt(grad_space_sum, space_proj_out)
        .astype(BHALF)
        .reshape(frames_dev, span_rows, local_heads, HEAD_DIM)
    )
    space_grad_query, space_grad_key, space_grad_value = space_backward(
        space_query, space_keys, space_values, space_log, grad_space_att, score_scale
    )
    grad_space_qkv = (
        jnp.stack([space_grad_query, space_grad_key, space_grad_value], axis=2)
        .astype(BHALF)
        .reshape(space_rows, 3 * local_width)
    )
    space_in_grad = matmul_tn(space_normed, grad_space_qkv).reshape(model_width, 3, local_width)
    space_pair_grad = pair_sums(grad_space_qkv, local_width)
    grad_space_norm = (
        lax.psum(matmul_nt(grad_space_qkv, space_in_mat).astype(jnp.bfloat16), "head")
        .astype(jnp.float32)
        .reshape(frames_dev, span_rows, model_width)
    )
    grad_space_in, space_gain_grad, space_beta_grad = norm_back(
        grad_space_norm, space_gain, space_stat, space_inv, 1.0
    )
    grad_mid = grad_after + grad_space_in[:, 1:]
    cls_in_part = exact_tn(onehot, grad_space_in[:, 0])
    grad_time_res = to_positions(grad_mid.astype(BHALF)).reshape(time_rows, model_width)
    linear_grad = matmul_tn(
        time_mid, lax.dynamic_slice_in_dim(grad_time_res, col_start, local_width, 1)
    )
    linear_shift_grad = jnp.sum(grad_time_res.astype(FLOAT), axis=0)
    grad_time_mid = matmul_nt(grad_time_res, time_linear).astype(BHALF)
    time_out_grad = matmul_tn(time_att, grad_time_mid)
    time_shift_grad = jnp.sum(grad_time_mid.astype(FLOAT), axis=0)
    grad_time_att = (
        matmul_nt(grad_time_mid, time_proj_out)
        .astype(BHALF)
        .reshape(frames_all, pos_dev, local_heads, HEAD_DIM)
    )
    time_grad_query, time_grad_key, time_grad_value = time_backward(
        time_query, time_keys, time_values, valid, time_log, grad_time_att, score_scale, band_reach
    )
    grad_time_qkv = (
        jnp.stack([time_grad_query, time_grad_key, time_grad_value], axis=2)
        .astype(BHALF)
        .reshape(time_rows, 3 * local_width)
    )
    time_in_grad = matmul_tn(time_normed, grad_time_qkv).reshape(model_width, 3, local_width)
    time_pair_grad = pair_sums(grad_time_qkv, local_width)
    grad_time_norm = (
        lax.psum(matmul_nt(grad_time_qkv, time_in_mat).astype(jnp.bfloat16), "head")
        .astype(jnp.float32)
        .reshape(frames_all, pos_dev, model_width)
    )
    grad_time_in, time_gain_grad, time_beta_grad = norm_back(
        grad_time_norm, time_gain, time_stat, time_inv, 1.0
    )
    grad_tokens_time = to_frames(grad_time_in.astype(BHALF))
    tokens_grad = (grad_mid + grad_tokens_time.astype(FLOAT)).astype(BHALF)
    summed = (
        lax.psum_scatter(time_gain_grad, "seq", scatter_dimension=0, tiled=True),
        lax.psum_scatter(time_in_grad, "seq", scatter_dimension=0, tiled=True),
        lax.psum_scatter(time_out_grad, "seq", scatter_dimension=1, tiled=True),
        lax.psum_scatter(linear_grad, "seq", scatter_dimension=0, tiled=True),
        lax.psum_scatter(space_gain_grad, "seq", scatter_dimension=0, tiled=True),
        lax.psum_scatter(space_in_grad, "seq", scatter_dimension=0, tiled=True),
        lax.psum_scatter(space_out_grad, "seq", scatter_dimension=1, tiled=True),
        lax.psum_scatter(mlp_gain_grad, "seq", scatter_dimension=0, tiled=True),
        lax.psum_scatter(up_grad, "seq", scatter_dimension=0, tiled=True),
        lax.psum_scatter(down_grad, "seq", scatter_dimension=1, tiled=True),
        lax.psum_scatter(cls_in_part, "seq", scatter_dimension=1, tiled=True),
    )
    shifts = lax.psum(
        (
            time_beta_grad,
            time_pair_grad,
            time_shift_grad,
            linear_shift_grad,
            space_beta_grad,
            space_pair_grad,
            space_shift_grad,
            mlp_beta_grad,
            up_shift_grad,
            down_shift_grad,
        ),
        "seq",
    )
    col_width = model_width // seq_count
    cls_direct = lax.dynamic_slice_in_dim(grad_cls_mid, seq_rank * col_width, col_width, 1)
    cls_tokens_grad = summed[10] + cls_direct
    return (
        block_out,
        cls_out,
        tokens_grad,
        cls_tokens_grad,
        summed[0],
        shifts[0],
        summed[1],
        shifts[1],
        summed[2],
        shifts[2],
        summed[3],
        shifts[3],
        summed[4],
        shifts[4],
        summed[5],
        shifts[5],
        summed[6],
        shifts[6],
        summed[7],
        shifts[7],
        summed[8],
        shifts[8],
        summed[9],
        shifts[9],
    )


MESH = pl.DeviceIdType.MESH
ROWS = 208
HALF = 16
SLOTS = 2 * HALF


def dot_nn(left, right):
    return jnp.dot(left, right, preferred_element_type=FLOAT)


def dot_nt(left, right):
    return lax.dot_general(left, right, (((1,), (1,)), ((), ())), preferred_element_type=FLOAT)


def dot_tn(left, right):
    return lax.dot_general(left, right, (((0,), (0,)), ((), ())), preferred_element_type=FLOAT)


def iota(shape, axis):
    return lax.broadcasted_iota(jnp.int32, shape, axis)


def scratch_shapes(dims):
    frames, seq, width, model, hidden = dims["frames"], dims["seq"], dims["width"], dims["model"], dims["hidden"]
    rows, every, heads = frames * ROWS, frames * seq, width // HEAD_DIM
    half, low = model // 2, BHALF
    vm = pltpu.VMEM
    shapes = dict(
        tok=vm((dims["patches"], frames, model), low),
        out_grad=vm((dims["patches"], frames, model), low),
        w_ti=vm((3 * width, model), low),
        w_si=vm((3 * width, model), low),
        w_tl=vm((model, model), low),
        w_up=vm((model, hidden), low),
        w_dn=vm((hidden, model), low),
        w_to=vm((2, 2, width, model), low),
        w_so=vm((2, 2, width, model), low),
        x32=vm((rows, model), FLOAT),
        gr32=vm((rows, model), FLOAT),
        t32=vm((rows, model), FLOAT),
        u32=vm((rows, model), FLOAT),
        dact=vm((rows, hidden), FLOAT),
        xh_t=vm((rows, model), FLOAT),
        xh_s=vm((rows, model), FLOAT),
        xh_m=vm((rows, model), FLOAT),
        inv=vm((3, rows, 128), FLOAT),
        n_t=vm((rows, model), low),
        n_s=vm((rows, model), low),
        n_m=vm((rows, model), low),
        gr16=vm((rows, model), low),
        mid16=vm((rows, model), low),
        act=vm((rows, hidden), low),
        act_k=vm((rows, hidden), low),
        gpre=vm((rows, hidden), low),
        gpre_k=vm((rows, hidden), low),
        gss=vm((rows, model), low),
        gtr=vm((rows, model), low),
        gtm=vm((rows, model), low),
        sqkv=vm((rows, 3 * width), low),
        dsq=vm((rows, 3 * width), low),
        dtq=vm((rows, 3 * width), low),
        gatt=vm((rows, width), low),
        sel=vm((seq * SLOTS, ROWS), low),
        les=vm((ROWS, seq * SLOTS), low),
        tmask=vm((every * HALF, every * HALF), FLOAT),
        p_t=vm((2 * heads, every * HALF, every * HALF), FLOAT),
        p_s=vm((frames * heads, ROWS, ROWS), FLOAT),
        q_send=vm((frames, seq, 2, HALF, 3 * width), low),
        q_pos=vm((2, every, HALF, 3 * width), low),
        a_pos=vm((2, every, HALF, width), low),
        a_recv=vm((2, seq, frames, HALF, width), low),
        g_send=vm((frames, seq, 2, HALF, width), low),
        g_pos=vm((2, every, HALF, width), low),
        d_pos=vm((2, every, HALF, 3 * width), low),
        d_recv=vm((2, seq, frames, HALF, 3 * width), low),
        att_t=vm((2, 2, rows, width), low),
        att_s=vm((2, 2, rows, width), low),
        part=vm((4, 2, rows, half), low),
        pair=vm((4, rows, half), low),
        other=vm((4, rows, half), low),
        total=vm((4, 2, rows, half), low),
        cls_send=vm((8, width), FLOAT),
        cls_recv=vm((seq, 8, width), FLOAT),
        cls_head=vm((4, 8, model), FLOAT),
        gcm=vm((8, model), FLOAT),
        v_send=vm((3, 8, model), FLOAT),
        v_recv=vm((3, seq, 8, model), FLOAT),
        v_head=vm((4, 8, model), FLOAT),
    )
    for name, columns in grad_columns(dims):
        share = model // seq
        shapes["g_" + name] = vm((seq // 4, 2, 2, share, columns), low)
        shapes["y_" + name] = vm((2, seq // 4, share, columns), low)
        shapes["z_" + name] = vm((seq // 4, share, columns), low)
        shapes["x_" + name] = vm((share, columns), low)
    for name in VECTORS:
        shapes[name] = vm((hidden if name == "m_ub" else model,), FLOAT)
    for name in PAIRS:
        shapes[name] = vm((2, width), FLOAT)
    shapes["load"] = pltpu.SemaphoreType.DMA((32,))
    shapes["sent"] = pltpu.SemaphoreType.DMA((320,))
    shapes["got"] = pltpu.SemaphoreType.DMA((320,))
    return shapes


def grad_columns(dims):
    width, model, hidden = dims["width"], dims["model"], dims["hidden"]
    return (
        ("dn", hidden),
        ("up", hidden),
        ("s", 4 * width),
        ("l", 2 * width),
        ("ta", 2 * width),
        ("tb", width),
    )


VECTORS = ("t_gain", "t_beta", "t_ob", "t_lb", "s_gain", "s_beta", "s_ob", "m_gain", "m_beta", "m_db", "m_ub")
PAIRS = ("t_qv", "s_qv")
MATRICES = ("tok", "out_grad", "w_ti", "w_to", "w_tl", "w_si", "w_so", "w_up", "w_dn")
INPUTS = ("lens", "cls", "cls_grad") + tuple("h_" + name for name in VECTORS + PAIRS + MATRICES)
OUTPUTS = ("o_blk", "o_cls", "o_tok", "o_vec")


class Refs:
    pass


class Exchange:
    def __init__(self, out, into):
        self.wait_send, self.wait_recv = out.wait_send, into.wait_recv


def layer_kernel(dims, names, *refs):
    k = Refs()
    for name, ref in zip(names, refs):
        setattr(k, name, ref)
    frames, seq, width, model, hidden = dims["frames"], dims["seq"], dims["width"], dims["model"], dims["hidden"]
    patches, clips, pos = dims["patches"], dims["clips"], dims["pos"]
    rows, every, heads, half = frames * ROWS, frames * seq, width // HEAD_DIM, model // 2
    zs = seq // 2
    share_rows = model // seq
    scale = HEAD_DIM ** (-0.5)
    s, h = lax.axis_index("seq"), lax.axis_index("head")
    z, y = s // 2, s % 2
    x, c = h // 2, h % 2
    other_c = 1 - c
    sister, across, diagonal = (s, x * 2 + other_c), (s, (1 - x) * 2 + c), (s, (1 - x) * 2 + other_c)
    y_peer = (z * 2 + 1 - y, h)
    peers = [((z + i) % zs) * 2 + (y + j) % 2 for i in range(zs) for j in range(2) if i or j]
    givers = [((z + zs - i) % zs) * 2 + (y + j) % 2 for i in range(zs) for j in range(2) if i or j]
    used = [0]

    def send(src, dst, device, lands):
        index = used[0]
        used[0] += 1
        sems = dict(send_sem=k.sent.at[index], recv_sem=k.got.at[index], device_id=device, device_id_type=MESH)
        copy = pltpu.make_async_remote_copy(src_ref=src, dst_ref=dst, **sems)
        copy.start()
        copy = Exchange(copy, pltpu.make_async_remote_copy(src_ref=src, dst_ref=lands, **sems))
        unsent.append(copy)
        return copy

    unsent = []
    loads = [0]

    def load(src, dst):
        copy = pltpu.make_async_copy(src, dst, k.load.at[loads[0]])
        loads[0] += 1
        copy.start()
        return copy

    places = {"w_to": k.w_to.at[0, c], "w_so": k.w_so.at[0, c]}
    order = ("tok", "t_gain", "t_beta", "w_ti", "t_qv", "w_to", "w_so", "out_grad", "w_dn") + VECTORS[2:] + ("s_qv", "w_tl", "w_si", "w_up")
    loading = {name: load(getattr(k, "h_" + name), places.get(name, getattr(k, name))) for name in order}

    def need(*wanted):
        for name in wanted:
            loading.pop(name).wait()

    barrier = pltpu.get_barrier_semaphore()
    everyone = [(p, h) for p in peers] + [sister, across, diagonal]
    for device in everyone:
        pl.semaphore_signal(barrier, inc=1, device_id=device, device_id_type=MESH)

    def vec(name):
        if name in loading:
            need(name)
        return getattr(k, name)[...].reshape(1, -1)

    def qkv_row(name):
        need(name)
        pair = getattr(k, name)
        return jnp.concatenate([pair[0:1, :], jnp.zeros((1, width), FLOAT), pair[1:2, :]], axis=-1)

    def chosen(slot, row, outer):
        if outer:
            device, place = slot // SLOTS, slot % SLOTS
        else:
            device, place = slot // HALF % seq, slot // (HALF * seq) * HALF + slot % HALF
        hit = (device * pos + place == row) & (place < pos) & (row < patches)
        return jnp.where(hit, 1.0, 0.0).astype(BHALF)

    k.sel[...] = chosen(iota((seq * SLOTS, ROWS), 0), iota((seq * SLOTS, ROWS), 1), True)
    ends = []
    for i in range(clips):
        ends.append(k.lens[i] + (ends[-1] if i else 0))

    def clip_of(frame):
        total = (frame >= ends[0]).astype(jnp.int32)
        for end in ends[1:]:
            total = total + (frame >= end).astype(jnp.int32)
        return total

    onehot = []
    for f in range(frames):
        own = clip_of(jnp.full((1, model), s * frames + f, jnp.int32))
        onehot.append([(own == i).astype(FLOAT) for i in range(clips)])
    per_len = [1.0 / jnp.full((1, model), k.lens[i], jnp.int32).astype(FLOAT) for i in range(clips)]
    cls32 = k.cls[...].astype(FLOAT)
    cls_row = [sum(onehot[f][i] * cls32[i : i + 1] for i in range(clips)) for f in range(frames)]
    tail = ROWS - patches

    def set_tail(ref, f, first):
        used_rows = sum(r.shape[0] for r in first)
        fill = [jnp.zeros((tail - used_rows, model), FLOAT)] if used_rows < tail else []
        ref[f * ROWS + patches : (f + 1) * ROWS, :] = jnp.concatenate(list(first) + fill, axis=0)

    def eight(values):
        missing = 8 - sum(v.shape[0] for v in values)
        fill = [jnp.zeros((missing, values[0].shape[1]), FLOAT)] if missing else []
        return jnp.concatenate(list(values) + fill, axis=0)

    def frame(f):
        return slice(f * ROWS, (f + 1) * ROWS)

    def norm(src, which, gain, shift, xhat, out, r):
        v = src[r, :]
        center = v - jnp.mean(v, axis=-1, keepdims=True)
        invstd = lax.rsqrt(jnp.mean(center * center, axis=-1, keepdims=True) + EPS)
        n = center * invstd
        xhat[r, :] = n
        k.inv[which, r, :] = jnp.broadcast_to(invstd, (v.shape[0], 128))
        out[r, :] = (n * gain + shift).astype(BHALF)

    def arrived(copies):
        for copy in copies:
            copy.wait_recv()

    def to_slots(f, value, src):
        moved = dot_nn(k.sel[...], value).astype(BHALF)
        src[f] = moved.reshape(seq, 2, HALF, value.shape[-1])

    def scatter(f, value, src, dst):
        to_slots(f, value, src)
        to = frames * s + f
        copies = [
            [send(src.at[f, p, b], dst.at[b, to], (p, h), dst.at[b, frames * q + f]) for p, q in zip(peers, givers)]
            for b in range(2)
        ]
        dst[:, to] = src[f, s]
        return copies

    def gather(b, src, dst):
        copies = [
            send(src.at[b, pl.ds(frames * p, frames)], dst.at[b, s], (p, h), dst.at[b, q]) for p, q in zip(peers, givers)
        ]
        dst[b, s] = src[b, pl.ds(frames * s, frames)]
        return copies

    def gathered(f, src):
        return dot_nn(k.les[...], src[:, :, f].reshape(seq * SLOTS, src.shape[-1])).astype(BHALF)

    need("tok")
    t_gain, t_beta, t_qb = vec("t_gain"), vec("t_beta"), qkv_row("t_qv")
    q_copies = []
    for f in range(frames):
        k.x32[f * ROWS : f * ROWS + patches, :] = k.tok[:, f, :].astype(FLOAT)
        set_tail(k.x32, f, [])
        norm(k.x32, 0, t_gain, t_beta, k.xh_t, k.n_t, frame(f))
        if f == 0:
            need("w_ti")
        qkv = (dot_nt(k.n_t[frame(f), :], k.w_ti[...]) + t_qb).astype(BHALF)
        if f == 0:
            pl.semaphore_wait(barrier, len(everyone))
        q_copies.append(scatter(f, qkv, k.q_send, k.q_pos))

    def share(ref):
        return (
            send(ref.at[0, c], ref.at[0, c], sister, ref.at[0, other_c]),
            send(ref.at[0, c], ref.at[1, c], across, ref.at[1, c]),
        )

    def pass_on(ref):
        return send(ref.at[1, c], ref.at[1, c], sister, ref.at[1, other_c])

    need("w_to", "w_so")
    w_to_near, w_to_far = share(k.w_to)
    w_so_near, w_so_far = share(k.w_so)

    k.les[...] = chosen(iota((ROWS, seq * SLOTS), 1), iota((ROWS, seq * SLOTS), 0), False)
    span = every * HALF
    left, right = iota((span, span), 0), iota((span, span), 1)
    same = (left % HALF == right % HALF) & (clip_of(left // HALF) == clip_of(right // HALF))
    near = jnp.abs(left // HALF - right // HALF) < MAXLEN
    k.tmask[...] = jnp.where(same & near, 0.0, NEG)
    need("out_grad")
    cls_g = k.cls_grad[...].astype(FLOAT)
    for f in range(frames):
        k.gr32[f * ROWS : f * ROWS + patches, :] = k.out_grad[:, f, :].astype(FLOAT)
        set_tail(k.gr32, f, [cls_g] if f == 0 else [])
        k.gr16[frame(f), :] = k.gr32[frame(f), :].astype(BHALF)
    need("w_dn")
    k.dact[...] = dot_nt(k.gr16[...], k.w_dn[...])
    w_to_far.wait_recv()
    w_to_last = pass_on(k.w_to)
    w_so_far.wait_recv()
    w_so_last = pass_on(k.w_so)

    def attend(q, key, value, mask, p_ref):
        scores = dot_nt(q, key) * scale + mask
        e = jnp.exp(scores - jnp.max(scores, axis=-1, keepdims=True))
        p = e * (1.0 / jnp.sum(e, axis=-1, keepdims=True))
        p_ref[...] = p
        return dot_nn(p.astype(BHALF), value).astype(BHALF)

    def attend_back(q, key, value, grad, p_ref):
        p = p_ref[...]
        grad_p = p * dot_nt(grad, value)
        grad_s = (grad_p - p * jnp.sum(grad_p, axis=-1, keepdims=True)).astype(BHALF)
        grad_q = (dot_nn(grad_s, key) * scale).astype(BHALF)
        grad_k = (dot_tn(grad_s, q) * scale).astype(BHALF)
        grad_v = dot_tn(p.astype(BHALF), grad).astype(BHALF)
        return grad_q, grad_k, grad_v

    def head_of(value, part, j):
        at = part * width + j * HEAD_DIM
        return value[:, at : at + HEAD_DIM]

    def attend_all(qkv, mask, p_ref, first):
        out = [
            attend(*[head_of(qkv, i, j) for i in range(3)], mask, p_ref.at[first + j]) for j in range(heads)
        ]
        return jnp.concatenate(out, axis=-1)

    def attend_back_all(qkv, grad, p_ref, first):
        out = [
            attend_back(*[head_of(qkv, i, j) for i in range(3)], head_of(grad, 0, j), p_ref.at[first + j])
            for j in range(heads)
        ]
        return jnp.concatenate([out[j][i] for i in range(3) for j in range(heads)], axis=-1)

    a_copies = []
    for b in range(2):
        for copies in q_copies:
            arrived(copies[b])
        out = attend_all(k.q_pos[b].reshape(span, 3 * width), k.tmask[...], k.p_t, b * heads)
        k.a_pos[b] = out.reshape(every, HALF, width)
        a_copies += gather(b, k.a_pos, k.a_recv)
    arrived(a_copies)

    def features(f, att):
        r = frame(f)
        return (
            send(att.at[0, c, r], att.at[0, c, r], sister, att.at[0, other_c, r]),
            send(att.at[0, c, r], att.at[1, c, r], across, att.at[1, c, r]),
        )

    def own_part(f, att, weight, copies):
        r = frame(f)
        copies[0].wait_recv()
        k.t32[r, :] = dot_nn(att[0, 0, r], weight[0, 0]) + dot_nn(att[0, 1, r], weight[0, 1])

    def features_on(f, att, copies):
        copies[1].wait_recv()
        r = frame(f)
        return send(att.at[1, c, r], att.at[1, c, r], sister, att.at[1, other_c, r])

    def both_parts(f, att, weight, copy):
        r = frame(f)
        copy.wait_recv()
        k.u32[r, :] = dot_nn(att[1, 0, r], weight[1, 0]) + dot_nn(att[1, 1, r], weight[1, 1])
        own, other = k.t32[r, :], k.u32[r, :]
        return jnp.where(x == 0, own, other) + jnp.where(x == 0, other, own)

    ta_copies = []
    for f in range(frames):
        k.att_t[0, c, frame(f), :] = gathered(f, k.a_recv)
        ta_copies.append(features(f, k.att_t))
    arrived([w_to_near, w_to_last])
    t_ob, t_lb, s_gain, s_beta, s_qb = vec("t_ob"), vec("t_lb"), vec("s_gain"), vec("s_beta"), qkv_row("s_qv")
    need("w_tl", "w_si")
    in_frame = jnp.where(iota((1, ROWS), 1) < patches + 1, 0.0, NEG)
    for f in range(frames):
        own_part(f, k.att_t, k.w_to, ta_copies[f])
    ta_last, sa_copies = [], []
    for f in range(frames):
        ta_last.append(features_on(f, k.att_t, ta_copies[f]))
    for f in range(frames):
        r = frame(f)
        k.mid16[r, :] = (both_parts(f, k.att_t, k.w_to, ta_last[f]) + t_ob).astype(BHALF)
        res = (dot_nn(k.mid16[r, :], k.w_tl[...]) + t_lb).astype(BHALF)
        k.x32[r, :] = k.x32[r, :] + res.astype(FLOAT)
        set_tail(k.x32, f, [cls_row[f]])
        norm(k.x32, 1, s_gain, s_beta, k.xh_s, k.n_s, r)
        k.sqkv[r, :] = (dot_nt(k.n_s[r, :], k.w_si[...]) + s_qb).astype(BHALF)
        k.att_s[0, c, r, :] = attend_all(k.sqkv[r, :], in_frame, k.p_s, f * heads)
        sa_copies.append(features(f, k.att_s))
    lone = patches - (ROWS - HALF)
    feats = []
    for f in range(frames):
        last_rows = k.att_s[0, c, (f + 1) * ROWS - HALF : (f + 1) * ROWS, :].astype(FLOAT)
        feats.append(last_rows[lone : lone + 1])
    k.cls_send[...] = eight([sum(onehot[f][i][:, :width] * feats[f] for f in range(frames)) for i in range(clips)])
    cls_copies = [send(k.cls_send, k.cls_recv.at[s], (p, h), k.cls_recv.at[q]) for p, q in zip(peers, givers)]
    k.cls_recv[s] = k.cls_send[...]
    arrived([w_so_near, w_so_last])
    s_ob, m_gain, m_beta = vec("s_ob"), vec("m_gain"), vec("m_beta")
    for f in range(frames):
        own_part(f, k.att_s, k.w_so, sa_copies[f])
    sa_last = []
    for f in range(frames):
        sa_last.append(features_on(f, k.att_s, sa_copies[f]))
    arrived(cls_copies)
    feat = k.cls_recv[0]
    for i in range(1, seq):
        feat = feat + k.cls_recv[i]
    high = feat.astype(BHALF)
    rest = (feat - high.astype(FLOAT)).astype(BHALF)
    k.cls_head[h] = dot_nn(high, k.w_so[0, c]) + dot_nn(rest, k.w_so[0, c])
    cls_copies = [send(k.cls_head.at[h], k.cls_head.at[h], d, k.cls_head.at[d[1]]) for d in (sister, across, diagonal)]
    cls_at = [slice(f * ROWS + patches, f * ROWS + patches + 1) for f in range(frames)]
    for f in range(frames):
        r = frame(f)
        k.x32[r, :] = k.x32[r, :] + (both_parts(f, k.att_s, k.w_so, sa_last[f]) + s_ob)
        set_tail(k.x32, f, [])

    first_seq = jnp.where(s == 0, 1.0, 0.0)
    m_ub = vec("m_ub")
    need("w_up")

    def up_rows(r):
        norm(k.x32, 2, m_gain, m_beta, k.xh_m, k.n_m, r)
        k.t32[r, :] = dot_nn(k.n_m[r, :], k.w_up[...])

    def kept(r):
        at = r.start + iota((r.stop - r.start, 1), 0)
        return jnp.where((at >= patches) & (at < ROWS), first_seq, 1.0)

    def gelu_rows(r):
        pre = k.t32[r, :] + m_ub
        cdf = 0.5 * (1.0 + lax.erf(pre * 0.7071067811865476))
        slope = cdf + pre * jnp.exp(-0.5 * pre * pre) * 0.3989422804014327
        act = pre * cdf
        grad = k.dact[r, :] * slope
        k.act[r, :] = act.astype(BHALF)
        k.gpre[r, :] = grad.astype(BHALF)
        if r.start == 0:
            act, grad = act * kept(r), grad * kept(r)
        k.act_k[r, :] = act.astype(BHALF)
        k.gpre_k[r, :] = grad.astype(BHALF)

    def sum_open(i, f, lhs, rhs, dot):
        r = frame(f)
        for b in range(2):
            cut = slice(b * half, (b + 1) * half)
            k.part[i, b, r, :] = dot(lhs[r, :], rhs[cut, :] if dot is dot_nt else rhs[:, cut]).astype(BHALF)
        return send(k.part.at[i, other_c, r], k.pair.at[i, r], sister, k.pair.at[i, r])

    def sum_across(i, f, copy):
        r = frame(f)
        copy.wait_recv()
        k.part[i, c, r, :] = (k.part[i, c, r, :].astype(FLOAT) + k.pair[i, r, :].astype(FLOAT)).astype(BHALF)
        return send(k.part.at[i, c, r], k.other.at[i, r], across, k.other.at[i, r])

    def sum_close(i, f, copy):
        r = frame(f)
        copy.wait_recv()
        k.total[i, c, r, :] = (k.part[i, c, r, :].astype(FLOAT) + k.other[i, r, :].astype(FLOAT)).astype(BHALF)
        return send(k.total.at[i, c, r], k.total.at[i, c, r], sister, k.total.at[i, other_c, r])

    def rows_of(ref, i, r):
        return jnp.concatenate([ref[i, 0, r, :], ref[i, 1, r, :]], axis=-1).astype(FLOAT)

    z_hi, z_lo = z // 2, z % 2
    z_near, z_far = ((z + 1 - 2 * z_lo) * 2 + y, h), (((z + 2) % zs) * 2 + y, h)
    z_first = ('up',)

    def grad_make(name, *pairs):
        g = getattr(k, "g_" + name)
        parts = [dot_tn(lhs, rhs).astype(BHALF) for lhs, rhs in pairs]
        value = parts[0] if len(parts) == 1 else jnp.concatenate(parts, axis=-1)
        g[...] = value.reshape(g.shape)

    class Reduction:
        def __init__(self, name):
            self.name, self.g = name, getattr(k, "g_" + name)
            self.first, self.second, self.third = [getattr(k, kind + name) for kind in ("y_", "z_", "x_")]
            ways = [(y, y_peer), (z_lo, z_near)]
            (self.one, self.peer_one), (self.two, self.peer_two) = ways[::-1] if name in z_first else ways

        def at(self, one, two):
            return (slice(None), one, two) if self.name in z_first else (slice(None), two, one)

        def add(self, at, got):
            self.g[at] = (self.g[at].astype(FLOAT) + got.astype(FLOAT)).astype(BHALF)

    def grad_open(name):
        job = Reduction(name)
        job.copies = []
        for two in (1 - job.two, job.two):
            into = job.first.at[two]
            job.copies.append(send(job.g.at[job.at(1 - job.one, two)], into, job.peer_one, into))
        return job

    def grad_near(job):
        job.copies[0].wait_recv()
        away, kept_here = job.at(job.one, 1 - job.two), job.at(job.one, job.two)
        job.add(away, job.first[1 - job.two])
        copy = send(job.g.at[away], job.second, job.peer_two, job.second)
        job.copies[1].wait_recv()
        job.add(kept_here, job.first[job.two])
        job.copies = [copy]
        return job

    def grad_far(job):
        job.copies[0].wait_recv()
        job.add(job.at(job.one, job.two), job.second[...])
        job.copies = [send(job.g.at[1 - z_hi, z_lo, y], job.third, z_far, job.third)]
        return job

    def grad_close(job):
        job.copies[0].wait_recv()
        getattr(k, "o_" + job.name)[...] = job.g[z_hi, z_lo, y].astype(FLOAT) + job.third[...].astype(FLOAT)

    def vectors_send(which, values):
        value = eight(values)
        k.v_send[which] = value
        k.v_recv[which, s] = value
        into = k.v_recv.at[which]
        return [send(k.v_send.at[which], into.at[s], (p, h), into.at[q]) for p, q in zip(peers, givers)]

    def vectors_close(which, copies):
        arrived(copies)
        value = k.v_recv[which, 0]
        for i in range(1, seq):
            value = value + k.v_recv[which, i]
        return value

    ones = jnp.ones((8, rows), BHALF)
    at = iota((8, rows), 1)
    ones_kept = jnp.where((at >= patches) & (at < ROWS), first_seq, 1.0).astype(BHALF)

    def col_sums(ref, weights=None):
        out = dot_nn(ones if weights is None else weights, ref[...])[0:1]
        if out.shape[1] < model:
            out = jnp.concatenate([out, jnp.zeros((1, model - out.shape[1]), FLOAT)], axis=-1)
        return out

    def column_sum(v):
        return jnp.sum(v, axis=0, keepdims=True)

    def add_all(lists):
        return [sum(v) for v in zip(*lists)]

    def norm_back(i, which, gain, xhat, r, keep):
        g = rows_of(k.total, i, r)
        n = xhat[r, :]
        gh = g * gain
        m1 = jnp.mean(gh, axis=-1, keepdims=True)
        m2 = jnp.mean(gh * n, axis=-1, keepdims=True)
        dx = k.inv[which, r, 0:1] * (gh - m1 - n * m2)
        w = g * kept(r) if keep and r.start == 0 else g
        return dx, (column_sum(w * n), column_sum(w))

    m_sum = [None] * frames
    for f in range(1, frames):
        up_rows(frame(f))
        gelu_rows(frame(f))
        m_sum[f] = sum_open(0, f, k.gpre, k.w_up, dot_nt)
    up_rows(frame(0))
    for f in range(1, frames):
        m_sum[f] = sum_across(0, f, m_sum[f])
    arrived(cls_copies)
    cls_sum = k.cls_head[0] + k.cls_head[1] + k.cls_head[2] + k.cls_head[3]
    set_tail(k.x32, 0, [cls32[i : i + 1] + cls_sum[i : i + 1] * per_len[i] + s_ob for i in range(clips)])
    up_rows(slice(ROWS - HALF, ROWS))
    gelu_rows(frame(0))
    m_sum[0] = sum_open(0, 0, k.gpre, k.w_up, dot_nt)
    o_sum = [sum_open(1, f, k.act, k.w_dn, dot_nn) for f in range(frames)]
    m_sum[0] = sum_across(0, 0, m_sum[0])
    grad_make("dn", (k.gr16[...], k.act_k[...]))
    j_dn = grad_open("dn")
    grad_make("up", (k.n_m[...], k.gpre_k[...]))
    j_up = grad_open("up")
    ub_grad, db_grad = col_sums(k.gpre_k), col_sums(k.gr16, ones_kept)
    m_last, sums = [None] * frames, [None] * frames
    backwards = list(range(1, frames)) + [0]
    for f in backwards:
        m_last[f] = sum_close(0, f, m_sum[f])
    for f in backwards:
        m_last[f].wait_recv()
        dx, sums[f] = norm_back(0, 2, m_gain, k.xh_m, frame(f), True)
        k.gr32[frame(f), :] = k.gr32[frame(f), :] + dx
    grad_cls_mid = k.gr32[patches : patches + clips, :]
    k.gcm[...] = eight([grad_cls_mid])
    shares = [
        sum(onehot[f][i] * (grad_cls_mid[i : i + 1] * per_len[i]) for i in range(clips)) for f in range(frames)
    ]

    def space_back(f):
        r = frame(f)
        set_tail(k.gr32, f, [shares[f]])
        k.gss[r, :] = k.gr32[r, :].astype(BHALF)
        set_tail(k.gr32, f, [])
        grad = dot_nt(k.gss[r, :], k.w_so[0, c]).astype(BHALF)
        k.dsq[r, :] = attend_back_all(k.sqkv[r, :], grad, k.p_s, f * heads)
        return sum_open(2, f, k.dsq, k.w_si, dot_nn)

    s_sum = []
    for f in range(frames):
        s_sum.append(space_back(f))
        if f:
            s_sum[f - 1] = sum_across(2, f - 1, s_sum[f - 1])
    m_rows = add_all(sums) + [ub_grad, db_grad]
    s_sum[-1] = sum_across(2, frames - 1, s_sum[-1])
    j_dn = grad_near(j_dn)
    j_up = grad_near(j_up)
    v_m = vectors_send(0, m_rows)
    grad_make("s", (k.n_s[...], k.dsq[...]), (k.gss[...], k.att_s[0, c]))
    j_s = grad_open("s")
    s_rows = [col_sums(k.gss), col_sums(k.dsq)]
    s_last = [sum_close(2, f, s_sum[f]) for f in range(frames)]

    g_copies, cls_in = [], []
    for f in range(frames):
        r = frame(f)
        s_last[f].wait_recv()
        dx, sums[f] = norm_back(2, 1, s_gain, k.xh_s, r, False)
        k.gr32[r, :] = k.gr32[r, :] + dx
        cls_in.append(k.gr32[cls_at[f], :])
        set_tail(k.gr32, f, [])
        k.gtr[r, :] = k.gr32[r, :].astype(BHALF)
        k.gtm[r, :] = dot_nt(k.gtr[r, :], k.w_tl[...]).astype(BHALF)
        grad = dot_nt(k.gtm[r, :], k.w_to[0, c]).astype(BHALF)
        g_copies.append(scatter(f, grad, k.g_send, k.g_pos))
    o_sum = [sum_across(1, f, o_sum[f]) for f in range(frames)]
    j_dn = grad_far(j_dn)
    j_up = grad_far(j_up)
    pick = (iota((model, width), 0) == h * width + iota((model, width), 1)).astype(FLOAT).astype(BHALF)
    grad_make("l", (k.mid16[...], dot_nn(k.gtr[...], pick).astype(BHALF)), (k.gtm[...], k.att_t[0, c]))
    j_l = grad_open("l")
    d_copies = []
    for b in range(2):
        for copies in g_copies:
            arrived(copies[b])
            value = attend_back_all(
            k.q_pos[b].reshape(span, 3 * width), k.g_pos[b].reshape(span, width), k.p_t, b * heads
        )
        k.d_pos[b] = value.reshape(every, HALF, 3 * width)
        d_copies += gather(b, k.d_pos, k.d_recv)
    j_s = grad_near(j_s)
    cls_parts = [sum(onehot[f][i] * cls_in[f] for f in range(frames)) for i in range(clips)]
    v_s = vectors_send(1, add_all(sums) + s_rows + cls_parts)
    t_rows = [col_sums(k.gtm), col_sums(k.gtr)]
    o_last = [sum_close(1, f, o_sum[f]) for f in range(frames)]
    m_vec = vectors_close(0, v_m)
    k.o_vec[0:8, :] = m_vec
    m_db = vec("m_db")
    for f in range(frames):
        r = frame(f)
        o_last[f].wait_recv()
        out = k.x32[r, :] + rows_of(k.total, 1, r) + m_db
        k.o_blk[:, f, :] = out[:patches].astype(BHALF)
        if f == 0:
            k.o_cls[...] = out[patches : patches + clips].astype(BHALF)
    grad_close(j_dn)
    grad_close(j_up)
    j_l = grad_near(j_l)
    arrived(d_copies)
    t_sum, shared = [], []
    for f in range(frames):
        k.dtq[frame(f), :] = gathered(f, k.d_recv)
        t_sum.append(sum_open(3, f, k.dtq, k.w_ti, dot_nn))
    grad_make("ta", (k.n_t[...], k.dtq[:, : 2 * width]))
    j_ta = grad_open("ta")
    for f in range(frames):
        g = rows_of(k.part, 3, frame(f))
        shared.append((column_sum(g * k.xh_t[frame(f), :]), column_sum(g)))
        t_sum[f] = sum_across(3, f, t_sum[f])
    grad_make("tb", (k.n_t[...], k.dtq[:, 2 * width :]))
    j_tb = grad_open("tb")
    v_t = vectors_send(2, add_all(shared) + [t_rows[0], col_sums(k.dtq), t_rows[1]])
    j_s = grad_far(j_s)
    s_vec = vectors_close(1, v_s)
    k.o_vec[8:16, :] = s_vec + jnp.concatenate([jnp.zeros((4, model), FLOAT), k.gcm[0:4, :]], axis=0)
    j_l = grad_far(j_l)
    j_ta = grad_near(j_ta)
    t_last = [sum_close(3, 0, t_sum[0])]
    t_vec = vectors_close(2, v_t)
    k.v_head[h] = t_vec
    h_copies = [send(k.v_head.at[h], k.v_head.at[h], d, k.v_head.at[d[1]]) for d in (sister, across, diagonal)]
    t_last += [sum_close(3, f, t_sum[f]) for f in range(1, frames)]
    for f in range(frames):
        r = frame(f)
        t_last[f].wait_recv()
        if f == 0:
            j_tb = grad_near(j_tb)
        dx, _ = norm_back(3, 0, t_gain, k.xh_t, r, False)
        out = k.gr32[r, :] + dx.astype(BHALF).astype(FLOAT)
        k.o_tok[:, f, :] = out[:patches].astype(BHALF)
    j_ta = grad_far(j_ta)
    j_tb = grad_far(j_tb)
    grad_close(j_s)
    grad_close(j_l)
    arrived(h_copies)
    over_head = k.v_head[0] + k.v_head[1] + k.v_head[2] + k.v_head[3]
    k.o_vec[16:24, :] = jnp.concatenate([over_head[0:2], t_vec[2:8]], axis=0)
    grad_close(j_ta)
    grad_close(j_tb)
    for copy in unsent:
        copy.wait_send()


def finish_kernel(dims, h_blk, h_tok, vec, cls_out, g_dn, g_up, g_s, g_l, g_ta, g_tb, *refs):
    width, model, seq = dims["width"], dims["model"], dims["seq"]
    share, clips = model // seq, dims["clips"]
    o_blk, o_cls, o_tok, cls, tg, tb, ti, tp, to, tob, tl, tlb, sg, sb, si, sp, so, sob, mg, mb, up, ub, dn, db = refs
    o_blk[...] = h_blk[...]
    o_tok[...] = h_tok[...]
    s = lax.axis_index("seq")
    v = vec[...]
    mine = pltpu.roll(v, (model - share * s) % model, 1)[:, :share]
    for out, row in ((mg, 0), (sg, 8), (tg, 16)):
        out[...] = mine[row : row + 1].reshape(share)
    for out, row in ((mb, 1), (ub, 2), (db, 3), (sb, 9), (sob, 10), (tb, 17), (tob, 18), (tlb, 20)):
        out[...] = v[row : row + 1].reshape(model)
    cls[...] = mine[12 : 12 + clips]
    o_cls[...] = cls_out[...]
    for out, row in ((sp, 11), (tp, 19)):
        out[0:1, :] = v[row : row + 1, :width]
        out[1:2, :] = v[row : row + 1, 2 * width : 3 * width]
    for i in range(3):
        si[i] = g_s[:, i * width : (i + 1) * width]
    ti[0], ti[1], ti[2] = g_ta[:, :width], g_ta[:, width:], g_tb[...]
    tl[...] = g_l[:, :width]
    up[...] = g_up[...]
    dn[...] = g_dn[...]
    to[...] = g_l[:, width:].T
    so[...] = g_s[:, 3 * width :].T


def fused_body(
    tokens,
    cls_tokens,
    clip_lengths,
    time_gain,
    time_beta,
    time_proj_in,
    time_qv_bias,
    time_proj_out,
    time_out_bias,
    time_linear,
    time_linear_bias,
    space_gain,
    space_beta,
    space_proj_in,
    space_qv_bias,
    space_proj_out,
    space_out_bias,
    mlp_gain,
    mlp_beta,
    mlp_up,
    mlp_up_bias,
    mlp_down,
    mlp_down_bias,
    out_grad,
    cls_grad,
):
    frames, patches, model = tokens.shape
    seq = lax.axis_size("seq")
    width, hidden, clips = time_proj_in.shape[2], mlp_up.shape[1], clip_lengths.shape[0]
    dims = dict(
        frames=frames,
        patches=patches,
        model=model,
        seq=seq,
        width=width,
        hidden=hidden,
        clips=clips,
        pos=-(-patches // seq),
    )

    def frames_inner(v):
        return jnp.transpose(v, (1, 0, 2))

    def outputs_first(v):
        return jnp.transpose(v, (1, 2, 0)).reshape(3 * width, model)

    scratch = scratch_shapes(dims)
    grads = grad_columns(dims)
    share = model // seq
    shape = jax.ShapeDtypeStruct
    vmem, anywhere = pl.BlockSpec(memory_space=pltpu.VMEM), pl.BlockSpec(memory_space=pl.ANY)
    inner = (patches, frames, model)
    outs = [
        shape(inner, BHALF),
        shape(cls_tokens.shape, BHALF),
        shape(inner, BHALF),
        shape((24, model), FLOAT),
    ] + [shape((share, columns), FLOAT) for _, columns in grads]
    names = list(INPUTS) + list(OUTPUTS) + ["o_" + name for name, _ in grads] + list(scratch)
    results = pl.pallas_call(
        functools.partial(layer_kernel, dims, names),
        out_shape=outs,
        in_specs=[pl.BlockSpec(memory_space=pltpu.SMEM)] + [vmem] * 2 + [anywhere] * (len(INPUTS) - 3),
        out_specs=[vmem] * len(outs),
        scratch_shapes=list(scratch.values()),
        compiler_params=pltpu.CompilerParams(
            collective_id=0, has_side_effects=True, vmem_limit_bytes=62 * 1024 * 1024
        ),
        name="layer",
    )(
        clip_lengths,
        cls_tokens,
        cls_grad,
        time_gain,
        time_beta,
        time_out_bias,
        time_linear_bias,
        space_gain,
        space_beta,
        space_out_bias,
        mlp_gain,
        mlp_beta,
        mlp_down_bias,
        mlp_up_bias,
        time_qv_bias,
        space_qv_bias,
        frames_inner(tokens),
        frames_inner(out_grad),
        outputs_first(time_proj_in),
        time_proj_out,
        time_linear,
        outputs_first(space_proj_in),
        space_proj_out,
        mlp_up,
        mlp_down,
    )
    blk, cls_out, tok, vectors = results[:4]
    row, gain = shape((model,), FLOAT), shape((share,), FLOAT)
    proj, pair = shape((3, share, width), FLOAT), shape((2, width), FLOAT)
    out_shape = [
        shape(inner, BHALF),
        shape(cls_tokens.shape, BHALF),
        shape(inner, BHALF),
        shape((clips, share), FLOAT),
        gain,
        row,
        proj,
        pair,
        shape((width, share), FLOAT),
        row,
        shape((share, width), FLOAT),
        row,
        gain,
        row,
        proj,
        pair,
        shape((width, share), FLOAT),
        row,
        gain,
        row,
        shape((share, hidden), FLOAT),
        shape((hidden,), FLOAT),
        shape((share, hidden), FLOAT),
        row,
    ]
    last = pl.pallas_call(
        functools.partial(finish_kernel, dims),
        out_shape=out_shape,
        in_specs=[vmem] * 10,
        out_specs=[vmem] * len(out_shape),
        compiler_params=pltpu.CompilerParams(vmem_limit_bytes=62 * 1024 * 1024),
        name="finish",
    )(blk, tok, vectors, cls_out, *results[4:])
    last = list(last)
    for i in (0, 2, 6, 14):
        last[i] = jnp.transpose(last[i], (1, 0, 2))
    last[22] = last[22].T
    return tuple(last)


def solution(mesh):
    placed = (
        P("seq", None, None),
        P(),
        P(),
        P(),
        P(),
        P(None, None, "head"),
        P(None, "head"),
        P("head", None),
        P(),
        P(),
        P(),
        P(),
        P(),
        P(None, None, "head"),
        P(None, "head"),
        P("head", None),
        P(),
        P(),
        P(),
        P(None, "head"),
        P("head"),
        P("head", None),
        P(),
        P("seq", None, None),
        P(),
    )
    fused = mesh.shape["seq"] == 8 and mesh.shape["head"] == 4
    return jax.shard_map(
        fused_body if fused else body,
        mesh=mesh,
        in_specs=placed,
        out_specs=(
            P("seq", None, None),
            P(),
            P("seq", None, None),
            P(None, "seq"),
            P("seq"),
            P(),
            P("seq", None, "head"),
            P(None, "head"),
            P("head", "seq"),
            P(),
            P("seq", "head"),
            P(),
            P("seq"),
            P(),
            P("seq", None, "head"),
            P(None, "head"),
            P("head", "seq"),
            P(),
            P("seq"),
            P(),
            P("seq", "head"),
            P("head"),
            P("head", "seq"),
            P(),
        ),
        check_vma=False,
    )
```

```python
import functools

import jax
import jax.numpy as jnp
from jax import lax
from jax.experimental import pallas as pl
from jax.experimental.pallas import tpu as pltpu
from jax.sharding import PartitionSpec as P

HEAD_DIM = 64
PATCH = 196
MAXLEN = 8


EPS = 1e-06
NEG = -1e30
FLOAT = jnp.float32
BHALF = jnp.bfloat16


def matmul_plain(left, right):
    return jnp.dot(left, right, preferred_element_type=FLOAT)


def matmul_tn(left, right):
    return lax.dot_general(left, right, (((0,), (0,)), ((), ())), preferred_element_type=FLOAT)


def matmul_nt(left, right):
    return lax.dot_general(left, right, (((1,), (1,)), ((), ())), preferred_element_type=FLOAT)


def exact_tn(left, right):
    return lax.dot_general(
        left,
        right,
        (((0,), (0,)), ((), ())),
        precision=lax.Precision.HIGHEST,
        preferred_element_type=FLOAT,
    )


def exact_nn(left, right):
    return jnp.dot(left, right, precision=lax.Precision.HIGHEST, preferred_element_type=FLOAT)


def layer_norm(rows, gain, shift):
    center = rows - jnp.mean(rows, axis=-1, keepdims=True)
    invstd = lax.rsqrt(jnp.mean(center * center, axis=-1, keepdims=True) + EPS)
    normed = center * invstd
    return (normed * gain + shift, normed, invstd)


def norm_back(grad_out, gain, normed, invstd, row_weight):
    feature_count = grad_out.shape[-1]
    grad_norm = grad_out * gain
    weighted = grad_out * row_weight
    gain_grad = jnp.sum((weighted * normed).reshape(-1, feature_count), axis=0)
    shift_grad = jnp.sum(weighted.reshape(-1, feature_count), axis=0)
    first_mean = jnp.mean(grad_norm, axis=-1, keepdims=True)
    second_mean = jnp.mean(grad_norm * normed, axis=-1, keepdims=True)
    return (invstd * (grad_norm - first_mean - normed * second_mean), gain_grad, shift_grad)


def qkv_shift(pair):
    return jnp.stack([pair[0], jnp.zeros_like(pair[0]), pair[1]], axis=0).reshape(-1)


def pair_sums(grad_qkv, local_width):
    sums = jnp.sum(grad_qkv.astype(FLOAT).reshape(-1, 3, local_width), axis=0)
    return jnp.stack([sums[0], sums[2]], axis=0)


def gelu_slope(pre):
    normal_cdf = 0.5 * (1.0 + jax.scipy.special.erf(pre * 0.7071067811865476))
    return normal_cdf + pre * jnp.exp(-0.5 * pre * pre) * 0.3989422804014327


def band_stack(values, band_reach):
    frames = values.shape[0]
    padded = jnp.pad(values, ((band_reach, band_reach),) + ((0, 0),) * (values.ndim - 1))
    return jnp.stack(
        [padded[offset : offset + frames] for offset in range(2 * band_reach + 1)], axis=2
    )


def band_return(contrib, band_reach):
    frames = contrib.shape[0]
    padded = jnp.pad(contrib, ((band_reach, band_reach),) + ((0, 0),) * (contrib.ndim - 1))
    total = jnp.zeros((frames,) + contrib.shape[1:2] + contrib.shape[3:], FLOAT)
    for offset in range(2 * band_reach + 1):
        start = 2 * band_reach - offset
        total = total + padded[start : start + frames, :, offset]
    return total


def to_positions(frame_major):
    frames_dev, patches, columns = frame_major.shape
    seq_count = lax.axis_size("seq")
    pos_dev = (patches + seq_count - 1) // seq_count
    padded = jnp.pad(frame_major, ((0, 0), (0, pos_dev * seq_count - patches), (0, 0)))
    moved = lax.all_to_all(
        padded.reshape(frames_dev, seq_count, pos_dev, columns),
        "seq",
        split_axis=1,
        concat_axis=0,
        tiled=True,
    )
    return moved.reshape(frames_dev * seq_count, pos_dev, columns)


def to_frames(pos_major):
    frames_all, pos_dev, columns = pos_major.shape
    seq_count = lax.axis_size("seq")
    moved = lax.all_to_all(
        pos_major.reshape(frames_all, 1, pos_dev, columns),
        "seq",
        split_axis=0,
        concat_axis=1,
        tiled=True,
    )
    return moved.reshape(frames_all // seq_count, seq_count * pos_dev, columns)[:, :PATCH]


def head_cols(pieces):
    return lax.all_gather(pieces, "head", axis=2, tiled=True)


def time_scores(queries, key_band, valid, score_scale):
    raw = (
        jnp.einsum("fphd,fpohd->fpho", queries, key_band, preferred_element_type=FLOAT)
        * score_scale
    )
    return jnp.where(valid[:, None, None, :], raw, NEG)


def time_forward(queries, key_band, value_band, valid, score_scale):
    scores = time_scores(queries, key_band, valid, score_scale)
    largest = jnp.max(scores, axis=-1, keepdims=True)
    exponent = jnp.exp(scores - largest)
    totals = jnp.sum(exponent, axis=-1, keepdims=True)
    attend = (exponent / totals).astype(BHALF)
    result = jnp.einsum("fpho,fpohd->fphd", attend, value_band, preferred_element_type=FLOAT)
    return (result, largest + jnp.log(totals))


def time_backward(
    queries, key_band, value_band, valid, log_total, grad_out, score_scale, band_reach
):
    scores = time_scores(queries, key_band, valid, score_scale)
    attend = jnp.exp(scores - log_total)
    grad_attend = jnp.einsum("fphd,fpohd->fpho", grad_out, value_band, preferred_element_type=FLOAT)
    row_dot = jnp.sum(attend * grad_attend, axis=-1, keepdims=True)
    grad_score = (attend * (grad_attend - row_dot)).astype(BHALF)
    grad_query = (
        jnp.einsum("fpho,fpohd->fphd", grad_score, key_band, preferred_element_type=FLOAT)
        * score_scale
    )
    key_part = (
        jnp.einsum("fpho,fphd->fpohd", grad_score, queries, preferred_element_type=FLOAT)
        * score_scale
    )
    value_part = jnp.einsum(
        "fpho,fphd->fpohd", attend.astype(BHALF), grad_out, preferred_element_type=FLOAT
    )
    return (grad_query, band_return(key_part, band_reach), band_return(value_part, band_reach))


def space_forward(queries, key_rows, value_rows, score_scale):
    scores = (
        jnp.einsum("fqhd,fkhd->fhqk", queries, key_rows, preferred_element_type=FLOAT) * score_scale
    )
    largest = jnp.max(scores, axis=-1, keepdims=True)
    exponent = jnp.exp(scores - largest)
    totals = jnp.sum(exponent, axis=-1, keepdims=True)
    attend = (exponent / totals).astype(BHALF)
    result = jnp.einsum("fhqk,fkhd->fqhd", attend, value_rows, preferred_element_type=FLOAT)
    return (result, largest + jnp.log(totals))


def space_backward(queries, key_rows, value_rows, log_total, grad_out, score_scale):
    scores = (
        jnp.einsum("fqhd,fkhd->fhqk", queries, key_rows, preferred_element_type=FLOAT) * score_scale
    )
    attend = jnp.exp(scores - log_total)
    grad_attend = jnp.einsum("fqhd,fkhd->fhqk", grad_out, value_rows, preferred_element_type=FLOAT)
    row_dot = jnp.sum(attend * grad_attend, axis=-1, keepdims=True)
    grad_score = (attend * (grad_attend - row_dot)).astype(BHALF)
    grad_query = (
        jnp.einsum("fhqk,fkhd->fqhd", grad_score, key_rows, preferred_element_type=FLOAT)
        * score_scale
    )
    grad_key = (
        jnp.einsum("fhqk,fqhd->fkhd", grad_score, queries, preferred_element_type=FLOAT)
        * score_scale
    )
    grad_value = jnp.einsum(
        "fhqk,fqhd->fkhd", attend.astype(BHALF), grad_out, preferred_element_type=FLOAT
    )
    return (grad_query, grad_key, grad_value)


def body(
    tokens,
    cls_tokens,
    clip_lengths,
    time_gain,
    time_beta,
    time_proj_in,
    time_qv_bias,
    time_proj_out,
    time_out_bias,
    time_linear,
    time_linear_bias,
    space_gain,
    space_beta,
    space_proj_in,
    space_qv_bias,
    space_proj_out,
    space_out_bias,
    mlp_gain,
    mlp_beta,
    mlp_up,
    mlp_up_bias,
    mlp_down,
    mlp_down_bias,
    out_grad,
    cls_grad,
):
    frames_dev, patches, model_width = tokens.shape
    seq_count = lax.axis_size("seq")
    frames_all = frames_dev * seq_count
    clip_count = clip_lengths.shape[0]
    local_width = time_proj_in.shape[2]
    local_heads = local_width // HEAD_DIM
    band_reach = MAXLEN - 1
    score_scale = HEAD_DIM ** (-0.5)
    seq_rank = lax.axis_index("seq")
    head_rank = lax.axis_index("head")
    clip_ends = jnp.sum(
        jnp.where(jnp.tri(clip_lengths.shape[0], dtype=bool), clip_lengths[None, :], 0), axis=1
    )
    frame_ids = jnp.arange(frames_all, dtype=jnp.int32)
    clip_of = jnp.sum((frame_ids[:, None] >= clip_ends[None, :]).astype(jnp.int32), axis=1)
    clip_pad = jnp.pad(clip_of, (band_reach, band_reach), constant_values=-1)
    valid = jnp.stack(
        [clip_pad[offset : offset + frames_all] == clip_of for offset in range(2 * band_reach + 1)],
        axis=1,
    )
    local_clip = lax.dynamic_slice_in_dim(clip_of, seq_rank * frames_dev, frames_dev)
    onehot = (local_clip[:, None] == jnp.arange(clip_count, dtype=jnp.int32)[None, :]).astype(FLOAT)
    lengths = clip_lengths.astype(FLOAT)
    time_in = to_positions(tokens)
    pos_dev = time_in.shape[1]
    time_rows = frames_all * pos_dev
    time_normed, time_stat, time_inv = layer_norm(time_in.astype(FLOAT), time_gain, time_beta)
    time_normed = time_normed.astype(BHALF).reshape(time_rows, model_width)
    time_in_mat = time_proj_in.reshape(model_width, 3 * local_width)
    time_qkv = (
        (matmul_plain(time_normed, time_in_mat) + qkv_shift(time_qv_bias))
        .astype(BHALF)
        .reshape(frames_all, pos_dev, 3, local_heads, HEAD_DIM)
    )
    time_query = time_qkv[:, :, 0]
    time_keys = band_stack(time_qkv[:, :, 1], band_reach)
    time_values = band_stack(time_qkv[:, :, 2], band_reach)
    time_att, time_log = time_forward(time_query, time_keys, time_values, valid, score_scale)
    time_att = time_att.astype(BHALF).reshape(time_rows, local_width)
    time_mid = (
        lax.psum(matmul_plain(time_att, time_proj_out).astype(jnp.bfloat16), "head").astype(
            jnp.float32
        )
        + time_out_bias
    ).astype(BHALF)
    col_start = head_rank * local_width
    linear_cols = lax.dynamic_slice_in_dim(time_linear, col_start, local_width, 1)
    linear_shift = lax.dynamic_slice_in_dim(time_linear_bias, col_start, local_width)
    time_part = (
        (matmul_plain(time_mid, linear_cols) + linear_shift)
        .astype(BHALF)
        .reshape(frames_all, pos_dev, local_width)
    )
    time_res = to_frames(head_cols(time_part))
    mid = tokens.astype(FLOAT) + time_res.astype(FLOAT)
    span_rows = patches + 1
    space_rows = frames_dev * span_rows
    cls_rows = matmul_plain(onehot.astype(BHALF), cls_tokens)
    space_in = jnp.concatenate([cls_rows[:, None, :], mid], axis=1)
    space_normed, space_stat, space_inv = layer_norm(space_in, space_gain, space_beta)
    space_normed = space_normed.astype(BHALF).reshape(space_rows, model_width)
    space_in_mat = space_proj_in.reshape(model_width, 3 * local_width)
    space_qkv = (
        (matmul_plain(space_normed, space_in_mat) + qkv_shift(space_qv_bias))
        .astype(BHALF)
        .reshape(frames_dev, span_rows, 3, local_heads, HEAD_DIM)
    )
    space_query = space_qkv[:, :, 0]
    space_keys = space_qkv[:, :, 1]
    space_values = space_qkv[:, :, 2]
    space_att, space_log = space_forward(space_query, space_keys, space_values, score_scale)
    space_att = space_att.astype(BHALF).reshape(space_rows, local_width)
    space_sum = (
        lax.psum(matmul_plain(space_att, space_proj_out).astype(jnp.bfloat16), "head").astype(
            jnp.float32
        )
        + space_out_bias
    ).reshape(frames_dev, span_rows, model_width)
    after = mid + space_sum[:, 1:]
    cls_part = exact_tn(onehot, space_sum[:, 0])
    cls_mid = cls_tokens.astype(FLOAT) + lax.psum(cls_part, "seq") / lengths[:, None]
    tok_rows = frames_dev * patches
    rows = jnp.concatenate([after.reshape(tok_rows, model_width), cls_mid], axis=0)
    mlp_normed, mlp_stat, mlp_inv = layer_norm(rows, mlp_gain, mlp_beta)
    mlp_normed = mlp_normed.astype(BHALF)
    pre = matmul_plain(mlp_normed, mlp_up) + mlp_up_bias
    act = jax.nn.gelu(pre, approximate=False).astype(BHALF)
    result = (
        rows
        + lax.psum(matmul_plain(act, mlp_down).astype(jnp.bfloat16), "head").astype(jnp.float32)
        + mlp_down_bias
    )
    block_out = result[:tok_rows].reshape(frames_dev, patches, model_width).astype(BHALF)
    cls_out = result[tok_rows:].astype(BHALF)
    first_seq = (seq_rank == 0).astype(FLOAT)
    keep_rows = jnp.concatenate(
        [jnp.ones((tok_rows, 1), FLOAT), jnp.ones((clip_count, 1), FLOAT) * first_seq], axis=0
    )
    keep_half = keep_rows.astype(BHALF)
    grad_rows = jnp.concatenate([out_grad.reshape(tok_rows, model_width), cls_grad], axis=0)
    down_grad = matmul_tn(act * keep_half, grad_rows)
    down_shift_grad = jnp.sum(grad_rows.astype(FLOAT) * keep_rows, axis=0)
    grad_pre = (matmul_nt(grad_rows, mlp_down) * gelu_slope(pre)).astype(BHALF)
    up_grad = matmul_tn(mlp_normed * keep_half, grad_pre)
    up_shift_grad = jnp.sum(grad_pre.astype(FLOAT) * keep_rows, axis=0)
    grad_mlp_norm = lax.psum(matmul_nt(grad_pre, mlp_up).astype(jnp.bfloat16), "head").astype(
        jnp.float32
    )
    grad_mlp_in, mlp_gain_grad, mlp_beta_grad = norm_back(
        grad_mlp_norm, mlp_gain, mlp_stat, mlp_inv, keep_rows
    )
    grad_total = grad_rows.astype(FLOAT) + grad_mlp_in
    grad_after = grad_total[:tok_rows].reshape(frames_dev, patches, model_width)
    grad_cls_mid = grad_total[tok_rows:]
    cls_share = exact_nn(onehot, grad_cls_mid / lengths[:, None])
    grad_space_sum = (
        jnp.concatenate([cls_share[:, None, :], grad_after], axis=1)
        .astype(BHALF)
        .reshape(space_rows, model_width)
    )
    space_out_grad = matmul_tn(space_att, grad_space_sum)
    space_shift_grad = jnp.sum(grad_space_sum.astype(FLOAT), axis=0)
    grad_space_att = (
        matmul_nt(grad_space_sum, space_proj_out)
        .astype(BHALF)
        .reshape(frames_dev, span_rows, local_heads, HEAD_DIM)
    )
    space_grad_query, space_grad_key, space_grad_value = space_backward(
        space_query, space_keys, space_values, space_log, grad_space_att, score_scale
    )
    grad_space_qkv = (
        jnp.stack([space_grad_query, space_grad_key, space_grad_value], axis=2)
        .astype(BHALF)
        .reshape(space_rows, 3 * local_width)
    )
    space_in_grad = matmul_tn(space_normed, grad_space_qkv).reshape(model_width, 3, local_width)
    space_pair_grad = pair_sums(grad_space_qkv, local_width)
    grad_space_norm = (
        lax.psum(matmul_nt(grad_space_qkv, space_in_mat).astype(jnp.bfloat16), "head")
        .astype(jnp.float32)
        .reshape(frames_dev, span_rows, model_width)
    )
    grad_space_in, space_gain_grad, space_beta_grad = norm_back(
        grad_space_norm, space_gain, space_stat, space_inv, 1.0
    )
    grad_mid = grad_after + grad_space_in[:, 1:]
    cls_in_part = exact_tn(onehot, grad_space_in[:, 0])
    grad_time_res = to_positions(grad_mid.astype(BHALF)).reshape(time_rows, model_width)
    linear_grad = matmul_tn(
        time_mid, lax.dynamic_slice_in_dim(grad_time_res, col_start, local_width, 1)
    )
    linear_shift_grad = jnp.sum(grad_time_res.astype(FLOAT), axis=0)
    grad_time_mid = matmul_nt(grad_time_res, time_linear).astype(BHALF)
    time_out_grad = matmul_tn(time_att, grad_time_mid)
    time_shift_grad = jnp.sum(grad_time_mid.astype(FLOAT), axis=0)
    grad_time_att = (
        matmul_nt(grad_time_mid, time_proj_out)
        .astype(BHALF)
        .reshape(frames_all, pos_dev, local_heads, HEAD_DIM)
    )
    time_grad_query, time_grad_key, time_grad_value = time_backward(
        time_query, time_keys, time_values, valid, time_log, grad_time_att, score_scale, band_reach
    )
    grad_time_qkv = (
        jnp.stack([time_grad_query, time_grad_key, time_grad_value], axis=2)
        .astype(BHALF)
        .reshape(time_rows, 3 * local_width)
    )
    time_in_grad = matmul_tn(time_normed, grad_time_qkv).reshape(model_width, 3, local_width)
    time_pair_grad = pair_sums(grad_time_qkv, local_width)
    grad_time_norm = (
        lax.psum(matmul_nt(grad_time_qkv, time_in_mat).astype(jnp.bfloat16), "head")
        .astype(jnp.float32)
        .reshape(frames_all, pos_dev, model_width)
    )
    grad_time_in, time_gain_grad, time_beta_grad = norm_back(
        grad_time_norm, time_gain, time_stat, time_inv, 1.0
    )
    grad_tokens_time = to_frames(grad_time_in.astype(BHALF))
    tokens_grad = (grad_mid + grad_tokens_time.astype(FLOAT)).astype(BHALF)
    summed = (
        lax.psum_scatter(time_gain_grad, "seq", scatter_dimension=0, tiled=True),
        lax.psum_scatter(time_in_grad, "seq", scatter_dimension=0, tiled=True),
        lax.psum_scatter(time_out_grad, "seq", scatter_dimension=1, tiled=True),
        lax.psum_scatter(linear_grad, "seq", scatter_dimension=0, tiled=True),
        lax.psum_scatter(space_gain_grad, "seq", scatter_dimension=0, tiled=True),
        lax.psum_scatter(space_in_grad, "seq", scatter_dimension=0, tiled=True),
        lax.psum_scatter(space_out_grad, "seq", scatter_dimension=1, tiled=True),
        lax.psum_scatter(mlp_gain_grad, "seq", scatter_dimension=0, tiled=True),
        lax.psum_scatter(up_grad, "seq", scatter_dimension=0, tiled=True),
        lax.psum_scatter(down_grad, "seq", scatter_dimension=1, tiled=True),
        lax.psum_scatter(cls_in_part, "seq", scatter_dimension=1, tiled=True),
    )
    shifts = lax.psum(
        (
            time_beta_grad,
            time_pair_grad,
            time_shift_grad,
            linear_shift_grad,
            space_beta_grad,
            space_pair_grad,
            space_shift_grad,
            mlp_beta_grad,
            up_shift_grad,
            down_shift_grad,
        ),
        "seq",
    )
    col_width = model_width // seq_count
    cls_direct = lax.dynamic_slice_in_dim(grad_cls_mid, seq_rank * col_width, col_width, 1)
    cls_tokens_grad = summed[10] + cls_direct
    return (
        block_out,
        cls_out,
        tokens_grad,
        cls_tokens_grad,
        summed[0],
        shifts[0],
        summed[1],
        shifts[1],
        summed[2],
        shifts[2],
        summed[3],
        shifts[3],
        summed[4],
        shifts[4],
        summed[5],
        shifts[5],
        summed[6],
        shifts[6],
        summed[7],
        shifts[7],
        summed[8],
        shifts[8],
        summed[9],
        shifts[9],
    )


MESH = pl.DeviceIdType.MESH
ROWS = 208
HALF = 16
SLOTS = 2 * HALF


def dot_nn(left, right):
    return jnp.dot(left, right, preferred_element_type=FLOAT)


def dot_nt(left, right):
    return lax.dot_general(left, right, (((1,), (1,)), ((), ())), preferred_element_type=FLOAT)


def dot_tn(left, right):
    return lax.dot_general(left, right, (((0,), (0,)), ((), ())), preferred_element_type=FLOAT)


def iota(shape, axis):
    return lax.broadcasted_iota(jnp.int32, shape, axis)


def scratch_shapes(dims):
    frames, seq, width, model, hidden = dims["frames"], dims["seq"], dims["width"], dims["model"], dims["hidden"]
    rows, every, heads = frames * ROWS, frames * seq, width // HEAD_DIM
    half, low = model // 2, BHALF
    vm = pltpu.VMEM
    shapes = dict(
        tok=vm((dims["patches"], frames, model), low),
        out_grad=vm((dims["patches"], frames, model), low),
        w_ti=vm((3 * width, model), low),
        w_si=vm((3 * width, model), low),
        w_tl=vm((model, model), low),
        w_up=vm((model, hidden), low),
        w_dn=vm((hidden, model), low),
        w_to=vm((2, 2, width, model), low),
        w_so=vm((2, 2, width, model), low),
        x32=vm((rows, model), FLOAT),
        gr32=vm((rows, model), FLOAT),
        t32=vm((rows, model), FLOAT),
        u32=vm((rows, model), FLOAT),
        dact=vm((rows, hidden), FLOAT),
        xh_t=vm((rows, model), FLOAT),
        xh_s=vm((rows, model), FLOAT),
        xh_m=vm((rows, model), FLOAT),
        inv=vm((3, rows, 128), FLOAT),
        n_t=vm((rows, model), low),
        n_s=vm((rows, model), low),
        n_m=vm((rows, model), low),
        gr16=vm((rows, model), low),
        mid16=vm((rows, model), low),
        act=vm((rows, hidden), low),
        act_k=vm((rows, hidden), low),
        gpre=vm((rows, hidden), low),
        gpre_k=vm((rows, hidden), low),
        gss=vm((rows, model), low),
        gtr=vm((rows, model), low),
        gtm=vm((rows, model), low),
        sqkv=vm((rows, 3 * width), low),
        dsq=vm((rows, 3 * width), low),
        dtq=vm((rows, 3 * width), low),
        gatt=vm((rows, width), low),
        sel=vm((seq * SLOTS, ROWS), low),
        les=vm((ROWS, seq * SLOTS), low),
        tmask=vm((every * HALF, every * HALF), FLOAT),
        p_t=vm((2 * heads, every * HALF, every * HALF), FLOAT),
        p_s=vm((frames * heads, ROWS, ROWS), FLOAT),
        q_send=vm((frames, seq, 2, HALF, 3 * width), low),
        q_pos=vm((2, every, HALF, 3 * width), low),
        a_pos=vm((2, every, HALF, width), low),
        a_recv=vm((2, seq, frames, HALF, width), low),
        g_send=vm((frames, seq, 2, HALF, width), low),
        g_pos=vm((2, every, HALF, width), low),
        d_pos=vm((2, every, HALF, 3 * width), low),
        d_recv=vm((2, seq, frames, HALF, 3 * width), low),
        att_t=vm((2, 2, rows, width), low),
        att_s=vm((2, 2, rows, width), low),
        part=vm((4, 2, rows, half), low),
        pair=vm((4, rows, half), low),
        other=vm((4, rows, half), low),
        total=vm((4, 2, rows, half), low),
        cls_send=vm((8, width), FLOAT),
        cls_recv=vm((seq, 8, width), FLOAT),
        cls_head=vm((4, 8, model), FLOAT),
        gcm=vm((8, model), FLOAT),
        v_send=vm((3, 8, model), FLOAT),
        v_recv=vm((3, seq, 8, model), FLOAT),
        v_head=vm((4, 8, model), FLOAT),
    )
    for name, columns in grad_columns(dims):
        share = model // seq
        shapes["g_" + name] = vm((seq // 4, 2, 2, share, columns), low)
        shapes["y_" + name] = vm((2, seq // 4, share, columns), low)
        shapes["z_" + name] = vm((seq // 4, share, columns), low)
        shapes["x_" + name] = vm((share, columns), low)
    for name in VECTORS:
        shapes[name] = vm((hidden if name == "m_ub" else model,), FLOAT)
    for name in PAIRS:
        shapes[name] = vm((2, width), FLOAT)
    shapes["load"] = pltpu.SemaphoreType.DMA((32,))
    shapes["sent"] = pltpu.SemaphoreType.DMA((320,))
    shapes["got"] = pltpu.SemaphoreType.DMA((320,))
    return shapes


def grad_columns(dims):
    width, model, hidden = dims["width"], dims["model"], dims["hidden"]
    return (
        ("dn", hidden),
        ("up", hidden),
        ("s", 4 * width),
        ("l", 2 * width),
        ("ta", 2 * width),
        ("tb", width),
    )


VECTORS = ("t_gain", "t_beta", "t_ob", "t_lb", "s_gain", "s_beta", "s_ob", "m_gain", "m_beta", "m_db", "m_ub")
PAIRS = ("t_qv", "s_qv")
MATRICES = ("tok", "out_grad", "w_ti", "w_to", "w_tl", "w_si", "w_so", "w_up", "w_dn")
INPUTS = ("lens", "cls", "cls_grad") + tuple("h_" + name for name in VECTORS + PAIRS + MATRICES)
OUTPUTS = ("o_blk", "o_cls", "o_tok", "o_vec")


class Refs:
    pass


class Exchange:
    def __init__(self, out, into):
        self.wait_send, self.wait_recv = out.wait_send, into.wait_recv


def layer_kernel(dims, names, *refs):
    k = Refs()
    for name, ref in zip(names, refs):
        setattr(k, name, ref)
    frames, seq, width, model, hidden = dims["frames"], dims["seq"], dims["width"], dims["model"], dims["hidden"]
    patches, clips, pos = dims["patches"], dims["clips"], dims["pos"]
    rows, every, heads, half = frames * ROWS, frames * seq, width // HEAD_DIM, model // 2
    zs = seq // 2
    share_rows = model // seq
    scale = HEAD_DIM ** (-0.5)
    s, h = lax.axis_index("seq"), lax.axis_index("head")
    z, y = s // 2, s % 2
    x, c = h // 2, h % 2
    other_c = 1 - c
    sister, across, diagonal = (s, x * 2 + other_c), (s, (1 - x) * 2 + c), (s, (1 - x) * 2 + other_c)
    y_peer = (z * 2 + 1 - y, h)
    peers = [((z + i) % zs) * 2 + (y + j) % 2 for i in range(zs) for j in range(2) if i or j]
    givers = [((z + zs - i) % zs) * 2 + (y + j) % 2 for i in range(zs) for j in range(2) if i or j]
    used = [0]

    def send(src, dst, device, lands):
        index = used[0]
        used[0] += 1
        sems = dict(send_sem=k.sent.at[index], recv_sem=k.got.at[index], device_id=device, device_id_type=MESH)
        copy = pltpu.make_async_remote_copy(src_ref=src, dst_ref=dst, **sems)
        copy.start()
        copy = Exchange(copy, pltpu.make_async_remote_copy(src_ref=src, dst_ref=lands, **sems))
        unsent.append(copy)
        return copy

    unsent = []
    loads = [0]

    def load(src, dst):
        copy = pltpu.make_async_copy(src, dst, k.load.at[loads[0]])
        loads[0] += 1
        copy.start()
        return copy

    places = {"w_to": k.w_to.at[0, c], "w_so": k.w_so.at[0, c]}
    order = ("tok", "t_gain", "t_beta", "w_ti", "t_qv", "w_to", "w_so", "out_grad", "w_dn") + VECTORS[2:] + ("s_qv", "w_tl", "w_si", "w_up")
    loading = {name: load(getattr(k, "h_" + name), places.get(name, getattr(k, name))) for name in order}

    def need(*wanted):
        for name in wanted:
            loading.pop(name).wait()

    barrier = pltpu.get_barrier_semaphore()
    everyone = [(p, h) for p in peers] + [sister, across, diagonal]
    for device in everyone:
        pl.semaphore_signal(barrier, inc=1, device_id=device, device_id_type=MESH)

    def vec(name):
        if name in loading:
            need(name)
        return getattr(k, name)[...].reshape(1, -1)

    def qkv_row(name):
        need(name)
        pair = getattr(k, name)
        return jnp.concatenate([pair[0:1, :], jnp.zeros((1, width), FLOAT), pair[1:2, :]], axis=-1)

    def chosen(slot, row, outer):
        if outer:
            device, place = slot // SLOTS, slot % SLOTS
        else:
            device, place = slot // HALF % seq, slot // (HALF * seq) * HALF + slot % HALF
        hit = (device * pos + place == row) & (place < pos) & (row < patches)
        return jnp.where(hit, 1.0, 0.0).astype(BHALF)

    k.sel[...] = chosen(iota((seq * SLOTS, ROWS), 0), iota((seq * SLOTS, ROWS), 1), True)
    ends = []
    for i in range(clips):
        ends.append(k.lens[i] + (ends[-1] if i else 0))

    def clip_of(frame):
        total = (frame >= ends[0]).astype(jnp.int32)
        for end in ends[1:]:
            total = total + (frame >= end).astype(jnp.int32)
        return total

    onehot = []
    for f in range(frames):
        own = clip_of(jnp.full((1, model), s * frames + f, jnp.int32))
        onehot.append([(own == i).astype(FLOAT) for i in range(clips)])
    per_len = [1.0 / jnp.full((1, model), k.lens[i], jnp.int32).astype(FLOAT) for i in range(clips)]
    cls32 = k.cls[...].astype(FLOAT)
    cls_row = [sum(onehot[f][i] * cls32[i : i + 1] for i in range(clips)) for f in range(frames)]
    tail = ROWS - patches

    def set_tail(ref, f, first):
        used_rows = sum(r.shape[0] for r in first)
        fill = [jnp.zeros((tail - used_rows, model), FLOAT)] if used_rows < tail else []
        ref[f * ROWS + patches : (f + 1) * ROWS, :] = jnp.concatenate(list(first) + fill, axis=0)

    def eight(values):
        missing = 8 - sum(v.shape[0] for v in values)
        fill = [jnp.zeros((missing, values[0].shape[1]), FLOAT)] if missing else []
        return jnp.concatenate(list(values) + fill, axis=0)

    def frame(f):
        return slice(f * ROWS, (f + 1) * ROWS)

    def norm(src, which, gain, shift, xhat, out, r):
        v = src[r, :]
        center = v - jnp.mean(v, axis=-1, keepdims=True)
        invstd = lax.rsqrt(jnp.mean(center * center, axis=-1, keepdims=True) + EPS)
        n = center * invstd
        xhat[r, :] = n
        k.inv[which, r, :] = jnp.broadcast_to(invstd, (v.shape[0], 128))
        out[r, :] = (n * gain + shift).astype(BHALF)

    def arrived(copies):
        for copy in copies:
            copy.wait_recv()

    def to_slots(f, value, src):
        moved = dot_nn(k.sel[...], value).astype(BHALF)
        src[f] = moved.reshape(seq, 2, HALF, value.shape[-1])

    def scatter(f, value, src, dst):
        to_slots(f, value, src)
        to = frames * s + f
        copies = [
            [send(src.at[f, p, b], dst.at[b, to], (p, h), dst.at[b, frames * q + f]) for p, q in zip(peers, givers)]
            for b in range(2)
        ]
        dst[:, to] = src[f, s]
        return copies

    def gather(b, src, dst):
        copies = [
            send(src.at[b, pl.ds(frames * p, frames)], dst.at[b, s], (p, h), dst.at[b, q]) for p, q in zip(peers, givers)
        ]
        dst[b, s] = src[b, pl.ds(frames * s, frames)]
        return copies

    def gathered(f, src):
        return dot_nn(k.les[...], src[:, :, f].reshape(seq * SLOTS, src.shape[-1])).astype(BHALF)

    need("tok")
    t_gain, t_beta, t_qb = vec("t_gain"), vec("t_beta"), qkv_row("t_qv")
    q_copies = []
    for f in range(frames):
        k.x32[f * ROWS : f * ROWS + patches, :] = k.tok[:, f, :].astype(FLOAT)
        set_tail(k.x32, f, [])
        norm(k.x32, 0, t_gain, t_beta, k.xh_t, k.n_t, frame(f))
        if f == 0:
            need("w_ti")
        qkv = (dot_nt(k.n_t[frame(f), :], k.w_ti[...]) + t_qb).astype(BHALF)
        if f == 0:
            pl.semaphore_wait(barrier, len(everyone))
        q_copies.append(scatter(f, qkv, k.q_send, k.q_pos))

    def share(ref):
        return (
            send(ref.at[0, c], ref.at[0, c], sister, ref.at[0, other_c]),
            send(ref.at[0, c], ref.at[1, c], across, ref.at[1, c]),
        )

    def pass_on(ref):
        return send(ref.at[1, c], ref.at[1, c], sister, ref.at[1, other_c])

    need("w_to", "w_so")
    w_to_near, w_to_far = share(k.w_to)
    w_so_near, w_so_far = share(k.w_so)

    k.les[...] = chosen(iota((ROWS, seq * SLOTS), 1), iota((ROWS, seq * SLOTS), 0), False)
    span = every * HALF
    left, right = iota((span, span), 0), iota((span, span), 1)
    same = (left % HALF == right % HALF) & (clip_of(left // HALF) == clip_of(right // HALF))
    near = jnp.abs(left // HALF - right // HALF) < MAXLEN
    k.tmask[...] = jnp.where(same & near, 0.0, NEG)
    need("out_grad")
    cls_g = k.cls_grad[...].astype(FLOAT)
    for f in range(frames):
        k.gr32[f * ROWS : f * ROWS + patches, :] = k.out_grad[:, f, :].astype(FLOAT)
        set_tail(k.gr32, f, [cls_g] if f == 0 else [])
        k.gr16[frame(f), :] = k.gr32[frame(f), :].astype(BHALF)
    need("w_dn")
    k.dact[...] = dot_nt(k.gr16[...], k.w_dn[...])
    w_to_far.wait_recv()
    w_to_last = pass_on(k.w_to)
    w_so_far.wait_recv()
    w_so_last = pass_on(k.w_so)

    def attend(q, key, value, mask, p_ref):
        scores = dot_nt(q, key) * scale + mask
        e = jnp.exp(scores - jnp.max(scores, axis=-1, keepdims=True))
        p = e * (1.0 / jnp.sum(e, axis=-1, keepdims=True))
        p_ref[...] = p
        return dot_nn(p.astype(BHALF), value).astype(BHALF)

    def attend_back(q, key, value, grad, p_ref):
        p = p_ref[...]
        grad_p = p * dot_nt(grad, value)
        grad_s = (grad_p - p * jnp.sum(grad_p, axis=-1, keepdims=True)).astype(BHALF)
        grad_q = (dot_nn(grad_s, key) * scale).astype(BHALF)
        grad_k = (dot_tn(grad_s, q) * scale).astype(BHALF)
        grad_v = dot_tn(p.astype(BHALF), grad).astype(BHALF)
        return grad_q, grad_k, grad_v

    def head_of(value, part, j):
        at = part * width + j * HEAD_DIM
        return value[:, at : at + HEAD_DIM]

    def attend_all(qkv, mask, p_ref, first):
        out = [
            attend(*[head_of(qkv, i, j) for i in range(3)], mask, p_ref.at[first + j]) for j in range(heads)
        ]
        return jnp.concatenate(out, axis=-1)

    def attend_back_all(qkv, grad, p_ref, first):
        out = [
            attend_back(*[head_of(qkv, i, j) for i in range(3)], head_of(grad, 0, j), p_ref.at[first + j])
            for j in range(heads)
        ]
        return jnp.concatenate([out[j][i] for i in range(3) for j in range(heads)], axis=-1)

    a_copies = []
    for b in range(2):
        for copies in q_copies:
            arrived(copies[b])
        out = attend_all(k.q_pos[b].reshape(span, 3 * width), k.tmask[...], k.p_t, b * heads)
        k.a_pos[b] = out.reshape(every, HALF, width)
        a_copies += gather(b, k.a_pos, k.a_recv)
    arrived(a_copies)

    def features(f, att):
        r = frame(f)
        return (
            send(att.at[0, c, r], att.at[0, c, r], sister, att.at[0, other_c, r]),
            send(att.at[0, c, r], att.at[1, c, r], across, att.at[1, c, r]),
        )

    def own_part(f, att, weight, copies):
        r = frame(f)
        copies[0].wait_recv()
        k.t32[r, :] = dot_nn(att[0, 0, r], weight[0, 0]) + dot_nn(att[0, 1, r], weight[0, 1])

    def features_on(f, att, copies):
        copies[1].wait_recv()
        r = frame(f)
        return send(att.at[1, c, r], att.at[1, c, r], sister, att.at[1, other_c, r])

    def both_parts(f, att, weight, copy):
        r = frame(f)
        copy.wait_recv()
        k.u32[r, :] = dot_nn(att[1, 0, r], weight[1, 0]) + dot_nn(att[1, 1, r], weight[1, 1])
        own, other = k.t32[r, :], k.u32[r, :]
        return jnp.where(x == 0, own, other) + jnp.where(x == 0, other, own)

    ta_copies = []
    for f in range(frames):
        k.att_t[0, c, frame(f), :] = gathered(f, k.a_recv)
        ta_copies.append(features(f, k.att_t))
    arrived([w_to_near, w_to_last])
    t_ob, t_lb, s_gain, s_beta, s_qb = vec("t_ob"), vec("t_lb"), vec("s_gain"), vec("s_beta"), qkv_row("s_qv")
    need("w_tl", "w_si")
    in_frame = jnp.where(iota((1, ROWS), 1) < patches + 1, 0.0, NEG)
    for f in range(frames):
        own_part(f, k.att_t, k.w_to, ta_copies[f])
    ta_last, sa_copies = [], []
    for f in range(frames):
        ta_last.append(features_on(f, k.att_t, ta_copies[f]))
    for f in range(frames):
        r = frame(f)
        k.mid16[r, :] = (both_parts(f, k.att_t, k.w_to, ta_last[f]) + t_ob).astype(BHALF)
        res = (dot_nn(k.mid16[r, :], k.w_tl[...]) + t_lb).astype(BHALF)
        k.x32[r, :] = k.x32[r, :] + res.astype(FLOAT)
        set_tail(k.x32, f, [cls_row[f]])
        norm(k.x32, 1, s_gain, s_beta, k.xh_s, k.n_s, r)
        k.sqkv[r, :] = (dot_nt(k.n_s[r, :], k.w_si[...]) + s_qb).astype(BHALF)
        k.att_s[0, c, r, :] = attend_all(k.sqkv[r, :], in_frame, k.p_s, f * heads)
        sa_copies.append(features(f, k.att_s))
    lone = patches - (ROWS - HALF)
    feats = []
    for f in range(frames):
        last_rows = k.att_s[0, c, (f + 1) * ROWS - HALF : (f + 1) * ROWS, :].astype(FLOAT)
        feats.append(last_rows[lone : lone + 1])
    k.cls_send[...] = eight([sum(onehot[f][i][:, :width] * feats[f] for f in range(frames)) for i in range(clips)])
    cls_copies = [send(k.cls_send, k.cls_recv.at[s], (p, h), k.cls_recv.at[q]) for p, q in zip(peers, givers)]
    k.cls_recv[s] = k.cls_send[...]
    arrived([w_so_near, w_so_last])
    s_ob, m_gain, m_beta = vec("s_ob"), vec("m_gain"), vec("m_beta")
    for f in range(frames):
        own_part(f, k.att_s, k.w_so, sa_copies[f])
    sa_last = []
    for f in range(frames):
        sa_last.append(features_on(f, k.att_s, sa_copies[f]))
    arrived(cls_copies)
    feat = k.cls_recv[0]
    for i in range(1, seq):
        feat = feat + k.cls_recv[i]
    high = feat.astype(BHALF)
    rest = (feat - high.astype(FLOAT)).astype(BHALF)
    k.cls_head[h] = dot_nn(high, k.w_so[0, c]) + dot_nn(rest, k.w_so[0, c])
    cls_copies = [send(k.cls_head.at[h], k.cls_head.at[h], d, k.cls_head.at[d[1]]) for d in (sister, across, diagonal)]
    cls_at = [slice(f * ROWS + patches, f * ROWS + patches + 1) for f in range(frames)]
    for f in range(frames):
        r = frame(f)
        k.x32[r, :] = k.x32[r, :] + (both_parts(f, k.att_s, k.w_so, sa_last[f]) + s_ob)
        set_tail(k.x32, f, [])

    first_seq = jnp.where(s == 0, 1.0, 0.0)
    m_ub = vec("m_ub")
    need("w_up")

    def up_rows(r):
        norm(k.x32, 2, m_gain, m_beta, k.xh_m, k.n_m, r)
        k.t32[r, :] = dot_nn(k.n_m[r, :], k.w_up[...])

    def kept(r):
        at = r.start + iota((r.stop - r.start, 1), 0)
        return jnp.where((at >= patches) & (at < ROWS), first_seq, 1.0)

    def gelu_rows(r):
        pre = k.t32[r, :] + m_ub
        cdf = 0.5 * (1.0 + lax.erf(pre * 0.7071067811865476))
        slope = cdf + pre * jnp.exp(-0.5 * pre * pre) * 0.3989422804014327
        act = pre * cdf
        grad = k.dact[r, :] * slope
        k.act[r, :] = act.astype(BHALF)
        k.gpre[r, :] = grad.astype(BHALF)
        if r.start == 0:
            act, grad = act * kept(r), grad * kept(r)
        k.act_k[r, :] = act.astype(BHALF)
        k.gpre_k[r, :] = grad.astype(BHALF)

    def sum_open(i, f, lhs, rhs, dot):
        r = frame(f)
        for b in range(2):
            cut = slice(b * half, (b + 1) * half)
            k.part[i, b, r, :] = dot(lhs[r, :], rhs[cut, :] if dot is dot_nt else rhs[:, cut]).astype(BHALF)
        return send(k.part.at[i, other_c, r], k.pair.at[i, r], sister, k.pair.at[i, r])

    def sum_across(i, f, copy):
        r = frame(f)
        copy.wait_recv()
        k.part[i, c, r, :] = (k.part[i, c, r, :].astype(FLOAT) + k.pair[i, r, :].astype(FLOAT)).astype(BHALF)
        return send(k.part.at[i, c, r], k.other.at[i, r], across, k.other.at[i, r])

    def sum_close(i, f, copy):
        r = frame(f)
        copy.wait_recv()
        k.total[i, c, r, :] = (k.part[i, c, r, :].astype(FLOAT) + k.other[i, r, :].astype(FLOAT)).astype(BHALF)
        return send(k.total.at[i, c, r], k.total.at[i, c, r], sister, k.total.at[i, other_c, r])

    def rows_of(ref, i, r):
        return jnp.concatenate([ref[i, 0, r, :], ref[i, 1, r, :]], axis=-1).astype(FLOAT)

    z_hi, z_lo = z // 2, z % 2
    z_near, z_far = ((z + 1 - 2 * z_lo) * 2 + y, h), (((z + 2) % zs) * 2 + y, h)
    z_first = ('up',)

    def grad_make(name, *pairs):
        g = getattr(k, "g_" + name)
        parts = [dot_tn(lhs, rhs).astype(BHALF) for lhs, rhs in pairs]
        value = parts[0] if len(parts) == 1 else jnp.concatenate(parts, axis=-1)
        g[...] = value.reshape(g.shape)

    class Reduction:
        def __init__(self, name):
            self.name, self.g = name, getattr(k, "g_" + name)
            self.first, self.second, self.third = [getattr(k, kind + name) for kind in ("y_", "z_", "x_")]
            ways = [(y, y_peer), (z_lo, z_near)]
            (self.one, self.peer_one), (self.two, self.peer_two) = ways[::-1] if name in z_first else ways

        def at(self, one, two):
            return (slice(None), one, two) if self.name in z_first else (slice(None), two, one)

        def add(self, at, got):
            self.g[at] = (self.g[at].astype(FLOAT) + got.astype(FLOAT)).astype(BHALF)

    def grad_open(name):
        job = Reduction(name)
        job.copies = []
        for two in (1 - job.two, job.two):
            into = job.first.at[two]
            job.copies.append(send(job.g.at[job.at(1 - job.one, two)], into, job.peer_one, into))
        return job

    def grad_near(job):
        job.copies[0].wait_recv()
        away, kept_here = job.at(job.one, 1 - job.two), job.at(job.one, job.two)
        job.add(away, job.first[1 - job.two])
        copy = send(job.g.at[away], job.second, job.peer_two, job.second)
        job.copies[1].wait_recv()
        job.add(kept_here, job.first[job.two])
        job.copies = [copy]
        return job

    def grad_far(job):
        job.copies[0].wait_recv()
        job.add(job.at(job.one, job.two), job.second[...])
        job.copies = [send(job.g.at[1 - z_hi, z_lo, y], job.third, z_far, job.third)]
        return job

    def grad_close(job):
        job.copies[0].wait_recv()
        getattr(k, "o_" + job.name)[...] = job.g[z_hi, z_lo, y].astype(FLOAT) + job.third[...].astype(FLOAT)

    def vectors_send(which, values):
        value = eight(values)
        k.v_send[which] = value
        k.v_recv[which, s] = value
        into = k.v_recv.at[which]
        return [send(k.v_send.at[which], into.at[s], (p, h), into.at[q]) for p, q in zip(peers, givers)]

    def vectors_close(which, copies):
        arrived(copies)
        value = k.v_recv[which, 0]
        for i in range(1, seq):
            value = value + k.v_recv[which, i]
        return value

    ones = jnp.ones((8, rows), BHALF)
    at = iota((8, rows), 1)
    ones_kept = jnp.where((at >= patches) & (at < ROWS), first_seq, 1.0).astype(BHALF)

    def col_sums(ref, weights=None):
        out = dot_nn(ones if weights is None else weights, ref[...])[0:1]
        if out.shape[1] < model:
            out = jnp.concatenate([out, jnp.zeros((1, model - out.shape[1]), FLOAT)], axis=-1)
        return out

    def column_sum(v):
        return jnp.sum(v, axis=0, keepdims=True)

    def add_all(lists):
        return [sum(v) for v in zip(*lists)]

    def norm_back(i, which, gain, xhat, r, keep):
        g = rows_of(k.total, i, r)
        n = xhat[r, :]
        gh = g * gain
        m1 = jnp.mean(gh, axis=-1, keepdims=True)
        m2 = jnp.mean(gh * n, axis=-1, keepdims=True)
        dx = k.inv[which, r, 0:1] * (gh - m1 - n * m2)
        w = g * kept(r) if keep and r.start == 0 else g
        return dx, (column_sum(w * n), column_sum(w))

    m_sum = [None] * frames
    for f in range(1, frames):
        up_rows(frame(f))
        gelu_rows(frame(f))
        m_sum[f] = sum_open(0, f, k.gpre, k.w_up, dot_nt)
    up_rows(frame(0))
    for f in range(1, frames):
        m_sum[f] = sum_across(0, f, m_sum[f])
    arrived(cls_copies)
    cls_sum = k.cls_head[0] + k.cls_head[1] + k.cls_head[2] + k.cls_head[3]
    set_tail(k.x32, 0, [cls32[i : i + 1] + cls_sum[i : i + 1] * per_len[i] + s_ob for i in range(clips)])
    up_rows(slice(ROWS - HALF, ROWS))
    gelu_rows(frame(0))
    m_sum[0] = sum_open(0, 0, k.gpre, k.w_up, dot_nt)
    o_sum = [sum_open(1, f, k.act, k.w_dn, dot_nn) for f in range(frames)]
    m_sum[0] = sum_across(0, 0, m_sum[0])
    grad_make("dn", (k.gr16[...], k.act_k[...]))
    j_dn = grad_open("dn")
    grad_make("up", (k.n_m[...], k.gpre_k[...]))
    j_up = grad_open("up")
    ub_grad, db_grad = col_sums(k.gpre_k), col_sums(k.gr16, ones_kept)
    m_last, sums = [None] * frames, [None] * frames
    backwards = list(range(1, frames)) + [0]
    for f in backwards:
        m_last[f] = sum_close(0, f, m_sum[f])
    for f in backwards:
        m_last[f].wait_recv()
        dx, sums[f] = norm_back(0, 2, m_gain, k.xh_m, frame(f), True)
        k.gr32[frame(f), :] = k.gr32[frame(f), :] + dx
    grad_cls_mid = k.gr32[patches : patches + clips, :]
    k.gcm[...] = eight([grad_cls_mid])
    shares = [
        sum(onehot[f][i] * (grad_cls_mid[i : i + 1] * per_len[i]) for i in range(clips)) for f in range(frames)
    ]

    def space_back(f):
        r = frame(f)
        set_tail(k.gr32, f, [shares[f]])
        k.gss[r, :] = k.gr32[r, :].astype(BHALF)
        set_tail(k.gr32, f, [])
        grad = dot_nt(k.gss[r, :], k.w_so[0, c]).astype(BHALF)
        k.dsq[r, :] = attend_back_all(k.sqkv[r, :], grad, k.p_s, f * heads)
        return sum_open(2, f, k.dsq, k.w_si, dot_nn)

    s_sum = []
    for f in range(frames):
        s_sum.append(space_back(f))
        if f:
            s_sum[f - 1] = sum_across(2, f - 1, s_sum[f - 1])
    m_rows = add_all(sums) + [ub_grad, db_grad]
    s_sum[-1] = sum_across(2, frames - 1, s_sum[-1])
    j_dn = grad_near(j_dn)
    j_up = grad_near(j_up)
    v_m = vectors_send(0, m_rows)
    grad_make("s", (k.n_s[...], k.dsq[...]), (k.gss[...], k.att_s[0, c]))
    j_s = grad_open("s")
    s_rows = [col_sums(k.gss), col_sums(k.dsq)]
    s_last = [sum_close(2, f, s_sum[f]) for f in range(frames)]

    old = len(unsent)
    g_copies, cls_in = [], []
    for f in range(frames):
        r = frame(f)
        s_last[f].wait_recv()
        dx, sums[f] = norm_back(2, 1, s_gain, k.xh_s, r, False)
        k.gr32[r, :] = k.gr32[r, :] + dx
        cls_in.append(k.gr32[cls_at[f], :])
        set_tail(k.gr32, f, [])
        k.gtr[r, :] = k.gr32[r, :].astype(BHALF)
        k.gtm[r, :] = dot_nt(k.gtr[r, :], k.w_tl[...]).astype(BHALF)
        grad = dot_nt(k.gtm[r, :], k.w_to[0, c]).astype(BHALF)
        g_copies.append(scatter(f, grad, k.g_send, k.g_pos))
    o_sum = [sum_across(1, f, o_sum[f]) for f in range(frames)]
    j_dn = grad_far(j_dn)
    j_up = grad_far(j_up)
    pick = (iota((model, width), 0) == h * width + iota((model, width), 1)).astype(FLOAT).astype(BHALF)
    grad_make("l", (k.mid16[...], dot_nn(k.gtr[...], pick).astype(BHALF)), (k.gtm[...], k.att_t[0, c]))
    j_l = grad_open("l")
    newer = len(unsent)
    d_copies = []
    for b in range(2):
        for copies in g_copies:
            arrived(copies[b])
            value = attend_back_all(
            k.q_pos[b].reshape(span, 3 * width), k.g_pos[b].reshape(span, width), k.p_t, b * heads
        )
        k.d_pos[b] = value.reshape(every, HALF, 3 * width)
        d_copies += gather(b, k.d_pos, k.d_recv)
    j_s = grad_near(j_s)
    cls_parts = [sum(onehot[f][i] * cls_in[f] for f in range(frames)) for i in range(clips)]
    v_s = vectors_send(1, add_all(sums) + s_rows + cls_parts)
    t_rows = [col_sums(k.gtm), col_sums(k.gtr)]
    o_last = [sum_close(1, f, o_sum[f]) for f in range(frames)]
    m_vec = vectors_close(0, v_m)
    k.o_vec[0:8, :] = m_vec
    m_db = vec("m_db")
    for f in range(frames):
        r = frame(f)
        o_last[f].wait_recv()
        out = k.x32[r, :] + rows_of(k.total, 1, r) + m_db
        k.o_blk[:, f, :] = out[:patches].astype(BHALF)
        if f == 0:
            k.o_cls[...] = out[patches : patches + clips].astype(BHALF)
    grad_close(j_dn)
    grad_close(j_up)
    j_l = grad_near(j_l)
    for copy in unsent[:old]:
        copy.wait_send()
    arrived(d_copies)
    t_sum, shared = [], []
    for f in range(frames):
        k.dtq[frame(f), :] = gathered(f, k.d_recv)
        t_sum.append(sum_open(3, f, k.dtq, k.w_ti, dot_nn))
    grad_make("ta", (k.n_t[...], k.dtq[:, : 2 * width]))
    j_ta = grad_open("ta")
    for f in range(frames):
        g = rows_of(k.part, 3, frame(f))
        shared.append((column_sum(g * k.xh_t[frame(f), :]), column_sum(g)))
        t_sum[f] = sum_across(3, f, t_sum[f])
    grad_make("tb", (k.n_t[...], k.dtq[:, 2 * width :]))
    j_tb = grad_open("tb")
    v_t = vectors_send(2, add_all(shared) + [t_rows[0], col_sums(k.dtq), t_rows[1]])
    for copy in unsent[old:newer]:
        copy.wait_send()
    j_s = grad_far(j_s)
    s_vec = vectors_close(1, v_s)
    k.o_vec[8:16, :] = s_vec + jnp.concatenate([jnp.zeros((4, model), FLOAT), k.gcm[0:4, :]], axis=0)
    j_l = grad_far(j_l)
    j_ta = grad_near(j_ta)
    t_last = [sum_close(3, 0, t_sum[0])]
    t_vec = vectors_close(2, v_t)
    k.v_head[h] = t_vec
    h_copies = [send(k.v_head.at[h], k.v_head.at[h], d, k.v_head.at[d[1]]) for d in (sister, across, diagonal)]
    t_last += [sum_close(3, f, t_sum[f]) for f in range(1, frames)]
    for f in range(frames):
        r = frame(f)
        t_last[f].wait_recv()
        if f == 0:
            j_tb = grad_near(j_tb)
        dx, _ = norm_back(3, 0, t_gain, k.xh_t, r, False)
        out = k.gr32[r, :] + dx.astype(BHALF).astype(FLOAT)
        k.o_tok[:, f, :] = out[:patches].astype(BHALF)
    j_ta = grad_far(j_ta)
    j_tb = grad_far(j_tb)
    grad_close(j_s)
    grad_close(j_l)
    arrived(h_copies)
    over_head = k.v_head[0] + k.v_head[1] + k.v_head[2] + k.v_head[3]
    k.o_vec[16:24, :] = jnp.concatenate([over_head[0:2], t_vec[2:8]], axis=0)
    grad_close(j_ta)
    grad_close(j_tb)
    for copy in unsent[newer:]:
        copy.wait_send()


def finish_kernel(dims, h_blk, h_tok, vec, cls_out, g_dn, g_up, g_s, g_l, g_ta, g_tb, *refs):
    width, model, seq = dims["width"], dims["model"], dims["seq"]
    share, clips = model // seq, dims["clips"]
    o_blk, o_cls, o_tok, cls, tg, tb, ti, tp, to, tob, tl, tlb, sg, sb, si, sp, so, sob, mg, mb, up, ub, dn, db = refs
    o_blk[...] = h_blk[...]
    o_tok[...] = h_tok[...]
    s = lax.axis_index("seq")
    v = vec[...]
    mine = pltpu.roll(v, (model - share * s) % model, 1)[:, :share]
    for out, row in ((mg, 0), (sg, 8), (tg, 16)):
        out[...] = mine[row : row + 1].reshape(share)
    for out, row in ((mb, 1), (ub, 2), (db, 3), (sb, 9), (sob, 10), (tb, 17), (tob, 18), (tlb, 20)):
        out[...] = v[row : row + 1].reshape(model)
    cls[...] = mine[12 : 12 + clips]
    o_cls[...] = cls_out[...]
    for out, row in ((sp, 11), (tp, 19)):
        out[0:1, :] = v[row : row + 1, :width]
        out[1:2, :] = v[row : row + 1, 2 * width : 3 * width]
    for i in range(3):
        si[i] = g_s[:, i * width : (i + 1) * width]
    ti[0], ti[1], ti[2] = g_ta[:, :width], g_ta[:, width:], g_tb[...]
    tl[...] = g_l[:, :width]
    up[...] = g_up[...]
    dn[...] = g_dn[...]
    to[...] = g_l[:, width:].T
    so[...] = g_s[:, 3 * width :].T


def fused_body(
    tokens,
    cls_tokens,
    clip_lengths,
    time_gain,
    time_beta,
    time_proj_in,
    time_qv_bias,
    time_proj_out,
    time_out_bias,
    time_linear,
    time_linear_bias,
    space_gain,
    space_beta,
    space_proj_in,
    space_qv_bias,
    space_proj_out,
    space_out_bias,
    mlp_gain,
    mlp_beta,
    mlp_up,
    mlp_up_bias,
    mlp_down,
    mlp_down_bias,
    out_grad,
    cls_grad,
):
    frames, patches, model = tokens.shape
    seq = lax.axis_size("seq")
    width, hidden, clips = time_proj_in.shape[2], mlp_up.shape[1], clip_lengths.shape[0]
    dims = dict(
        frames=frames,
        patches=patches,
        model=model,
        seq=seq,
        width=width,
        hidden=hidden,
        clips=clips,
        pos=-(-patches // seq),
    )

    def frames_inner(v):
        return jnp.transpose(v, (1, 0, 2))

    def outputs_first(v):
        return jnp.transpose(v, (1, 2, 0)).reshape(3 * width, model)

    scratch = scratch_shapes(dims)
    grads = grad_columns(dims)
    share = model // seq
    shape = jax.ShapeDtypeStruct
    vmem, anywhere = pl.BlockSpec(memory_space=pltpu.VMEM), pl.BlockSpec(memory_space=pl.ANY)
    inner = (patches, frames, model)
    outs = [
        shape(inner, BHALF),
        shape(cls_tokens.shape, BHALF),
        shape(inner, BHALF),
        shape((24, model), FLOAT),
    ] + [shape((share, columns), FLOAT) for _, columns in grads]
    names = list(INPUTS) + list(OUTPUTS) + ["o_" + name for name, _ in grads] + list(scratch)
    results = pl.pallas_call(
        functools.partial(layer_kernel, dims, names),
        out_shape=outs,
        in_specs=[pl.BlockSpec(memory_space=pltpu.SMEM)] + [vmem] * 2 + [anywhere] * (len(INPUTS) - 3),
        out_specs=[vmem] * len(outs),
        scratch_shapes=list(scratch.values()),
        compiler_params=pltpu.CompilerParams(
            collective_id=0, has_side_effects=True, vmem_limit_bytes=62 * 1024 * 1024
        ),
        name="layer",
    )(
        clip_lengths,
        cls_tokens,
        cls_grad,
        time_gain,
        time_beta,
        time_out_bias,
        time_linear_bias,
        space_gain,
        space_beta,
        space_out_bias,
        mlp_gain,
        mlp_beta,
        mlp_down_bias,
        mlp_up_bias,
        time_qv_bias,
        space_qv_bias,
        frames_inner(tokens),
        frames_inner(out_grad),
        outputs_first(time_proj_in),
        time_proj_out,
        time_linear,
        outputs_first(space_proj_in),
        space_proj_out,
        mlp_up,
        mlp_down,
    )
    blk, cls_out, tok, vectors = results[:4]
    row, gain = shape((model,), FLOAT), shape((share,), FLOAT)
    proj, pair = shape((3, share, width), FLOAT), shape((2, width), FLOAT)
    out_shape = [
        shape(inner, BHALF),
        shape(cls_tokens.shape, BHALF),
        shape(inner, BHALF),
        shape((clips, share), FLOAT),
        gain,
        row,
        proj,
        pair,
        shape((width, share), FLOAT),
        row,
        shape((share, width), FLOAT),
        row,
        gain,
        row,
        proj,
        pair,
        shape((width, share), FLOAT),
        row,
        gain,
        row,
        shape((share, hidden), FLOAT),
        shape((hidden,), FLOAT),
        shape((share, hidden), FLOAT),
        row,
    ]
    last = pl.pallas_call(
        functools.partial(finish_kernel, dims),
        out_shape=out_shape,
        in_specs=[vmem] * 10,
        out_specs=[vmem] * len(out_shape),
        compiler_params=pltpu.CompilerParams(vmem_limit_bytes=62 * 1024 * 1024),
        name="finish",
    )(blk, tok, vectors, cls_out, *results[4:])
    last = list(last)
    for i in (0, 2, 6, 14):
        last[i] = jnp.transpose(last[i], (1, 0, 2))
    last[22] = last[22].T
    return tuple(last)


def solution(mesh):
    placed = (
        P("seq", None, None),
        P(),
        P(),
        P(),
        P(),
        P(None, None, "head"),
        P(None, "head"),
        P("head", None),
        P(),
        P(),
        P(),
        P(),
        P(),
        P(None, None, "head"),
        P(None, "head"),
        P("head", None),
        P(),
        P(),
        P(),
        P(None, "head"),
        P("head"),
        P("head", None),
        P(),
        P("seq", None, None),
        P(),
    )
    fused = mesh.shape["seq"] == 8 and mesh.shape["head"] == 4
    return jax.shard_map(
        fused_body if fused else body,
        mesh=mesh,
        in_specs=placed,
        out_specs=(
            P("seq", None, None),
            P(),
            P("seq", None, None),
            P(None, "seq"),
            P("seq"),
            P(),
            P("seq", None, "head"),
            P(None, "head"),
            P("head", "seq"),
            P(),
            P("seq", "head"),
            P(),
            P("seq"),
            P(),
            P("seq", None, "head"),
            P(None, "head"),
            P("head", "seq"),
            P(),
            P("seq"),
            P(),
            P("seq", "head"),
            P("head"),
            P("head", "seq"),
            P(),
        ),
        check_vma=False,
    )
```
